128 devices in a mesh: dp: 16 (over x, y_lo, core), tensor: 8 (over y_hi, z).
Axes of the slice: x: 4, y: 4 (y_hi: 2, y_lo: 2; y = y_hi * 2 + y_lo), z: 4, core: 2. Of those that a mesh axis runs over, the one named last changes fastest.
Arguments:
- prompt_keys: bfloat16 [128, 512, 1024], P('dp', None, 'tensor'), may hold values from -6 to 6
- prompt_values: bfloat16 [128, 512, 1024], P('dp', None, 'tensor'), may hold values from -6 to 6
- query_states: bfloat16 [128, 64, 8192], P('dp', None, 'tensor'), may hold values from -140 to 140
- query_keys: bfloat16 [128, 64, 1024], P('dp', None, 'tensor'), may hold values from -6 to 6
- query_values: bfloat16 [128, 64, 1024], P('dp', None, 'tensor'), may hold values from -6 to 6
- lengths: int32 [128], P('dp'), may hold values from 1 to 512, 32768 in all
- residual: bfloat16 [128, 64, 8192], P('dp', None, 'tensor'), may hold values from -6 to 6
- out_weight: bfloat16 [8192, 8192], P('tensor', 'dp'), may hold values from -0.0625 to 0.0625
- final_gain: float32 [8192], P('tensor'), may hold values from 0.25 to 1.75
- conn_weight: bfloat16 [8192, 3584], P('tensor'), may hold values from -0.0625 to 0.0625
- owner: int32 [16, 8], P('dp'), may hold values from 0 to 7, each once within a row
- latents: bfloat16 [128, 1024, 128], P(('dp', 'tensor')), may hold values from -6 to 6
- noise: bfloat16 [128, 1024, 128], P(('dp', 'tensor')), may hold values from -6 to 6
- timesteps: int32 [128], P(('dp', 'tensor')), may hold values from 0 to 999
- patch_weight: bfloat16 [128, 1792], replicated, may hold values from -0.5 to 0.5
- time_embedding: float32 [1792], replicated, may hold values from -4 to 4
- image_norm_gain: float32 [1792], replicated, may hold values from 0.25 to 1.75
- query_matrix: bfloat16 [1792, 1792], replicated, may hold values from -0.125 to 0.125
- velocity_head_weight: bfloat16 [1792, 128], replicated, may hold values from -0.125 to 0.125
Outputs:
- velocity: float32 [128, 1024, 128], P(('dp', 'tensor'))
- query_grad: float32 [1792, 1792], P(('dp', 'tensor'))
The draws below stay inside these ranges and needn't reach their ends.
All inputs are finite; a program needn't handle non-finite values. No bound on the sum of `lengths` on one device may be relied on, other than what follows from the above.
Results may differ from the reference program's by a relative error of at most 0.025.
Values may be sent and summed in bfloat16 or wider, within the bound.
A program may use at most 128 MiB of HBM per device.

```python
import math
import jax
import jax.numpy as jnp
import numpy as np
from jax import lax

D = 8192
HEADS = 64
KV_HEADS = 8
HEAD = 128
NQ = 64
LMAX = 512
DHEAD = 112
W = 1792
PATCH = 128
IMG_TOK = 1024
NT = 1000
PROMPTS_GRP = 8
PROMPTS = 128
N_DP = 16
N_TENSOR = 8


def shared_keys(key):
    return jax.random.truncated_normal(key, -6.0, 6.0, (PROMPTS, LMAX, KV_HEADS * HEAD), jnp.float32)


def draw_prompt_keys(key, part):
    base = shared_keys(key)
    return base.astype(jnp.bfloat16)


def draw_query_states(key, part):
    key = jax.random.fold_in(key, 23)
    states = jax.random.truncated_normal(key, -6.0, 6.0, (PROMPTS, NQ, HEADS * HEAD), jnp.float32)
    return states.astype(jnp.bfloat16)


def plant(entries, rng, smallest, largest):
    longest = entries.shape.index(max(entries.shape))
    spots = []
    for shift in (0, 1):
        where = [jax.random.randint(jax.random.fold_in(rng, axis), (), 0, length) for axis, length in enumerate(entries.shape)]
        where[longest] = (where[longest] + shift) % entries.shape[longest]
        spots.append(tuple(where))
    return entries.at[spots[0]].set(smallest).at[spots[1]].set(largest)


def shard_levels(own_key, shape, pieces, smallest, largest):
    level = 1.0
    for axis_at, blocks in pieces:
        steps = jax.random.uniform(jax.random.fold_in(jax.random.fold_in(own_key, 6), axis_at), (blocks,), jnp.float32, smallest / len(pieces), largest / len(pieces))
        level = level * jnp.repeat(jnp.exp(steps), shape[axis_at] // blocks).reshape((-1,) + (1,) * (len(shape) - 1 - axis_at))
    return level


def length_profile(number_of, total, bound, lean):
    loads = [(1 << 20) // math.isqrt(rank ** lean) + 1 for rank in range(2, number_of + 1)]
    rest, holding = total - bound - (number_of - 1), [1] * (number_of - 1)
    while rest > 0:
        candidates = [i for i in range(number_of - 1) if holding[i] < bound]
        whole, left = sum([loads[i] for i in candidates]), rest
        for i in candidates:
            extra = min(bound - holding[i], max(1, left * loads[i] // whole), rest)
            holding[i] = holding[i] + extra
            rest = rest - extra
    return np.array([bound] + holding)


def uneven_parts(rng, amount, total, reach, lean):
    if amount == 2:
        one = jax.random.randint(rng, (), max(1, total - reach), min(reach, total - 1) + 1)
        return jnp.stack([one, total - one])
    sizes = jnp.asarray(length_profile(amount, total, reach, lean), jnp.int32)
    pairs = (amount - 1) // 2
    giver, receiver = sizes[1:1 + 2 * pairs:2], sizes[2:2 + 2 * pairs:2]
    room = jnp.minimum(giver - 1, reach - receiver)
    shifted = jax.random.randint(jax.random.fold_in(rng, 1), (pairs,), 0, 1 << 20) % (room + 1)
    sizes = sizes.at[1:1 + 2 * pairs:2].set(giver - shifted).at[2:2 + 2 * pairs:2].set(receiver + shifted)
    return sizes[jax.random.permutation(jax.random.fold_in(rng, 2), amount)]


def bell_draw(rng, dims, spread, limit, cuts=(), held_as=jnp.bfloat16):
    result = jax.random.normal(rng, dims, jnp.float32) * spread
    if len(cuts) > 0:
        result = shard_levels(rng, dims, cuts, -0.22, 0.18) * result
    return jnp.clip(result, min=-limit, max=limit).astype(held_as)


def setup_inputs(seed: int = 0) -> dict:
    arg_keys = jax.random.split(jax.random.key(seed), 20)
    return {
        "prompt_keys": draw_prompt_keys(jax.random.fold_in(arg_keys[19], 71), 0),
        "prompt_values": bell_draw(arg_keys[1], (PROMPTS, LMAX, KV_HEADS * HEAD), 1.0, 6.0, ((0, 16), (2, 8))),
        "query_states": draw_query_states(jax.random.fold_in(arg_keys[19], 71), 0),
        "query_keys": bell_draw(arg_keys[3], (PROMPTS, NQ, KV_HEADS * HEAD), 1.0, 6.0, ((0, 16), (2, 8))),
        "query_values": bell_draw(arg_keys[4], (PROMPTS, NQ, KV_HEADS * HEAD), 1.0, 6.0, ((0, 16), (2, 8))),
        "lengths": uneven_parts(arg_keys[5], PROMPTS, PROMPTS * LMAX // 2, LMAX, 2).astype(jnp.int32),
        "residual": bell_draw(arg_keys[6], (PROMPTS, NQ, D), 1.0, 6.0, ((0, 16), (2, 8))),
        "out_weight": bell_draw(arg_keys[7], (HEADS * HEAD, D), (HEADS * HEAD) ** -0.5, 0.0625, ((0, 8), (1, 16))),
        "final_gain": jnp.clip(1.0 + 0.15 * jax.random.normal(arg_keys[8], (D,), jnp.float32), 0.25, 1.75),
        "conn_weight": bell_draw(arg_keys[9], (D, 2 * W), D ** -0.5, 0.0625, ((0, 8),)),
        "owner": jax.vmap(lambda own: jax.random.permutation(own, PROMPTS_GRP))(jax.random.split(arg_keys[10], N_DP)).reshape((N_DP, PROMPTS_GRP)).astype(jnp.int32),
        "latents": bell_draw(arg_keys[11], (PROMPTS, IMG_TOK, PATCH), 1.0, 6.0, ((0, 128),)),
        "noise": bell_draw(arg_keys[12], (PROMPTS, IMG_TOK, PATCH), 1.0, 6.0, ((0, 128),)),
        "timesteps": plant(jax.random.randint(arg_keys[13], (PROMPTS,), 0, NT), jax.random.fold_in(arg_keys[13], 1), 0, NT - 1).astype(jnp.int32),
        "patch_weight": bell_draw(arg_keys[14], (PATCH, W), PATCH ** -0.5, 0.5),
        "time_embedding": bell_draw(arg_keys[15], (W,), 1.0, 4.0, (), jnp.float32),
        "image_norm_gain": jnp.clip(1.0 + 0.15 * jax.random.normal(arg_keys[16], (W,), jnp.float32), 0.25, 1.75),
        "query_matrix": bell_draw(arg_keys[17], (W, W), W ** -0.5, 0.125),
        "velocity_head_weight": bell_draw(arg_keys[18], (W, PATCH), W ** -0.5, 0.125),
    }


eps = 1e-06
grad_gain = 16.0

def llm_attend(queries, keys, values, own_keys, own_values, lens):
    prompts, rows, width = queries.shape
    klen = keys.shape[1]
    kv_count = keys.shape[2] // HEAD
    group = width // HEAD // kv_count
    scale = 1.0 / HEAD ** 0.5
    qr = queries.reshape(prompts, rows, kv_count, group, HEAD).astype(jnp.float32)
    kr = keys.reshape(prompts, klen, kv_count, HEAD).astype(jnp.float32)
    vr = values.reshape(prompts, klen, kv_count, HEAD).astype(jnp.float32)
    ok = own_keys.reshape(prompts, rows, kv_count, HEAD).astype(jnp.float32)
    ov = own_values.reshape(prompts, rows, kv_count, HEAD).astype(jnp.float32)
    first = jnp.einsum('pikgd,pjkd->pkgij', qr, kr) * scale
    second = jnp.einsum('pikgd,pjkd->pkgij', qr, ok) * scale
    valid = jnp.arange(klen)[None, :] < lens[:, None]
    first = jnp.where(valid[:, None, None, None, :], first, -jnp.inf)
    causal = jnp.arange(rows)[None, :] <= jnp.arange(rows)[:, None]
    second = jnp.where(causal[None, None, None], second, -jnp.inf)
    top = jnp.maximum(lax.optimization_barrier(jnp.max(first, -1, keepdims=True)), lax.optimization_barrier(jnp.max(second, -1, keepdims=True)))
    efirst = jnp.exp(first - top)
    esecond = jnp.exp(second - top)
    total = lax.optimization_barrier(jnp.sum(efirst, -1, keepdims=True)) + lax.optimization_barrier(jnp.sum(esecond, -1, keepdims=True))
    pfirst = (efirst / total).astype(jnp.bfloat16).astype(jnp.float32)
    psecond = (esecond / total).astype(jnp.bfloat16).astype(jnp.float32)
    out = jnp.einsum('pkgij,pjkd->pikgd', pfirst, vr) + jnp.einsum('pkgij,pjkd->pikgd', psecond, ov)
    return out.reshape(prompts, rows, width).astype(jnp.bfloat16)

def flow_matching_step(condition_rows, latents, noise, step_count, patch_weight, time_embedding, image_norm_gain, query_matrix, velocity_head_weight, count_of_rows):
    images, tokens, patch = latents.shape
    width = query_matrix.shape[0]
    heads = width // DHEAD
    scale = 1.0 / DHEAD ** 0.5
    tval = ((step_count.astype(jnp.float32) + 0.5) / NT)[:, None, None]
    noisy = ((1.0 - tval) * latents.astype(jnp.float32) + tval * noise.astype(jnp.float32)).astype(jnp.bfloat16)
    h = jnp.dot(noisy.reshape(-1, patch), patch_weight, preferred_element_type=jnp.float32).reshape(images, tokens, width)
    h = h + tval * time_embedding
    normed = (h * lax.rsqrt(lax.optimization_barrier(jnp.mean(h * h, -1, keepdims=True)) + eps) * image_norm_gain).astype(jnp.bfloat16)
    normalized_rows = normed.reshape(-1, width)
    qd = jnp.dot(normalized_rows, query_matrix, preferred_element_type=jnp.float32).astype(jnp.bfloat16)
    qd = qd.reshape(images, tokens, heads, DHEAD).astype(jnp.float32)
    keys = condition_rows[:, :, :width].reshape(images, -1, heads, DHEAD).astype(jnp.float32)
    vals = condition_rows[:, :, width:].reshape(images, -1, heads, DHEAD).astype(jnp.float32)
    scores = jnp.einsum('itnd,ijnd->intj', qd, keys) * scale
    expo = jnp.exp(scores)
    probs = expo / lax.optimization_barrier(jnp.sum(expo, -1, keepdims=True))
    pround = probs.astype(jnp.bfloat16).astype(jnp.float32)
    attn = jnp.einsum('intj,ijnd->itnd', pround, vals).reshape(images, tokens, width).astype(jnp.bfloat16)
    mixed = (h + attn.astype(jnp.float32)).astype(jnp.bfloat16)
    velocity = jnp.dot(mixed.reshape(-1, width), velocity_head_weight, preferred_element_type=jnp.float32).reshape(images, tokens, patch)
    target = noise.astype(jnp.float32) - latents.astype(jnp.float32)
    dvel = ((velocity - target) * (grad_gain / count_of_rows ** 0.5)).astype(jnp.bfloat16)
    dmixed = jnp.dot(dvel.reshape(-1, patch), velocity_head_weight.T, preferred_element_type=jnp.float32).astype(jnp.bfloat16)
    dmixed = dmixed.reshape(images, tokens, heads, DHEAD).astype(jnp.float32)
    dprob = jnp.einsum('itnd,ijnd->intj', dmixed, vals)
    dscore = (probs * (dprob - lax.optimization_barrier(jnp.sum(probs * dprob, -1, keepdims=True))) * scale).astype(jnp.bfloat16)
    query_delta = jnp.einsum('intj,ijnd->itnd', dscore.astype(jnp.float32), keys).reshape(-1, width).astype(jnp.bfloat16)
    return (velocity, normalized_rows, query_delta)

def reference(prompt_keys, prompt_values, query_states, query_keys, query_values, lengths, residual, out_weight, final_gain, conn_weight, owner, latents, noise, timesteps, patch_weight, time_embedding, image_norm_gain, query_matrix, velocity_head_weight):
    groups = owner.shape[0]
    per_group = owner.shape[1]
    count_of_rows = latents.shape[0] * latents.shape[1]
    head_block = out_weight.shape[0] // N_TENSOR
    feat_block = D // N_TENSOR

    def one_group(items):
        pk, pv, qs, qk, qv, lens, res, own, latent_input, noise_sample, step_count = items
        attended = llm_attend(qs, pk, pv, qk, qv, lens).reshape(per_group * NQ, -1)
        summed = jnp.zeros((per_group * NQ, D), jnp.float32)
        for block in range(N_TENSOR):
            term = jnp.dot(attended[:, block * head_block:(block + 1) * head_block], out_weight[block * head_block:(block + 1) * head_block], preferred_element_type=jnp.float32)
            summed = summed + term.astype(jnp.bfloat16).astype(jnp.float32)
        llm_out = res.reshape(per_group * NQ, D).astype(jnp.float32) + summed
        stat = lax.optimization_barrier(jnp.mean(llm_out * llm_out, -1))
        scaled = (llm_out * final_gain).astype(jnp.bfloat16)
        csum = jnp.zeros((per_group * NQ, conn_weight.shape[1]), jnp.float32)
        for block in range(N_TENSOR):
            term = jnp.dot(scaled[:, block * feat_block:(block + 1) * feat_block], conn_weight[block * feat_block:(block + 1) * feat_block], preferred_element_type=jnp.float32)
            csum = csum + term.astype(jnp.bfloat16).astype(jnp.float32)
        condition_rows = (csum * lax.rsqrt(stat + eps)[:, None]).astype(jnp.bfloat16).reshape(per_group, NQ, -1)
        image_condition = jnp.take(condition_rows, own.astype(jnp.int32), axis=0)
        velocity, normalized_rows, query_delta = flow_matching_step(image_condition, latent_input, noise_sample, step_count, patch_weight, time_embedding, image_norm_gain, query_matrix, velocity_head_weight, count_of_rows)
        grad = jnp.dot(normalized_rows.T, query_delta, preferred_element_type=jnp.float32)
        return (velocity, grad)

    def split(arr):
        return arr.reshape((groups, per_group) + arr.shape[1:])
    items = (split(prompt_keys), split(prompt_values), split(query_states), split(query_keys), split(query_values), split(lengths), split(residual), owner, split(latents), split(noise), split(timesteps))
    velocity, grads = lax.map(one_group, items)
    velocity = velocity.reshape(latents.shape)
    query_grad = lax.optimization_barrier(jnp.sum(grads, axis=0))
    return (velocity, query_grad)
```

```python
import math

import jax
import jax.numpy as jnp
from jax import lax
from jax.experimental import pallas as pl
from jax.experimental.pallas import tpu as pltpu
from jax.sharding import PartitionSpec as P

D = 8192
HEAD = 128
NQ = 64
DHEAD = 112
NT = 1000
W = 1792
IMG_HEADS = 16
F32 = jnp.float32
BF16 = jnp.bfloat16
MESH = pl.DeviceIdType.MESH

eps = 1e-06
grad_gain = 16.0

ROWS_BLOCK = 14
ROWS_PAD = 16
GRAY = ((0, 3), (1, 2))
PIECES = (384, 384, 256, 256, 256, 256)
STARTS = (0, 384, 768, 1024, 1280, 1536)
KEY_WINDOWS = (0, 384, 896, 1280)
SCORE_WINDOWS = (0, 128, 256, 384, 512, 640, 768)


def nt_dot(a, b):
    return lax.dot_general(a, b, (((1,), (1,)), ((), ())), preferred_element_type=F32)


def nn_dot(a, b):
    return jnp.dot(a, b, preferred_element_type=F32)


def place_of_block(natural):
    z, y_hi = natural % 4, natural // 4 % 2
    core, y_lo, x = natural // 8 % 2, natural // 16 % 2, natural // 32
    place = core
    for i in (x, y_hi * 2 + y_lo, z):
        a, b = (i + i // 2) % 2, i // 2
        place = place * 4 + a * 2 + b
    return place


def head_mask(rows, width, head, base):
    lane = lax.broadcasted_iota(jnp.int32, (rows, width), 1) + base
    return (lane >= head * DHEAD) & (lane < (head + 1) * DHEAD)


def only_head(block, head, base):
    return jnp.where(head_mask(*block.shape, head, base), block.astype(F32), 0.0).astype(BF16)


def step_kernel(
    gain, q_ref, hv_ref, lat_ref, noise_ref, cond_ref, vhw_ref, vel_ref, dq_ref, kbd, kflat, vw, ones, probs, dsc
):
    scale = 1.0 / DHEAD**0.5
    keys = cond_ref.shape[0]

    @pl.when(pl.program_id(0) == 0)
    def _():
        for g, base in enumerate(KEY_WINDOWS):
            vals = []
            for n in range(4):
                window = cond_ref[:, base : base + 512]
                kbd[g, n * keys : (n + 1) * keys, :] = only_head(window, 4 * g + n, base)
                window = cond_ref[:, W + base : W + base + 512]
                vals.append(only_head(window, 4 * g + n, base))
            vw[g] = nn_dot(jnp.concatenate(vals, 0), vhw_ref[base : base + 512, :]).astype(BF16)
        for tile, first in enumerate(SCORE_WINDOWS):
            for n in range(4):
                window = cond_ref[:, tile * 256 : (tile + 1) * 256]
                kflat[tile, n * keys : (n + 1) * keys, :] = only_head(window, first // keys + n, tile * 256)
        row = lax.broadcasted_iota(jnp.int32, (256, 256), 0) // keys
        column = lax.broadcasted_iota(jnp.int32, (256, 256), 1) // keys
        ones[...] = jnp.where(row == column, 1.0, 0.0).astype(BF16)

    velocity = hv_ref[...]
    for g, base in enumerate(KEY_WINDOWS):
        expo = jnp.exp(nt_dot(q_ref[:, base : base + 512], kbd[g]) * scale)
        total = nn_dot(jnp.minimum(expo, 3.38e38).astype(BF16), ones[...])
        p = expo / total
        probs[:, g * 256 : (g + 1) * 256] = p
        velocity = velocity + nn_dot(p.astype(BF16), vw[g])
    vel_ref[...] = velocity
    target = noise_ref[...].astype(F32) - lat_ref[...].astype(F32)
    dvel = ((velocity - target) * gain).astype(BF16)
    for g in range(4):
        p = probs[:, g * 256 : (g + 1) * 256]
        dprob = nt_dot(dvel, vw[g])
        both = p * dprob
        high = both.astype(BF16)
        low = (both - high.astype(F32)).astype(BF16)
        shift = nn_dot(high, ones[...]) + nn_dot(low, ones[...])
        dsc[:, g * 256 : (g + 1) * 256] = (p * (dprob - shift) * scale).astype(BF16)
    for tile, first in enumerate(SCORE_WINDOWS):
        dq_ref[:, tile * 256 : (tile + 1) * 256] = nn_dot(dsc[:, first : first + 256], kflat[tile]).astype(BF16)


def step(q, hv, latents, noise, cond, vhw, gain):
    tokens = q.shape[0]
    block = 256
    keys = cond.shape[0]
    whole = lambda a: pl.BlockSpec(a.shape, lambda i: (0,) * a.ndim)
    rows = lambda width: pl.BlockSpec((block, width), lambda i: (i, 0))
    return pl.pallas_call(
        lambda *refs: step_kernel(gain, *refs),
        grid=(tokens // block,),
        in_specs=[rows(W), rows(128), rows(128), rows(128), whole(cond), whole(vhw)],
        out_specs=[rows(128), rows(W)],
        out_shape=[jax.ShapeDtypeStruct((tokens, 128), F32), jax.ShapeDtypeStruct((tokens, W), BF16)],
        scratch_shapes=[
            pltpu.VMEM((4, 4 * keys, 512), BF16),
            pltpu.VMEM((7, 4 * keys, 256), BF16),
            pltpu.VMEM((4, 4 * keys, 128), BF16),
            pltpu.VMEM((256, 256), BF16),
            pltpu.VMEM((block, 1024), F32),
            pltpu.VMEM((block, 1024), BF16),
        ],
        compiler_params=pltpu.CompilerParams(vmem_limit_bytes=48 << 20),
        cost_estimate=pl.CostEstimate(flops=6 * 10**9, bytes_accessed=10 * 10**6, transcendentals=10**6),
        name="flow_step",
    )(q, hv, latents, noise, cond, vhw)


def places():
    dp, tensor = lax.axis_index("dp"), lax.axis_index("tensor")
    return dp // 4, (tensor // 4) * 2 + (dp // 2) % 2, tensor % 4, dp % 2


def device_at(x, y, z, core):
    return (x * 4 + (y % 2) * 2 + core, (y // 2) * 4 + z)


def link_partners(x, y, z, core):
    pair = lambda i: i + 1 - 2 * (i % 2)
    other = lambda i: 3 - i
    return (
        device_at(pair(x), y, z, core),
        device_at(other(x), y, z, core),
        device_at(x, pair(y), z, core),
        device_at(x, other(y), z, core),
        device_at(x, y, pair(z), core),
        device_at(x, y, other(z), core),
    )


def gray_bits(i):
    return (i + i // 2) % 2, i // 2


def grad_kernel(nt_ref, dq_ref, out_ref, *scratch):
    mine, away, sibling_part = scratch[0:6], scratch[6:12], scratch[12:18]
    landing = [scratch[18 + 6 * p : 24 + 6 * p] for p in range(6)]
    core_send, core_recv, send_sem, recv_sem = scratch[54:58]
    x, y, z, core = places()
    partners = link_partners(x, y, z, core)
    sibling = device_at(x, y, z, 1 - core)
    bits = gray_bits(x) + gray_bits(y) + gray_bits(z)

    barrier = pltpu.get_barrier_semaphore()
    for device in partners + (sibling,):
        pl.semaphore_signal(barrier, inc=1, device_id=device, device_id_type=MESH)
    pl.semaphore_wait(barrier, 7)

    def product(p, which, target):
        columns = pl.ds(STARTS[p], PIECES[p])

        def part(i, carry):
            rows = nt_ref[which, pl.ds(pl.multiple_of(i * 512, 512), 512), :]
            value = nn_dot(rows, dq_ref[:, columns]).astype(BF16)
            target[i] = value.reshape(2, 2, 2, 2, 2, ROWS_PAD, PIECES[p])
            return carry

        lax.fori_loop(0, 2, part, 0)

    def region(p, k, bit):
        index = []
        for dim in range(6):
            age = (dim - p) % 6
            index.append(bits[dim] if age < k else bit if age == k else slice(None))
        return tuple(index)

    def to_sibling(p):
        return pltpu.make_async_remote_copy(
            src_ref=away[p],
            dst_ref=sibling_part[p],
            send_sem=core_send.at[p],
            recv_sem=core_recv.at[p],
            device_id=sibling,
            device_id_type=MESH,
        )

    def exchange(p, k):
        dim = (p + k) % 6
        return pltpu.make_async_remote_copy(
            src_ref=mine[p].at[region(p, k, 1 - bits[dim])],
            dst_ref=landing[p][k],
            send_sem=send_sem.at[p, k],
            recv_sem=recv_sem.at[p, k],
            device_id=partners[dim],
            device_id_type=MESH,
        )

    sent = []
    flying = {}

    def send(p, copy):
        copy.start()
        flying[p] = copy
        sent.append(copy)

    def settle(p, k):
        flying[p].wait_recv()
        if k == 0:
            index = (slice(None),) * 6
            arrived = sibling_part[p]
        else:
            index = region(p, k - 1, bits[(p + k - 1) % 6])
            arrived = landing[p][k - 1]
        total = mine[p][index].astype(F32) + arrived[...].astype(F32)
        if k == 6:
            out_ref[:, STARTS[p] : STARTS[p] + PIECES[p]] = total
        else:
            mine[p][index] = total.astype(BF16)
            send(p, exchange(p, k))

    for p in range(7):
        if p < 6:
            product(p, 1 - core, away[p])
            send(p, to_sibling(p))
            product(p, core, mine[p])
        if p > 0:
            settle(p - 1, 0)
    for k in range(1, 7):
        for p in range(6):
            settle(p, k)
    for copy in sent:
        copy.wait_send()


def summed_gradient(normed_t, dq):
    tokens = dq.shape[0]
    full = [pltpu.VMEM((2,) * 6 + (ROWS_PAD, c), BF16) for c in PIECES]
    parts = [pltpu.VMEM((2,) * (5 - k) + (ROWS_PAD, c), BF16) for c in PIECES for k in range(6)]
    out = pl.pallas_call(
        grad_kernel,
        out_shape=jax.ShapeDtypeStruct((ROWS_PAD, W), F32),
        in_specs=[pl.BlockSpec(memory_space=pltpu.VMEM)] * 2,
        out_specs=pl.BlockSpec(memory_space=pltpu.VMEM),
        scratch_shapes=full
        + full
        + full
        + parts
        + [
            pltpu.SemaphoreType.DMA((6,)),
            pltpu.SemaphoreType.DMA((6,)),
            pltpu.SemaphoreType.DMA((6, 6)),
            pltpu.SemaphoreType.DMA((6, 6)),
        ],
        compiler_params=pltpu.CompilerParams(
            collective_id=1, has_side_effects=True, vmem_limit_bytes=48 << 20
        ),
        name="grad_sum",
    )(normed_t.reshape(2, -1, tokens), dq)
    return out[:ROWS_BLOCK]


def attend(m, owner_ref, len_ref, q_ref, pk_ref, pv_ref, ok_ref, ov_ref, att):
    prompt = owner_ref[0, m]
    length = len_ref[prompt]
    scale = 1.0 / HEAD**0.5
    own_k, own_v = ok_ref[prompt], ov_ref[prompt]
    keys, values = pk_ref[prompt], pv_ref[prompt]
    states = q_ref[prompt]
    heads = states.shape[1] // HEAD
    rows = jnp.concatenate([states[:, j * HEAD : (j + 1) * HEAD] for j in range(heads)], 0)
    first = nt_dot(rows, keys) * scale
    second = nt_dot(rows, own_k) * scale
    column = lax.broadcasted_iota(jnp.int32, first.shape, 1)
    first = jnp.where(column < length, first, -jnp.inf)
    row = lax.broadcasted_iota(jnp.int32, second.shape, 0) % NQ
    column = lax.broadcasted_iota(jnp.int32, second.shape, 1)
    second = jnp.where(column <= row, second, -jnp.inf)
    top = jnp.maximum(jnp.max(first, -1, keepdims=True), jnp.max(second, -1, keepdims=True))
    first, second = jnp.exp(first - top), jnp.exp(second - top)
    total = jnp.sum(first, -1, keepdims=True) + jnp.sum(second, -1, keepdims=True)
    out = nn_dot(first.astype(BF16), values) + nn_dot(second.astype(BF16), own_v)
    out = (out / total).astype(BF16)
    rows_at = pl.ds(pl.multiple_of(m * NQ, NQ), NQ)
    for j in range(heads):
        att[rows_at, j * HEAD : (j + 1) * HEAD] = out[j * NQ : (j + 1) * NQ]


def greet(devices):
    barrier = pltpu.get_barrier_semaphore()
    for device in devices:
        pl.semaphore_signal(barrier, inc=1, device_id=device, device_id_type=MESH)
    pl.semaphore_wait(barrier, len(devices))


def project_kernel(
    owner_ref,
    len_ref,
    q_ref,
    pk_ref,
    pv_ref,
    ok_ref,
    ov_ref,
    res_ref,
    w_ref,
    gain_ref,
    scaled_ref,
    sq_ref,
    att,
    wg,
    terms,
    land1,
    land2,
    zsum,
    landy,
    own_sem,
    w_send,
    w_recv,
    r_send,
    r_recv,
    y_send,
    y_recv,
):
    x, y, z, core = places()
    y_lo, y_hi = y % 2, y // 2
    xp, xo, xf = x + 1 - 2 * (x % 2), 3 - x, (x + 2) % 4
    at_y = device_at(x, y + 1 - 2 * y_lo, z, core)
    at_xp, at_xo = device_at(xp, y, z, core), device_at(xo, y, z, core)
    at_ze, at_zo = device_at(x, y, z + 1 - 2 * (z % 2), core), device_at(x, y, 3 - z, core)
    at_far = device_at(x, (y + 2) % 4, z, core)
    at_sib = device_at(x, y, z, 1 - core)
    bit_a, bit_b = gray_bits(z)
    sent, shared = [], []

    greet((at_y, at_xp, at_xo, at_ze, at_zo, at_far, at_sib))

    def share(xs, ys, h, target, own=False):
        slot = wg.at[xs, ys, core, h]
        number = len(shared)
        shared.append(target)
        copy = pltpu.make_async_remote_copy(
            src_ref=w_ref.at[:, h * 256 : (h + 1) * 256] if own else slot,
            dst_ref=slot,
            send_sem=w_send.at[number],
            recv_sem=w_recv.at[xs, ys, core, h],
            device_id=target,
            device_id_type=MESH,
        )
        copy.start()
        sent.append(copy)

    def arrived(xs, ys, cs, h):
        slot = wg.at[xs, ys, cs, h]
        pltpu.make_async_remote_copy(
            src_ref=slot,
            dst_ref=slot,
            send_sem=w_send.at[0],
            recv_sem=w_recv.at[xs, ys, cs, h],
            device_id=at_sib,
            device_id_type=MESH,
        ).wait_recv()

    def pass_on(xs, ys, h, *targets):
        arrived(xs, ys, core, h)
        for target in targets:
            share(xs, ys, h, target)

    keep = [
        pltpu.make_async_copy(w_ref.at[:, h * 256 : (h + 1) * 256], wg.at[x, y_lo, core, h], own_sem.at[h])
        for h in range(2)
    ]
    for h in range(2):
        for target in (at_xp, at_y, at_xo, at_sib):
            share(x, y_lo, h, target, own=True)
        keep[h].start()

    def prompts(start, end):
        def body(m, carry):
            attend(m, owner_ref, len_ref, q_ref, pk_ref, pv_ref, ok_ref, ov_ref, att)
            return carry

        lax.fori_loop(start, end, body, 0)

    prompts(0, 4)
    pass_on(x, 1 - y_lo, 0, at_xp, at_xo, at_sib)
    pass_on(xp, y_lo, 0, at_sib)
    pass_on(xo, y_lo, 0, at_xp, at_sib)
    prompts(4, 8)
    pass_on(x, 1 - y_lo, 1, at_xp, at_xo, at_sib)
    pass_on(xp, y_lo, 1, at_xo, at_sib)
    pass_on(xo, y_lo, 1, at_sib)
    for copy in keep:
        copy.wait()

    def reduce_copy(s, part, phase):
        block = terms.at[s, part]
        if phase == 0:
            source = block.at[1 - bit_a] if part == 0 else block.at[:, 1 - bit_b]
            landing = land1.at[s, part]
        else:
            source = block.at[bit_a, 1 - bit_b] if part == 0 else block.at[1 - bit_a, bit_b]
            landing = land2.at[s, part]
        return pltpu.make_async_remote_copy(
            src_ref=source,
            dst_ref=landing,
            send_sem=r_send.at[s, part, phase],
            recv_sem=r_recv.at[s, part, phase],
            device_id=at_ze if part == phase else at_zo,
            device_id_type=MESH,
        )

    flying = {}

    def launch(key, copy):
        copy.start()
        sent.append(copy)
        flying[key] = copy

    def multiply(s, half, cs, h):
        def body(i, carry):
            u, v = i // 2, i % 2
            value = nn_dot(att[...], wg[2 * half + u, v, cs, h]).astype(BF16)
            a, b = (u + v) % 2, u
            terms[s, 0, a, b] = value[:256]
            terms[s, 1, a, b] = value[256:]
            return carry

        lax.fori_loop(0, 4, body, 0)
        for part in range(2):
            launch((s, part), reduce_copy(s, part, 0))

    def halve(s):
        for part in range(2):
            flying[s, part].wait_recv()
            index = (s, 0, bit_a) if part == 0 else (s, 1, slice(None), bit_b)
            total = terms[index].astype(F32) + land1[s, part].astype(F32)
            terms[index] = total.astype(BF16)
            launch((s, part), reduce_copy(s, part, 1))

    def finish(s, half):
        for part in range(2):
            flying[s, part].wait_recv()
            total = terms[s, part, bit_a, bit_b].astype(F32) + land2[s, part].astype(F32)
            zsum[half, s % 4, part * 256 : (part + 1) * 256] = total.astype(BF16)
        if s >= 4:
            i = s - 4
            launch(
                ("y", i),
                pltpu.make_async_remote_copy(
                    src_ref=zsum.at[1 - y_hi, i],
                    dst_ref=landy.at[i],
                    send_sem=y_send.at[i],
                    recv_sem=y_recv.at[i],
                    device_id=at_far,
                    device_id_type=MESH,
                ),
            )

    def close(i, cs, h):
        flying["y", i].wait_recv()
        columns = pl.ds(pl.multiple_of(cs * 512 + h * 256, 256), 256)
        gain = gain_ref[:, columns]

        def body(m, carry):
            rows = pl.ds(pl.multiple_of(m * NQ, NQ), NQ)
            value = res_ref[owner_ref[0, m], :, columns].astype(F32)
            value = value + (zsum[y_hi, i, rows, :].astype(F32) + landy[i, rows, :].astype(F32))
            scaled_ref[rows, columns] = (value * gain).astype(BF16)
            square = value * value
            square = square[:, :128] + square[:, 128:]
            sq_ref[rows, :] = square if i == 0 else sq_ref[rows, :] + square
            return carry

        lax.fori_loop(0, 8, body, 0)

    halves = (x // 2, 1 - x // 2)
    order = [(halves[s // 4], (core, 1 - core)[s % 2], s // 2 % 2) for s in range(8)]
    for s in range(8):
        half, cs, h = order[s]
        if s == 0:
            pass_on(xp, 1 - y_lo, 0, at_sib)
        if s == 1:
            for xs in (x, xp):
                for ys in (y_lo, 1 - y_lo):
                    arrived(xs, ys, 1 - core, 0)
        if s == 2:
            pass_on(xp, 1 - y_lo, 1, at_sib)
            pass_on(xf, y_lo, 0, at_y, at_sib)
            pass_on(xf, y_lo, 1, at_y, at_sib)
        if s == 3:
            for xs in (x, xp):
                for ys in (y_lo, 1 - y_lo):
                    arrived(xs, ys, 1 - core, 1)
            pass_on(xo, 1 - y_lo, 0, at_sib)
            pass_on(xo, 1 - y_lo, 1, at_sib)
        if s in (4, 6):
            pass_on(xf, 1 - y_lo, s // 2 - 2, at_sib)
        if s in (5, 7):
            for xs in (xo, xf):
                for ys in (y_lo, 1 - y_lo):
                    arrived(xs, ys, 1 - core, s // 2 - 2)
        multiply(s, half, cs, h)
        if s >= 2:
            halve(s - 2)
        if s >= 4:
            finish(s - 4, order[s - 4][0])
    halve(6)
    finish(4, order[4][0])
    halve(7)
    for s in range(5, 8):
        finish(s, order[s][0])
        close(s - 5, *order[s - 1][1:])
    close(3, *order[7][1:])
    for copy in sent:
        copy.wait_send()


def projected(owner, lengths, query_states, prompt_keys, prompt_values, query_keys, query_values, residual, weight, gain):
    rows = query_states.shape[0] * NQ
    vmem, smem = pl.BlockSpec(memory_space=pltpu.VMEM), pl.BlockSpec(memory_space=pltpu.SMEM)
    return pl.pallas_call(
        project_kernel,
        out_shape=[jax.ShapeDtypeStruct((rows, 1024), BF16), jax.ShapeDtypeStruct((rows, 128), F32)],
        in_specs=[smem, smem] + [vmem] * 8,
        out_specs=[vmem] * 2,
        scratch_shapes=[
            pltpu.VMEM((rows, 1024), BF16),
            pltpu.VMEM((4, 2, 2, 2, 1024, 256), BF16),
            pltpu.VMEM((8, 2, 2, 2, 256, 256), BF16),
            pltpu.VMEM((8, 2, 2, 256, 256), BF16),
            pltpu.VMEM((8, 2, 256, 256), BF16),
            pltpu.VMEM((2, 4, rows, 256), BF16),
            pltpu.VMEM((4, rows, 256), BF16),
            pltpu.SemaphoreType.DMA((2,)),
            pltpu.SemaphoreType.DMA((32,)),
            pltpu.SemaphoreType.DMA((4, 2, 2, 2)),
            pltpu.SemaphoreType.DMA((8, 2, 2)),
            pltpu.SemaphoreType.DMA((8, 2, 2)),
            pltpu.SemaphoreType.DMA((4,)),
            pltpu.SemaphoreType.DMA((4,)),
        ],
        compiler_params=pltpu.CompilerParams(
            collective_id=2, has_side_effects=True, vmem_limit_bytes=58 << 20
        ),
        name="attend_project",
    )(
        owner,
        lengths,
        query_states,
        prompt_keys,
        prompt_values,
        query_keys,
        query_values,
        residual,
        weight,
        gain.reshape(1, -1),
    )


COLUMNS = 256
CHUNKS = 2 * W // COLUMNS
TOKENS = 256


def connect_kernel(
    step_ref,
    scaled_ref,
    sq_ref,
    lat_ref,
    noise_ref,
    pw_ref,
    vec_ref,
    vhw_ref,
    pwt_ref,
    col_ref,
    conn_hbm,
    qm_hbm,
    cond_ref,
    hv_ref,
    q_hbm,
    nt_hbm,
    conn,
    qm,
    q_out,
    nt_out,
    buf,
    land1,
    land2,
    land3,
    sqb,
    sq1,
    sq2,
    sq3,
    load_sem,
    out_sem,
    send_sem,
    recv_sem,
):
    x, y, z, core = places()
    y_hi = y // 2
    at_ze, at_zo = device_at(x, y, z + 1 - 2 * (z % 2), core), device_at(x, y, 3 - z, core)
    at_far = device_at(x, (y + 2) % 4, z, core)
    bit_a, bit_b = gray_bits(z)
    loads = [
        pltpu.make_async_copy(
            conn_hbm.at[:, part * 512 : (part + 1) * 512], conn.at[:, part * 512 : (part + 1) * 512], load_sem.at[part]
        )
        for part in range(7)
    ]
    loads.append(pltpu.make_async_copy(qm_hbm, qm, load_sem.at[7]))
    for copy in loads:
        copy.start()

    greet((at_ze, at_zo, at_far))

    sent = []
    flying = {}

    def send(j, phase):
        if j == CHUNKS:
            block, landing = sqb, (sq1, sq2, sq3)[phase]
        else:
            block, landing = buf.at[j], (land1, land2, land3)[phase].at[j]
        if phase == 0:
            source = block.at[:, 1 - bit_a] if j % 2 == 0 else block.at[:, :, 1 - bit_b]
        elif phase == 1:
            source = block.at[:, bit_a, 1 - bit_b] if j % 2 == 0 else block.at[:, 1 - bit_a, bit_b]
        else:
            source = block.at[1 - y_hi, bit_a, bit_b]
        copy = pltpu.make_async_remote_copy(
            src_ref=source,
            dst_ref=landing,
            send_sem=send_sem.at[j, phase],
            recv_sem=recv_sem.at[j, phase],
            device_id=at_far if phase == 2 else at_ze if phase == j % 2 else at_zo,
            device_id_type=MESH,
        )
        copy.start()
        sent.append(copy)
        flying[j] = copy

    def settle(j, phase):
        flying[j].wait_recv()
        if phase == 0:
            index = (slice(None), bit_a) if j % 2 == 0 else (slice(None), slice(None), bit_b)
        else:
            index = (slice(None), bit_a, bit_b)
        if j == CHUNKS:
            sqb[index] = sqb[index] + (sq1, sq2)[phase][...]
        else:
            index = (j,) + index
            total = buf[index].astype(F32) + (land1, land2)[phase][j].astype(F32)
            buf[index] = total.astype(BF16)
        send(j, phase + 1)

    def prelude(c):
        t = (step_ref[0].astype(F32) + 0.5) / NT
        rows = pl.ds(c * TOKENS, TOKENS)
        noisy = ((1.0 - t) * lat_ref[rows, :].astype(F32) + t * noise_ref[rows, :].astype(F32)).astype(BF16)
        hidden = nn_dot(noisy, pw_ref[...]) + t * vec_ref[0:1, :]
        scale = lax.rsqrt(jnp.mean(hidden * hidden, -1, keepdims=True) + eps)
        normed = (hidden * scale * vec_ref[1:2, :]).astype(BF16)
        hv_ref[rows, :] = nn_dot(hidden.astype(BF16), vhw_ref[...])
        q_out[c] = nn_dot(normed, qm[...]).astype(BF16)
        ht = nt_dot(pwt_ref[...], noisy) + t * col_ref[:, 0:1]
        scale_t = lax.rsqrt(jnp.sum(ht * ht, 0, keepdims=True) / W + eps)
        normed_t = (ht * scale_t * col_ref[:, 1:2]).astype(BF16)
        for natural in range(128):
            place = place_of_block(natural) * ROWS_PAD
            nt_out[c, place : place + ROWS_PAD, :] = normed_t[natural * ROWS_PAD : (natural + 1) * ROWS_PAD]
        copies = (
            pltpu.make_async_copy(q_out.at[c], q_hbm.at[c * TOKENS : (c + 1) * TOKENS, :], out_sem.at[c, 0]),
            pltpu.make_async_copy(nt_out.at[c], nt_hbm.at[:, c * TOKENS : (c + 1) * TOKENS], out_sem.at[c, 1]),
        )
        for copy in copies:
            copy.start()
        return copies

    def spread(block, value):
        for m in range(8):
            a, b = gray_bits(m % 4)
            block[m // 4, a, b] = value[m * NQ : (m + 1) * NQ]

    spread(sqb, sq_ref[...])
    send(CHUNKS, 0)
    for j in range(CHUNKS):
        if j % 2 == 0:
            loads[j // 2].wait()
        value = nn_dot(scaled_ref[...], conn[:, j * COLUMNS : (j + 1) * COLUMNS])
        spread(buf.at[j], value.astype(BF16))
        send(j, 0)
    loads[7].wait()
    stores = []
    chunks = [CHUNKS] + list(range(CHUNKS))
    for c in range(4):
        stores += prelude(c)
        for j in chunks[4 * c : 4 * c + 4]:
            settle(j, 0)
        for j in chunks[max(4 * c - 4, 0) : 4 * c]:
            settle(j, 1)
    for j in chunks[12:]:
        settle(j, 1)
    flying[CHUNKS].wait_recv()
    squares = sqb[y_hi, bit_a, bit_b] + sq3[...]
    factor = lax.rsqrt(jnp.sum(squares, -1, keepdims=True) / D + eps)
    for j in range(CHUNKS):
        flying[j].wait_recv()
        total = buf[j, y_hi, bit_a, bit_b].astype(F32) + land3[j].astype(F32)
        cond_ref[:, j * COLUMNS : (j + 1) * COLUMNS] = (total * factor).astype(BF16)
    for copy in stores:
        copy.wait()
    for copy in sent:
        copy.wait_send()


def connected(
    timesteps, scaled, squares, latents, noise, patch_weight, time_embedding, image_norm_gain, vhw, conn_weight, qm
):
    tokens = latents.shape[0]
    blocks = W // ROWS_BLOCK
    pad = ((0, 0), (0, ROWS_PAD - ROWS_BLOCK), (0, 0))
    pwt = jnp.pad(patch_weight.T.reshape(blocks, ROWS_BLOCK, -1), pad).reshape(blocks * ROWS_PAD, -1)
    vec = jnp.stack([time_embedding, image_norm_gain])
    col = jnp.pad(vec.T.reshape(blocks, ROWS_BLOCK, 2), pad).reshape(blocks * ROWS_PAD, 2)
    vmem, smem = pl.BlockSpec(memory_space=pltpu.VMEM), pl.BlockSpec(memory_space=pltpu.SMEM)
    anywhere = pl.BlockSpec(memory_space=pl.ANY)
    return pl.pallas_call(
        connect_kernel,
        out_shape=[
            jax.ShapeDtypeStruct((NQ, 2 * W), BF16),
            jax.ShapeDtypeStruct((tokens, 128), F32),
            jax.ShapeDtypeStruct((tokens, W), BF16),
            jax.ShapeDtypeStruct((blocks * ROWS_PAD, tokens), BF16),
        ],
        in_specs=[smem] + [vmem] * 9 + [anywhere] * 2,
        out_specs=[vmem, vmem, anywhere, anywhere],
        scratch_shapes=[
            pltpu.VMEM(conn_weight.shape, BF16),
            pltpu.VMEM(qm.shape, BF16),
            pltpu.VMEM((4, TOKENS, W), BF16),
            pltpu.VMEM((4, blocks * ROWS_PAD, TOKENS), BF16),
            pltpu.VMEM((CHUNKS, 2, 2, 2, NQ, COLUMNS), BF16),
            pltpu.VMEM((CHUNKS, 2, 2, NQ, COLUMNS), BF16),
            pltpu.VMEM((CHUNKS, 2, NQ, COLUMNS), BF16),
            pltpu.VMEM((CHUNKS, NQ, COLUMNS), BF16),
            pltpu.VMEM((2, 2, 2, NQ, 128), F32),
            pltpu.VMEM((2, 2, NQ, 128), F32),
            pltpu.VMEM((2, NQ, 128), F32),
            pltpu.VMEM((NQ, 128), F32),
            pltpu.SemaphoreType.DMA((8,)),
            pltpu.SemaphoreType.DMA((4, 2)),
            pltpu.SemaphoreType.DMA((CHUNKS + 1, 3)),
            pltpu.SemaphoreType.DMA((CHUNKS + 1, 3)),
        ],
        compiler_params=pltpu.CompilerParams(
            collective_id=3, has_side_effects=True, vmem_limit_bytes=58 << 20
        ),
        name="connect_prelude",
    )(timesteps, scaled, squares, latents, noise, patch_weight, vec, vhw, pwt, col, conn_weight, qm)


def on_device(
    prompt_keys,
    prompt_values,
    query_states,
    query_keys,
    query_values,
    lengths,
    residual,
    out_weight,
    final_gain,
    conn_weight,
    owner,
    latents,
    noise,
    timesteps,
    patch_weight,
    time_embedding,
    image_norm_gain,
    query_matrix,
    velocity_head_weight,
):
    count_of_rows = lax.axis_size("dp") * lax.axis_size("tensor") * latents.shape[1]
    scaled, squares = projected(
        owner,
        lengths,
        query_states,
        prompt_keys,
        prompt_values,
        query_keys,
        query_values,
        residual,
        out_weight,
        final_gain,
    )
    cond, hv, q, normed_t = connected(
        timesteps,
        scaled,
        squares,
        latents[0],
        noise[0],
        patch_weight,
        time_embedding,
        image_norm_gain,
        velocity_head_weight,
        conn_weight,
        query_matrix,
    )
    velocity, dq = step(
        q, hv, latents[0], noise[0], cond, velocity_head_weight, grad_gain / math.sqrt(count_of_rows)
    )
    return (velocity[None], summed_gradient(normed_t, dq))


def solution(mesh):
    return jax.shard_map(
        on_device,
        mesh=mesh,
        in_specs=(
            P("dp", None, "tensor"),
            P("dp", None, "tensor"),
            P("dp", None, "tensor"),
            P("dp", None, "tensor"),
            P("dp", None, "tensor"),
            P("dp"),
            P("dp", None, "tensor"),
            P("tensor", "dp"),
            P("tensor"),
            P("tensor", None),
            P("dp", None),
            P(("dp", "tensor"), None, None),
            P(("dp", "tensor"), None, None),
            P(("dp", "tensor")),
            P(),
            P(),
            P(),
            P(),
            P(),
        ),
        out_specs=(P(("dp", "tensor"), None, None), P(("dp", "tensor"), None)),
        check_vma=False,
    )
```

```python
import math

import jax
import jax.numpy as jnp
from jax import lax
from jax.experimental import pallas as pl
from jax.experimental.pallas import tpu as pltpu
from jax.sharding import PartitionSpec as P

D = 8192
HEAD = 128
NQ = 64
DHEAD = 112
NT = 1000
W = 1792
IMG_HEADS = 16
F32 = jnp.float32
BF16 = jnp.bfloat16
MESH = pl.DeviceIdType.MESH

eps = 1e-06
grad_gain = 16.0

ROWS_BLOCK = 14
ROWS_PAD = 16
PIECES = (384, 384, 256, 256, 256, 256)
STARTS = (0, 384, 768, 1024, 1280, 1536)
KEY_WINDOWS = (0, 384, 896, 1280)
SCORE_WINDOWS = (0, 128, 256, 384, 512, 640, 768)


def nt_dot(a, b):
    return lax.dot_general(a, b, (((1,), (1,)), ((), ())), preferred_element_type=F32)


def nn_dot(a, b):
    return jnp.dot(a, b, preferred_element_type=F32)


def head_mask(rows, width, head, base):
    lane = lax.broadcasted_iota(jnp.int32, (rows, width), 1) + base
    return (lane >= head * DHEAD) & (lane < (head + 1) * DHEAD)


def only_head(block, head, base):
    return jnp.where(head_mask(*block.shape, head, base), block.astype(F32), 0.0).astype(BF16)


def step_kernel(
    gain, q_ref, hv_ref, lat_ref, noise_ref, cond_ref, vhw_ref, vel_ref, dq_ref, kbd, kflat, vw, ones, probs, dsc
):
    scale = 1.0 / DHEAD**0.5
    keys = cond_ref.shape[0]

    @pl.when(pl.program_id(0) == 0)
    def _():
        for g, base in enumerate(KEY_WINDOWS):
            vals = []
            for n in range(4):
                window = cond_ref[:, base : base + 512]
                kbd[g, n * keys : (n + 1) * keys, :] = only_head(window, 4 * g + n, base)
                window = cond_ref[:, W + base : W + base + 512]
                vals.append(only_head(window, 4 * g + n, base))
            vw[g] = nn_dot(jnp.concatenate(vals, 0), vhw_ref[base : base + 512, :]).astype(BF16)
        for tile, first in enumerate(SCORE_WINDOWS):
            for n in range(4):
                window = cond_ref[:, tile * 256 : (tile + 1) * 256]
                kflat[tile, n * keys : (n + 1) * keys, :] = only_head(window, first // keys + n, tile * 256)
        row = lax.broadcasted_iota(jnp.int32, (256, 256), 0) // keys
        column = lax.broadcasted_iota(jnp.int32, (256, 256), 1) // keys
        ones[...] = jnp.where(row == column, 1.0, 0.0).astype(BF16)

    velocity = hv_ref[...]
    for g, base in enumerate(KEY_WINDOWS):
        expo = jnp.exp(nt_dot(q_ref[:, base : base + 512], kbd[g]) * scale)
        total = nn_dot(jnp.minimum(expo, 3.38e38).astype(BF16), ones[...])
        p = expo / total
        probs[:, g * 256 : (g + 1) * 256] = p
        velocity = velocity + nn_dot(p.astype(BF16), vw[g])
    vel_ref[...] = velocity
    target = noise_ref[...].astype(F32) - lat_ref[...].astype(F32)
    dvel = ((velocity - target) * gain).astype(BF16)
    for g in range(4):
        p = probs[:, g * 256 : (g + 1) * 256]
        dprob = nt_dot(dvel, vw[g])
        both = p * dprob
        high = both.astype(BF16)
        low = (both - high.astype(F32)).astype(BF16)
        shift = nn_dot(high, ones[...]) + nn_dot(low, ones[...])
        dsc[:, g * 256 : (g + 1) * 256] = (p * (dprob - shift) * scale).astype(BF16)
    for tile, first in enumerate(SCORE_WINDOWS):
        dq_ref[:, tile * 256 : (tile + 1) * 256] = nn_dot(dsc[:, first : first + 256], kflat[tile]).astype(BF16)


def step(q, hv, latents, noise, cond, vhw, gain):
    tokens = q.shape[0]
    block = 256
    keys = cond.shape[0]
    whole = lambda a: pl.BlockSpec(a.shape, lambda i: (0,) * a.ndim)
    rows = lambda width: pl.BlockSpec((block, width), lambda i: (i, 0))
    return pl.pallas_call(
        lambda *refs: step_kernel(gain, *refs),
        grid=(tokens // block,),
        in_specs=[rows(W), rows(128), rows(128), rows(128), whole(cond), whole(vhw)],
        out_specs=[rows(128), rows(W)],
        out_shape=[jax.ShapeDtypeStruct((tokens, 128), F32), jax.ShapeDtypeStruct((tokens, W), BF16)],
        scratch_shapes=[
            pltpu.VMEM((4, 4 * keys, 512), BF16),
            pltpu.VMEM((7, 4 * keys, 256), BF16),
            pltpu.VMEM((4, 4 * keys, 128), BF16),
            pltpu.VMEM((256, 256), BF16),
            pltpu.VMEM((block, 1024), F32),
            pltpu.VMEM((block, 1024), BF16),
        ],
        compiler_params=pltpu.CompilerParams(vmem_limit_bytes=48 << 20),
        cost_estimate=pl.CostEstimate(flops=6 * 10**9, bytes_accessed=10 * 10**6, transcendentals=10**6),
        name="flow_step",
    )(q, hv, latents, noise, cond, vhw)


def places():
    dp, tensor = lax.axis_index("dp"), lax.axis_index("tensor")
    return dp // 4, (tensor // 4) * 2 + (dp // 2) % 2, tensor % 4, dp % 2


def device_at(x, y, z, core):
    return (x * 4 + (y % 2) * 2 + core, (y // 2) * 4 + z)


def link_partners(x, y, z, core):
    pair = lambda i: i + 1 - 2 * (i % 2)
    other = lambda i: 3 - i
    return (
        device_at(pair(x), y, z, core),
        device_at(other(x), y, z, core),
        device_at(x, pair(y), z, core),
        device_at(x, other(y), z, core),
        device_at(x, y, pair(z), core),
        device_at(x, y, other(z), core),
    )


def gray_bits(i):
    return (i + i // 2) % 2, i // 2


def grad_kernel(nt_ref, dq_ref, out_ref, *scratch):
    mine, away, sibling_part = scratch[0:6], scratch[6:12], scratch[12:18]
    landing = [scratch[18 + 6 * p : 24 + 6 * p] for p in range(6)]
    core_send, core_recv, send_sem, recv_sem = scratch[54:58]
    x, y, z, core = places()
    partners = link_partners(x, y, z, core)
    sibling = device_at(x, y, z, 1 - core)
    bits = gray_bits(x) + gray_bits(y) + gray_bits(z)

    barrier = pltpu.get_barrier_semaphore()
    for device in partners + (sibling,):
        pl.semaphore_signal(barrier, inc=1, device_id=device, device_id_type=MESH)
    pl.semaphore_wait(barrier, 7)

    def product(p, which, target):
        columns = pl.ds(STARTS[p], PIECES[p])

        def part(i, carry):
            rows = nt_ref[which, pl.ds(pl.multiple_of(i * 512, 512), 512), :]
            value = nn_dot(rows, dq_ref[:, columns]).astype(BF16)
            target[i] = value.reshape(2, 2, 2, 2, 2, ROWS_PAD, PIECES[p])
            return carry

        lax.fori_loop(0, 2, part, 0)

    def region(p, k, bit):
        index = []
        for dim in range(6):
            age = (dim - p) % 6
            index.append(bits[dim] if age < k else bit if age == k else slice(None))
        return tuple(index)

    def to_sibling(p):
        return pltpu.make_async_remote_copy(
            src_ref=away[p],
            dst_ref=sibling_part[p],
            send_sem=core_send.at[p],
            recv_sem=core_recv.at[p],
            device_id=sibling,
            device_id_type=MESH,
        )

    def exchange(p, k):
        dim = (p + k) % 6
        return pltpu.make_async_remote_copy(
            src_ref=mine[p].at[region(p, k, 1 - bits[dim])],
            dst_ref=landing[p][k],
            send_sem=send_sem.at[p, k],
            recv_sem=recv_sem.at[p, k],
            device_id=partners[dim],
            device_id_type=MESH,
        )

    sent = []
    flying = {}

    def send(p, copy):
        copy.start()
        flying[p] = copy
        sent.append(copy)

    def settle(p, k):
        flying[p].wait_recv()
        if k == 0:
            index = (slice(None),) * 6
            arrived = sibling_part[p]
        else:
            index = region(p, k - 1, bits[(p + k - 1) % 6])
            arrived = landing[p][k - 1]
        total = mine[p][index].astype(F32) + arrived[...].astype(F32)
        if k == 6:
            out_ref[:, STARTS[p] : STARTS[p] + PIECES[p]] = total
        else:
            mine[p][index] = total.astype(BF16)
            send(p, exchange(p, k))

    for p in range(7):
        if p < 6:
            product(p, 1 - core, away[p])
            send(p, to_sibling(p))
            product(p, core, mine[p])
        if p > 0:
            settle(p - 1, 0)
    for k in range(1, 7):
        for p in range(6):
            settle(p, k)
    for copy in sent:
        copy.wait_send()


def summed_gradient(normed_t, dq):
    tokens = dq.shape[0]
    full = [pltpu.VMEM((2,) * 6 + (ROWS_PAD, c), BF16) for c in PIECES]
    parts = [pltpu.VMEM((2,) * (5 - k) + (ROWS_PAD, c), BF16) for c in PIECES for k in range(6)]
    out = pl.pallas_call(
        grad_kernel,
        out_shape=jax.ShapeDtypeStruct((ROWS_PAD, W), F32),
        in_specs=[pl.BlockSpec(memory_space=pltpu.VMEM)] * 2,
        out_specs=pl.BlockSpec(memory_space=pltpu.VMEM),
        scratch_shapes=full
        + full
        + full
        + parts
        + [
            pltpu.SemaphoreType.DMA((6,)),
            pltpu.SemaphoreType.DMA((6,)),
            pltpu.SemaphoreType.DMA((6, 6)),
            pltpu.SemaphoreType.DMA((6, 6)),
        ],
        compiler_params=pltpu.CompilerParams(
            collective_id=1, has_side_effects=True, vmem_limit_bytes=48 << 20
        ),
        name="grad_sum",
    )(normed_t.reshape(2, -1, tokens), dq)
    return out[:ROWS_BLOCK]


def attend(m, owner_ref, len_ref, q_ref, pk_ref, pv_ref, ok_ref, ov_ref, att):
    prompt = owner_ref[0, m]
    length = len_ref[prompt]
    scale = 1.0 / HEAD**0.5
    own_k, own_v = ok_ref[prompt], ov_ref[prompt]
    keys, values = pk_ref[prompt], pv_ref[prompt]
    states = q_ref[prompt]
    heads = states.shape[1] // HEAD
    rows = jnp.concatenate([states[:, j * HEAD : (j + 1) * HEAD] for j in range(heads)], 0)
    first = nt_dot(rows, keys) * scale
    second = nt_dot(rows, own_k) * scale
    column = lax.broadcasted_iota(jnp.int32, first.shape, 1)
    first = jnp.where(column < length, first, -jnp.inf)
    row = lax.broadcasted_iota(jnp.int32, second.shape, 0) % NQ
    column = lax.broadcasted_iota(jnp.int32, second.shape, 1)
    second = jnp.where(column <= row, second, -jnp.inf)
    top = jnp.maximum(jnp.max(first, -1, keepdims=True), jnp.max(second, -1, keepdims=True))
    first, second = jnp.exp(first - top), jnp.exp(second - top)
    total = jnp.sum(first, -1, keepdims=True) + jnp.sum(second, -1, keepdims=True)
    out = nn_dot(first.astype(BF16), values) + nn_dot(second.astype(BF16), own_v)
    out = (out / total).astype(BF16)
    rows_at = pl.ds(pl.multiple_of(m * NQ, NQ), NQ)
    for j in range(heads):
        att[rows_at, j * HEAD : (j + 1) * HEAD] = out[j * NQ : (j + 1) * NQ]


def greet(devices):
    barrier = pltpu.get_barrier_semaphore()
    for device in devices:
        pl.semaphore_signal(barrier, inc=1, device_id=device, device_id_type=MESH)
    pl.semaphore_wait(barrier, len(devices))


TOKENS = 256
GRAD_ROWS = 2048


def one_hot_rows(start, rows):
    row = lax.broadcasted_iota(jnp.int32, (rows, 1), 0) + start
    bit = lambda n: row // (ROWS_PAD << n) % 2
    at = lambda n: 2 * bit(n) + (bit(n) + bit(n + 1)) % 2
    z, y, x, core = at(0), at(2), at(4), bit(6)
    natural = ((x * 2 + y % 2) * 2 + core) * 8 + y // 2 * 4 + z
    inside = row % ROWS_PAD
    source = jnp.where(inside < ROWS_BLOCK, natural * ROWS_BLOCK + inside, -1)
    lane = lax.broadcasted_iota(jnp.int32, (rows, W), 1)
    return jnp.where(lane == source, 1.0, 0.0).astype(BF16)


def split_in_three(value):
    parts = []
    for _ in range(3):
        part = value.astype(BF16)
        parts.append(part)
        value = value - part.astype(F32)
    return parts


def project_kernel(
    owner_ref,
    len_ref,
    step_ref,
    q_ref,
    pk_ref,
    pv_ref,
    ok_ref,
    ov_ref,
    res_ref,
    gain_ref,
    lat_ref,
    noise_ref,
    pw_ref,
    time_ref,
    norm_ref,
    vhw_ref,
    w_hbm,
    qm_hbm,
    scaled_ref,
    sq_ref,
    hv_ref,
    q_hbm,
    nt_hbm,
    att,
    wg,
    terms,
    land_near,
    land_far,
    land_both,
    land_last,
    zsum,
    landy,
    qm,
    packed,
    pwt,
    col,
    q_out,
    nt_out,
    own_sem,
    qm_sem,
    out_sem,
    w_send,
    w_recv,
    r_send,
    r_recv,
    y_send,
    y_recv,
):
    x, y, z, core = places()
    y_lo, y_hi = y % 2, y // 2
    xp, xo, xf = x + 1 - 2 * (x % 2), 3 - x, (x + 2) % 4
    at_y = device_at(x, y + 1 - 2 * y_lo, z, core)
    at_xp, at_xo = device_at(xp, y, z, core), device_at(xo, y, z, core)
    at_ze, at_zo = device_at(x, y, z + 1 - 2 * (z % 2), core), device_at(x, y, 3 - z, core)
    at_far = device_at(x, (y + 2) % 4, z, core)
    at_sib = device_at(x, y, z, 1 - core)
    bit_a, bit_b = gray_bits(z)
    shared = []

    keep = [
        pltpu.make_async_copy(w_hbm.at[:, h * 256 : (h + 1) * 256], wg.at[x, y_lo, core, h], own_sem.at[h])
        for h in range(2)
    ]
    load_qm = pltpu.make_async_copy(qm_hbm, qm, qm_sem.at[0])
    for copy in keep + [load_qm]:
        copy.start()
    greet((at_y, at_xp, at_xo, at_ze, at_zo, at_far, at_sib))

    def share(xs, ys, h, *targets):
        slot = wg.at[xs, ys, core, h]
        for target in targets:
            copy = pltpu.make_async_remote_copy(
                src_ref=slot,
                dst_ref=slot,
                send_sem=w_send.at[len(shared)],
                recv_sem=w_recv.at[xs, ys, core, h],
                device_id=target,
                device_id_type=MESH,
            )
            copy.start()
            shared.append(copy)

    def arrived(xs, ys, cs, h):
        slot = wg.at[xs, ys, cs, h]
        pltpu.make_async_remote_copy(
            src_ref=slot,
            dst_ref=slot,
            send_sem=w_send.at[0],
            recv_sem=w_recv.at[xs, ys, cs, h],
            device_id=at_sib,
            device_id_type=MESH,
        ).wait_recv()

    def pass_on(xs, ys, h, *targets):
        arrived(xs, ys, core, h)
        share(xs, ys, h, *targets)

    def prepare():
        packed[0:128, :] = pw_ref[...]
        parts = split_in_three(time_ref[...]) + split_in_three(norm_ref[...])
        packed[128:256, :] = jnp.concatenate(parts + [jnp.zeros((122, W), BF16)], 0)

        def body(i, carry):
            rows = pl.ds(pl.multiple_of(i * 256, 256), 256)
            value = nt_dot(one_hot_rows(i * 256, 256), packed[...])
            pwt[rows, :] = value[:, :128].astype(BF16)
            col[rows, :] = value[:, 128:]
            return carry

        lax.fori_loop(0, GRAD_ROWS // 256, body, 0)

    def prelude(c):
        t = (step_ref[0].astype(F32) + 0.5) / NT
        rows = pl.ds(c * TOKENS, TOKENS)
        noisy = ((1.0 - t) * lat_ref[rows, :].astype(F32) + t * noise_ref[rows, :].astype(F32)).astype(BF16)
        hidden = nn_dot(noisy, pw_ref[...]) + t * time_ref[...]
        scale = lax.rsqrt(jnp.mean(hidden * hidden, -1, keepdims=True) + eps)
        normed = (hidden * scale * norm_ref[...]).astype(BF16)
        hv_ref[rows, :] = nn_dot(hidden.astype(BF16), vhw_ref[...])
        q_out[...] = nn_dot(normed, qm[...]).astype(BF16)
        time_col = col[:, 0:1] + col[:, 1:2] + col[:, 2:3]
        norm_col = col[:, 3:4] + col[:, 4:5] + col[:, 5:6]
        ht = nt_dot(pwt[...], noisy) + t * time_col
        scale_t = lax.rsqrt(jnp.sum(ht * ht, 0, keepdims=True) / W + eps)
        nt_out[...] = (ht * scale_t * norm_col).astype(BF16)
        copies = (
            pltpu.make_async_copy(q_out, q_hbm.at[c * TOKENS : (c + 1) * TOKENS, :], out_sem.at[c, 0]),
            pltpu.make_async_copy(nt_out, nt_hbm.at[:, c * TOKENS : (c + 1) * TOKENS], out_sem.at[c, 1]),
        )
        for copy in copies:
            copy.start()
        return copies

    def prompts(start, end):
        def body(m, carry):
            attend(m, owner_ref, len_ref, q_ref, pk_ref, pv_ref, ok_ref, ov_ref, att)
            return carry

        lax.fori_loop(start, end, body, 0)

    sources = (x, xp, xo, xf)
    second_bits = tuple(xs % 2 for xs in sources)
    subs = ((core, 0), (1 - core, 0), (core, 1), (1 - core, 1))

    def keeper(batch):
        return bit_b == second_bits[batch]

    def giver(batch):
        return bit_b != second_bits[batch]

    def remote(s, which, source, landing, device):
        return pltpu.make_async_remote_copy(
            src_ref=source,
            dst_ref=landing,
            send_sem=r_send.at[s, which],
            recv_sem=r_recv.at[s, which],
            device_id=device,
            device_id_type=MESH,
        )

    def near(s):
        return remote(s, 0, terms.at[s, 0, 1 - bit_a], land_near.at[s], at_ze)

    def far(s):
        return remote(s, 1, terms.at[s, 0, bit_a], land_far.at[s // 8, s % 4], at_zo)

    def both(s):
        return remote(s, 2, terms.at[s, 1], land_both.at[s // 8, s % 4], at_zo)

    def last(s):
        return remote(s, 3, terms.at[s, 1, 1 - bit_a], land_last.at[s // 8, s % 4], at_ze)

    def multiply(s):
        batch = s // 4
        cs, h = subs[s % 4]

        def body(v, carry):
            value = nn_dot(att[...], wg[sources[batch], v, cs, h]).astype(BF16)
            a = (second_bits[batch] + v) % 2
            terms[s, 0, a] = value[:256]
            terms[s, 1, a] = value[256:]
            return carry

        lax.fori_loop(0, 2, body, 0)
        near(s).start()

        @pl.when(giver(batch))
        def _():
            both(s).start()

    def halve(s):
        batch = s // 4
        near(s).wait_recv()
        total = terms[s, 0, bit_a].astype(F32) + land_near[s].astype(F32)
        terms[s, 0, bit_a] = total.astype(BF16)

        @pl.when(giver(batch))
        def _():
            far(s).start()

        @pl.when(keeper(batch))
        def _():
            both(s).wait_recv()
            total = terms[s, 1].astype(F32) + land_both[s // 8, s % 4].astype(F32)
            terms[s, 1] = total.astype(BF16)
            last(s).start()

    def finish(s):
        @pl.when(keeper(s // 4))
        def _():
            far(s).wait_recv()
            total = terms[s, 0, bit_a].astype(F32) + land_far[s // 8, s % 4].astype(F32)
            zsum[s // 8, s % 4, 0:256] = total.astype(BF16)
            last(s).wait_recv()
            total = terms[s, 1, bit_a].astype(F32) + land_last[s // 8, s % 4].astype(F32)
            zsum[s // 8, s % 4, 256:512] = total.astype(BF16)

    def across(p, i):
        return pltpu.make_async_remote_copy(
            src_ref=zsum.at[p, i],
            dst_ref=landy.at[i],
            send_sem=y_send.at[i],
            recv_sem=y_recv.at[i],
            device_id=at_far,
            device_id_type=MESH,
        )

    def cross(p, i):
        @pl.when((y_hi != x // 2) if p == 0 else (y_hi == x // 2))
        def _():
            across(p, i).start()

    def close(i):
        across(0, i).wait_recv()
        mine = (x // 2 + y_hi) % 2
        cs, h = subs[i]
        columns = pl.ds(pl.multiple_of(cs * 512 + h * 256, 256), 256)
        gain = gain_ref[:, columns]

        def body(m, carry):
            rows = pl.ds(pl.multiple_of(m * NQ, NQ), NQ)
            value = res_ref[owner_ref[0, m], :, columns].astype(F32)
            value = value + (zsum[mine, i, rows, :].astype(F32) + landy[i, rows, :].astype(F32))
            scaled_ref[rows, columns] = (value * gain).astype(BF16)
            square = value * value
            square = square[:, :128] + square[:, 128:]
            sq_ref[rows, :] = square if i == 0 else sq_ref[rows, :] + square
            return carry

        lax.fori_loop(0, 8, body, 0)

    def from_sibling(xs, h):
        for ys in (y_lo, 1 - y_lo):
            arrived(xs, ys, 1 - core, h)

    def steps(batch, h, lag_halve=4, lag_finish=8):
        for s in (4 * batch + 2 * h, 4 * batch + 2 * h + 1):
            if s % 2 == 1:
                from_sibling(sources[batch], h)
            multiply(s)
            if s >= lag_halve:
                halve(s - lag_halve)
            if s >= lag_finish:
                settle(s - lag_finish)

    def settle(s):
        finish(s)
        if 4 <= s < 8:
            cross(0, s - 4)
        if s >= 12:
            cross(1, s - 12)

    keep[0].wait()
    share(x, y_lo, 0, at_y, at_xp, at_xo, at_sib)
    prompts(0, 8)
    keep[1].wait()
    share(x, y_lo, 1, at_y)
    prepare()
    pass_on(x, 1 - y_lo, 0, at_xp, at_xo, at_sib)
    share(x, y_lo, 1, at_xp, at_xo, at_sib)
    pass_on(xp, y_lo, 0, at_sib)
    pass_on(xo, y_lo, 0, at_sib)
    steps(0, 0)
    load_qm.wait()
    stores = prelude(0)
    pass_on(x, 1 - y_lo, 1, at_xp, at_xo, at_sib)
    steps(0, 1)
    for copy in stores:
        copy.wait()
    stores = prelude(1)
    pass_on(xp, 1 - y_lo, 0, at_sib)
    share(xo, y_lo, 0, at_xp)
    pass_on(xp, y_lo, 1, at_xo, at_sib)
    pass_on(xo, y_lo, 1, at_sib)
    steps(1, 0)
    pass_on(xo, 1 - y_lo, 0, at_sib)
    for copy in stores:
        copy.wait()
    stores = prelude(2)
    pass_on(xp, 1 - y_lo, 1, at_sib)
    steps(1, 1)
    pass_on(xf, y_lo, 0, at_y, at_sib)
    steps(2, 0)
    pass_on(xo, 1 - y_lo, 1, at_sib)
    pass_on(xf, y_lo, 1, at_y, at_sib)
    steps(2, 1)
    for copy in stores:
        copy.wait()
    stores = prelude(3)
    pass_on(xf, 1 - y_lo, 0, at_sib)
    steps(3, 0)
    pass_on(xf, 1 - y_lo, 1, at_sib)
    steps(3, 1)
    settle(8)
    halve(12)
    settle(9)
    halve(13)
    settle(10)
    halve(14)
    settle(11)
    halve(15)
    for i in range(4):
        settle(12 + i)
        if i > 0:
            close(i - 1)
    close(3)
    for copy in stores:
        copy.wait()
    for copy in shared:
        copy.wait_send()
    for s in range(16):
        near(s).wait_send()

        @pl.when(giver(s // 4))
        def _():
            both(s).wait_send()
            far(s).wait_send()

        @pl.when(keeper(s // 4))
        def _():
            last(s).wait_send()

    for i in range(4):
        across(0, i).wait_send()


def projected(
    owner,
    lengths,
    timesteps,
    query_states,
    prompt_keys,
    prompt_values,
    query_keys,
    query_values,
    residual,
    gain,
    latents,
    noise,
    patch_weight,
    time_embedding,
    norm_gain,
    vhw,
    weight,
    qm,
):
    rows = query_states.shape[0] * NQ
    tokens = latents.shape[0]
    vmem, smem = pl.BlockSpec(memory_space=pltpu.VMEM), pl.BlockSpec(memory_space=pltpu.SMEM)
    anywhere = pl.BlockSpec(memory_space=pl.ANY)
    return pl.pallas_call(
        project_kernel,
        out_shape=[
            jax.ShapeDtypeStruct((rows, 1024), BF16),
            jax.ShapeDtypeStruct((rows, 128), F32),
            jax.ShapeDtypeStruct((tokens, 128), F32),
            jax.ShapeDtypeStruct((tokens, W), BF16),
            jax.ShapeDtypeStruct((GRAD_ROWS, tokens), BF16),
        ],
        in_specs=[smem] * 3 + [vmem] * 13 + [anywhere] * 2,
        out_specs=[vmem] * 3 + [anywhere] * 2,
        scratch_shapes=[
            pltpu.VMEM((rows, 1024), BF16),
            pltpu.VMEM((4, 2, 2, 2, 1024, 256), BF16),
            pltpu.VMEM((16, 2, 2, 256, 256), BF16),
            pltpu.VMEM((16, 256, 256), BF16),
            pltpu.VMEM((2, 4, 256, 256), BF16),
            pltpu.VMEM((2, 4, 2, 256, 256), BF16),
            pltpu.VMEM((2, 4, 256, 256), BF16),
            pltpu.VMEM((2, 4, rows, 256), BF16),
            pltpu.VMEM((4, rows, 256), BF16),
            pltpu.VMEM(qm.shape, BF16),
            pltpu.VMEM((256, W), BF16),
            pltpu.VMEM((GRAD_ROWS, 128), BF16),
            pltpu.VMEM((GRAD_ROWS, 128), F32),
            pltpu.VMEM((TOKENS, W), BF16),
            pltpu.VMEM((GRAD_ROWS, TOKENS), BF16),
            pltpu.SemaphoreType.DMA((2,)),
            pltpu.SemaphoreType.DMA((1,)),
            pltpu.SemaphoreType.DMA((4, 2)),
            pltpu.SemaphoreType.DMA((32,)),
            pltpu.SemaphoreType.DMA((4, 2, 2, 2)),
            pltpu.SemaphoreType.DMA((16, 4)),
            pltpu.SemaphoreType.DMA((16, 4)),
            pltpu.SemaphoreType.DMA((4,)),
            pltpu.SemaphoreType.DMA((4,)),
        ],
        compiler_params=pltpu.CompilerParams(
            collective_id=2, has_side_effects=True, vmem_limit_bytes=62 << 20
        ),
        name="attend_project",
    )(
        owner,
        lengths,
        timesteps,
        query_states,
        prompt_keys,
        prompt_values,
        query_keys,
        query_values,
        residual,
        gain.reshape(1, -1),
        latents,
        noise,
        patch_weight,
        time_embedding.reshape(1, -1),
        norm_gain.reshape(1, -1),
        vhw,
        weight,
        qm,
    )


COLUMNS = 256
CHUNKS = 2 * W // COLUMNS


def connect_kernel(
    scaled_ref,
    sq_ref,
    conn_hbm,
    cond_ref,
    conn,
    buf,
    land1,
    land2,
    land3,
    sqb,
    sq1,
    sq2,
    sq3,
    load_sem,
    send_sem,
    recv_sem,
):
    x, y, z, core = places()
    y_hi = y // 2
    at_ze, at_zo = device_at(x, y, z + 1 - 2 * (z % 2), core), device_at(x, y, 3 - z, core)
    at_far = device_at(x, (y + 2) % 4, z, core)
    bit_a, bit_b = gray_bits(z)
    loads = [
        pltpu.make_async_copy(
            conn_hbm.at[:, part * 512 : (part + 1) * 512], conn.at[:, part * 512 : (part + 1) * 512], load_sem.at[part]
        )
        for part in range(7)
    ]
    for copy in loads:
        copy.start()

    greet((at_ze, at_zo, at_far))

    sent = []
    flying = {}

    def send(j, phase):
        if j == CHUNKS:
            block, landing = sqb, (sq1, sq2, sq3)[phase]
        else:
            block, landing = buf.at[j], (land1, land2, land3)[phase].at[j]
        if phase == 0:
            source = block.at[:, 1 - bit_a] if j % 2 == 0 else block.at[:, :, 1 - bit_b]
        elif phase == 1:
            source = block.at[:, bit_a, 1 - bit_b] if j % 2 == 0 else block.at[:, 1 - bit_a, bit_b]
        else:
            source = block.at[1 - y_hi, bit_a, bit_b]
        copy = pltpu.make_async_remote_copy(
            src_ref=source,
            dst_ref=landing,
            send_sem=send_sem.at[j, phase],
            recv_sem=recv_sem.at[j, phase],
            device_id=at_far if phase == 2 else at_ze if phase == j % 2 else at_zo,
            device_id_type=MESH,
        )
        copy.start()
        sent.append(copy)
        flying[j] = copy

    def settle(j, phase):
        flying[j].wait_recv()
        if phase == 0:
            index = (slice(None), bit_a) if j % 2 == 0 else (slice(None), slice(None), bit_b)
        else:
            index = (slice(None), bit_a, bit_b)
        if j == CHUNKS:
            sqb[index] = sqb[index] + (sq1, sq2)[phase][...]
        else:
            index = (j,) + index
            total = buf[index].astype(F32) + (land1, land2)[phase][j].astype(F32)
            buf[index] = total.astype(BF16)
        send(j, phase + 1)

    def spread(block, value):
        for m in range(8):
            a, b = gray_bits(m % 4)
            block[m // 4, a, b] = value[m * NQ : (m + 1) * NQ]

    chunks = [CHUNKS] + list(range(CHUNKS))
    for n in range(CHUNKS + 1 + 10):
        if n == 0:
            spread(sqb, sq_ref[...])
            send(CHUNKS, 0)
        elif n <= CHUNKS:
            j = chunks[n]
            if j % 2 == 0:
                loads[j // 2].wait()
            value = nn_dot(scaled_ref[...], conn[:, j * COLUMNS : (j + 1) * COLUMNS])
            spread(buf.at[j], value.astype(BF16))
            send(j, 0)
        if 0 <= n - 6 <= CHUNKS:
            settle(chunks[n - 6], 0)
        if 0 <= n - 10 <= CHUNKS:
            settle(chunks[n - 10], 1)
    flying[CHUNKS].wait_recv()
    squares = sqb[y_hi, bit_a, bit_b] + sq3[...]
    factor = lax.rsqrt(jnp.sum(squares, -1, keepdims=True) / D + eps)
    for j in range(CHUNKS):
        flying[j].wait_recv()
        total = buf[j, y_hi, bit_a, bit_b].astype(F32) + land3[j].astype(F32)
        cond_ref[:, j * COLUMNS : (j + 1) * COLUMNS] = (total * factor).astype(BF16)
    for copy in sent:
        copy.wait_send()


def connected(scaled, squares, conn_weight):
    vmem = pl.BlockSpec(memory_space=pltpu.VMEM)
    return pl.pallas_call(
        connect_kernel,
        out_shape=jax.ShapeDtypeStruct((NQ, 2 * W), BF16),
        in_specs=[vmem, vmem, pl.BlockSpec(memory_space=pl.ANY)],
        out_specs=vmem,
        scratch_shapes=[
            pltpu.VMEM(conn_weight.shape, BF16),
            pltpu.VMEM((CHUNKS, 2, 2, 2, NQ, COLUMNS), BF16),
            pltpu.VMEM((CHUNKS, 2, 2, NQ, COLUMNS), BF16),
            pltpu.VMEM((CHUNKS, 2, NQ, COLUMNS), BF16),
            pltpu.VMEM((CHUNKS, NQ, COLUMNS), BF16),
            pltpu.VMEM((2, 2, 2, NQ, 128), F32),
            pltpu.VMEM((2, 2, NQ, 128), F32),
            pltpu.VMEM((2, NQ, 128), F32),
            pltpu.VMEM((NQ, 128), F32),
            pltpu.SemaphoreType.DMA((7,)),
            pltpu.SemaphoreType.DMA((CHUNKS + 1, 3)),
            pltpu.SemaphoreType.DMA((CHUNKS + 1, 3)),
        ],
        compiler_params=pltpu.CompilerParams(
            collective_id=3, has_side_effects=True, vmem_limit_bytes=58 << 20
        ),
        name="connect",
    )(scaled, squares, conn_weight)


def on_device(
    prompt_keys,
    prompt_values,
    query_states,
    query_keys,
    query_values,
    lengths,
    residual,
    out_weight,
    final_gain,
    conn_weight,
    owner,
    latents,
    noise,
    timesteps,
    patch_weight,
    time_embedding,
    image_norm_gain,
    query_matrix,
    velocity_head_weight,
):
    count_of_rows = lax.axis_size("dp") * lax.axis_size("tensor") * latents.shape[1]
    scaled, squares, hv, q, normed_t = projected(
        owner,
        lengths,
        timesteps,
        query_states,
        prompt_keys,
        prompt_values,
        query_keys,
        query_values,
        residual,
        final_gain,
        latents[0],
        noise[0],
        patch_weight,
        time_embedding,
        image_norm_gain,
        velocity_head_weight,
        out_weight,
        query_matrix,
    )
    cond = connected(scaled, squares, conn_weight)
    velocity, dq = step(
        q, hv, latents[0], noise[0], cond, velocity_head_weight, grad_gain / math.sqrt(count_of_rows)
    )
    return (velocity[None], summed_gradient(normed_t, dq))


def solution(mesh):
    return jax.shard_map(
        on_device,
        mesh=mesh,
        in_specs=(
            P("dp", None, "tensor"),
            P("dp", None, "tensor"),
            P("dp", None, "tensor"),
            P("dp", None, "tensor"),
            P("dp", None, "tensor"),
            P("dp"),
            P("dp", None, "tensor"),
            P("tensor", "dp"),
            P("tensor"),
            P("tensor", None),
            P("dp", None),
            P(("dp", "tensor"), None, None),
            P(("dp", "tensor"), None, None),
            P(("dp", "tensor")),
            P(),
            P(),
            P(),
            P(),
            P(),
        ),
        out_specs=(P(("dp", "tensor"), None, None), P(("dp", "tensor"), None)),
        check_vma=False,
    )
```

```python
import math

import jax
import jax.numpy as jnp
from jax import lax
from jax.experimental import pallas as pl
from jax.experimental.pallas import tpu as pltpu
from jax.sharding import PartitionSpec as P

D = 8192
HEAD = 128
NQ = 64
DHEAD = 112
NT = 1000
W = 1792
IMG_HEADS = 16
F32 = jnp.float32
BF16 = jnp.bfloat16
MESH = pl.DeviceIdType.MESH

eps = 1e-06
grad_gain = 16.0

ROWS_BLOCK = 14
ROWS_PAD = 16
PIECES = (384, 384, 256, 256, 256, 256)
STARTS = (0, 384, 768, 1024, 1280, 1536)
KEY_WINDOWS = (0, 384, 896, 1280)
SCORE_WINDOWS = (0, 128, 256, 384, 512, 640, 768)


def nt_dot(a, b):
    return lax.dot_general(a, b, (((1,), (1,)), ((), ())), preferred_element_type=F32)


def nn_dot(a, b):
    return jnp.dot(a, b, preferred_element_type=F32)


def head_mask(rows, width, head, base):
    lane = lax.broadcasted_iota(jnp.int32, (rows, width), 1) + base
    return (lane >= head * DHEAD) & (lane < (head + 1) * DHEAD)


def only_head(block, head, base):
    return jnp.where(head_mask(*block.shape, head, base), block.astype(F32), 0.0).astype(BF16)


def step_kernel(
    gain, q_ref, hv_ref, lat_ref, noise_ref, cond_ref, vhw_ref, vel_ref, dq_ref, kbd, kflat, vw, ones, probs, dsc
):
    scale = 1.0 / DHEAD**0.5
    keys = cond_ref.shape[0]

    @pl.when(pl.program_id(0) == 0)
    def _():
        for g, base in enumerate(KEY_WINDOWS):
            vals = []
            for n in range(4):
                window = cond_ref[:, base : base + 512]
                kbd[g, n * keys : (n + 1) * keys, :] = only_head(window, 4 * g + n, base)
                window = cond_ref[:, W + base : W + base + 512]
                vals.append(only_head(window, 4 * g + n, base))
            vw[g] = nn_dot(jnp.concatenate(vals, 0), vhw_ref[base : base + 512, :]).astype(BF16)
        for tile, first in enumerate(SCORE_WINDOWS):
            for n in range(4):
                window = cond_ref[:, tile * 256 : (tile + 1) * 256]
                kflat[tile, n * keys : (n + 1) * keys, :] = only_head(window, first // keys + n, tile * 256)
        row = lax.broadcasted_iota(jnp.int32, (256, 256), 0) // keys
        column = lax.broadcasted_iota(jnp.int32, (256, 256), 1) // keys
        ones[...] = jnp.where(row == column, 1.0, 0.0).astype(BF16)

    velocity = hv_ref[...]
    for g, base in enumerate(KEY_WINDOWS):
        expo = jnp.exp(nt_dot(q_ref[:, base : base + 512], kbd[g]) * scale)
        total = nn_dot(jnp.minimum(expo, 3.38e38).astype(BF16), ones[...])
        p = expo / total
        probs[:, g * 256 : (g + 1) * 256] = p
        velocity = velocity + nn_dot(p.astype(BF16), vw[g])
    vel_ref[...] = velocity
    target = noise_ref[...].astype(F32) - lat_ref[...].astype(F32)
    dvel = ((velocity - target) * gain).astype(BF16)
    for g in range(4):
        p = probs[:, g * 256 : (g + 1) * 256]
        dprob = nt_dot(dvel, vw[g])
        both = p * dprob
        high = both.astype(BF16)
        low = (both - high.astype(F32)).astype(BF16)
        shift = nn_dot(high, ones[...]) + nn_dot(low, ones[...])
        dsc[:, g * 256 : (g + 1) * 256] = (p * (dprob - shift) * scale).astype(BF16)
    for tile, first in enumerate(SCORE_WINDOWS):
        dq_ref[:, tile * 256 : (tile + 1) * 256] = nn_dot(dsc[:, first : first + 256], kflat[tile]).astype(BF16)


def step(q, hv, latents, noise, cond, vhw, gain):
    tokens = q.shape[0]
    block = 256
    keys = cond.shape[0]
    whole = lambda a: pl.BlockSpec(a.shape, lambda i: (0,) * a.ndim)
    rows = lambda width: pl.BlockSpec((block, width), lambda i: (i, 0))
    return pl.pallas_call(
        lambda *refs: step_kernel(gain, *refs),
        grid=(tokens // block,),
        in_specs=[rows(W), rows(128), rows(128), rows(128), whole(cond), whole(vhw)],
        out_specs=[rows(128), rows(W)],
        out_shape=[jax.ShapeDtypeStruct((tokens, 128), F32), jax.ShapeDtypeStruct((tokens, W), BF16)],
        scratch_shapes=[
            pltpu.VMEM((4, 4 * keys, 512), BF16),
            pltpu.VMEM((7, 4 * keys, 256), BF16),
            pltpu.VMEM((4, 4 * keys, 128), BF16),
            pltpu.VMEM((256, 256), BF16),
            pltpu.VMEM((block, 1024), F32),
            pltpu.VMEM((block, 1024), BF16),
        ],
        compiler_params=pltpu.CompilerParams(vmem_limit_bytes=48 << 20),
        cost_estimate=pl.CostEstimate(flops=6 * 10**9, bytes_accessed=10 * 10**6, transcendentals=10**6),
        name="flow_step",
    )(q, hv, latents, noise, cond, vhw)


def places():
    dp, tensor = lax.axis_index("dp"), lax.axis_index("tensor")
    return dp // 4, (tensor // 4) * 2 + (dp // 2) % 2, tensor % 4, dp % 2


def device_at(x, y, z, core):
    return (x * 4 + (y % 2) * 2 + core, (y // 2) * 4 + z)


def link_partners(x, y, z, core):
    pair = lambda i: i + 1 - 2 * (i % 2)
    other = lambda i: 3 - i
    return (
        device_at(pair(x), y, z, core),
        device_at(other(x), y, z, core),
        device_at(x, pair(y), z, core),
        device_at(x, other(y), z, core),
        device_at(x, y, pair(z), core),
        device_at(x, y, other(z), core),
    )


def gray_bits(i):
    return (i + i // 2) % 2, i // 2


def grad_kernel(nt_ref, dq_ref, out_ref, *scratch):
    mine, away, sibling_part = scratch[0:6], scratch[6:12], scratch[12:18]
    landing = [scratch[18 + 6 * p : 24 + 6 * p] for p in range(6)]
    core_send, core_recv, send_sem, recv_sem = scratch[54:58]
    x, y, z, core = places()
    partners = link_partners(x, y, z, core)
    sibling = device_at(x, y, z, 1 - core)
    bits = gray_bits(x) + gray_bits(y) + gray_bits(z)

    barrier = pltpu.get_barrier_semaphore()
    for device in partners + (sibling,):
        pl.semaphore_signal(barrier, inc=1, device_id=device, device_id_type=MESH)
    pl.semaphore_wait(barrier, 7)

    def product(p, which, target):
        columns = pl.ds(STARTS[p], PIECES[p])

        def part(i, carry):
            rows = nt_ref[which, pl.ds(pl.multiple_of(i * 512, 512), 512), :]
            value = nn_dot(rows, dq_ref[:, columns]).astype(BF16)
            target[i] = value.reshape(2, 2, 2, 2, 2, ROWS_PAD, PIECES[p])
            return carry

        lax.fori_loop(0, 2, part, 0)

    def region(p, k, bit):
        index = []
        for dim in range(6):
            age = (dim - p) % 6
            index.append(bits[dim] if age < k else bit if age == k else slice(None))
        return tuple(index)

    def to_sibling(p):
        return pltpu.make_async_remote_copy(
            src_ref=away[p],
            dst_ref=sibling_part[p],
            send_sem=core_send.at[p],
            recv_sem=core_recv.at[p],
            device_id=sibling,
            device_id_type=MESH,
        )

    def exchange(p, k):
        dim = (p + k) % 6
        return pltpu.make_async_remote_copy(
            src_ref=mine[p].at[region(p, k, 1 - bits[dim])],
            dst_ref=landing[p][k],
            send_sem=send_sem.at[p, k],
            recv_sem=recv_sem.at[p, k],
            device_id=partners[dim],
            device_id_type=MESH,
        )

    sent = []
    flying = {}

    def send(p, copy):
        copy.start()
        flying[p] = copy
        sent.append(copy)

    def settle(p, k):
        flying[p].wait_recv()
        if k == 0:
            index = (slice(None),) * 6
            arrived = sibling_part[p]
        else:
            index = region(p, k - 1, bits[(p + k - 1) % 6])
            arrived = landing[p][k - 1]
        total = mine[p][index].astype(F32) + arrived[...].astype(F32)
        if k == 6:
            out_ref[:, STARTS[p] : STARTS[p] + PIECES[p]] = total
        else:
            mine[p][index] = total.astype(BF16)
            send(p, exchange(p, k))

    for p in range(7):
        if p < 6:
            product(p, 1 - core, away[p])
            send(p, to_sibling(p))
            product(p, core, mine[p])
        if p > 0:
            settle(p - 1, 0)
    for k in range(1, 7):
        for p in range(6):
            settle(p, k)
    for copy in sent:
        copy.wait_send()


def summed_gradient(normed_t, dq):
    tokens = dq.shape[0]
    full = [pltpu.VMEM((2,) * 6 + (ROWS_PAD, c), BF16) for c in PIECES]
    parts = [pltpu.VMEM((2,) * (5 - k) + (ROWS_PAD, c), BF16) for c in PIECES for k in range(6)]
    out = pl.pallas_call(
        grad_kernel,
        out_shape=jax.ShapeDtypeStruct((ROWS_PAD, W), F32),
        in_specs=[pl.BlockSpec(memory_space=pltpu.VMEM)] * 2,
        out_specs=pl.BlockSpec(memory_space=pltpu.VMEM),
        scratch_shapes=full
        + full
        + full
        + parts
        + [
            pltpu.SemaphoreType.DMA((6,)),
            pltpu.SemaphoreType.DMA((6,)),
            pltpu.SemaphoreType.DMA((6, 6)),
            pltpu.SemaphoreType.DMA((6, 6)),
        ],
        compiler_params=pltpu.CompilerParams(
            collective_id=1, has_side_effects=True, vmem_limit_bytes=48 << 20
        ),
        name="grad_sum",
    )(normed_t.reshape(2, -1, tokens), dq)
    return out[:ROWS_BLOCK]


def attend(m, owner_ref, len_ref, q_ref, pk_ref, pv_ref, ok_ref, ov_ref, att):
    prompt = owner_ref[0, m]
    length = len_ref[prompt]
    scale = 1.0 / HEAD**0.5
    own_k, own_v = ok_ref[prompt], ov_ref[prompt]
    keys, values = pk_ref[prompt], pv_ref[prompt]
    states = q_ref[prompt]
    heads = states.shape[1] // HEAD
    rows = jnp.concatenate([states[:, j * HEAD : (j + 1) * HEAD] for j in range(heads)], 0)
    first = nt_dot(rows, keys) * scale
    second = nt_dot(rows, own_k) * scale
    column = lax.broadcasted_iota(jnp.int32, first.shape, 1)
    first = jnp.where(column < length, first, -jnp.inf)
    row = lax.broadcasted_iota(jnp.int32, second.shape, 0) % NQ
    column = lax.broadcasted_iota(jnp.int32, second.shape, 1)
    second = jnp.where(column <= row, second, -jnp.inf)
    top = jnp.maximum(jnp.max(first, -1, keepdims=True), jnp.max(second, -1, keepdims=True))
    first, second = jnp.exp(first - top), jnp.exp(second - top)
    total = jnp.sum(first, -1, keepdims=True) + jnp.sum(second, -1, keepdims=True)
    out = nn_dot(first.astype(BF16), values) + nn_dot(second.astype(BF16), own_v)
    out = (out / total).astype(BF16)
    rows_at = pl.ds(pl.multiple_of(m * NQ, NQ), NQ)
    for j in range(heads):
        att[rows_at, j * HEAD : (j + 1) * HEAD] = out[j * NQ : (j + 1) * NQ]


def greet(devices):
    barrier = pltpu.get_barrier_semaphore()
    for device in devices:
        pl.semaphore_signal(barrier, inc=1, device_id=device, device_id_type=MESH)
    pl.semaphore_wait(barrier, len(devices))


TOKENS = 256
GRAD_ROWS = 2048


def one_hot_rows(start, rows):
    row = lax.broadcasted_iota(jnp.int32, (rows, 1), 0) + start
    bit = lambda n: row // (ROWS_PAD << n) % 2
    at = lambda n: 2 * bit(n) + (bit(n) + bit(n + 1)) % 2
    z, y, x, core = at(0), at(2), at(4), bit(6)
    natural = ((x * 2 + y % 2) * 2 + core) * 8 + y // 2 * 4 + z
    inside = row % ROWS_PAD
    source = jnp.where(inside < ROWS_BLOCK, natural * ROWS_BLOCK + inside, -1)
    lane = lax.broadcasted_iota(jnp.int32, (rows, W), 1)
    return jnp.where(lane == source, 1.0, 0.0).astype(BF16)


def split_in_three(value):
    parts = []
    for _ in range(3):
        part = value.astype(BF16)
        parts.append(part)
        value = value - part.astype(F32)
    return parts


def project_kernel(
    owner_ref,
    len_ref,
    step_ref,
    q_ref,
    pk_ref,
    pv_ref,
    ok_ref,
    ov_ref,
    res_ref,
    gain_ref,
    lat_ref,
    noise_ref,
    pw_ref,
    time_ref,
    norm_ref,
    vhw_ref,
    w_hbm,
    qm_hbm,
    scaled_ref,
    sq_ref,
    hv_ref,
    q_hbm,
    nt_hbm,
    att,
    wg,
    terms,
    land_first,
    land_second,
    zsum,
    landy,
    qm,
    packed,
    pwt,
    col,
    q_out,
    nt_out,
    own_sem,
    qm_sem,
    out_sem,
    w_send,
    w_recv,
    r_send,
    r_recv,
    y_send,
    y_recv,
):
    x, y, z, core = places()
    y_lo, y_hi = y % 2, y // 2
    xp, xo, xf = x + 1 - 2 * (x % 2), 3 - x, (x + 2) % 4
    at_y = device_at(x, y + 1 - 2 * y_lo, z, core)
    at_xp, at_xo = device_at(xp, y, z, core), device_at(xo, y, z, core)
    at_ze, at_zo = device_at(x, y, z + 1 - 2 * (z % 2), core), device_at(x, y, 3 - z, core)
    at_far = device_at(x, (y + 2) % 4, z, core)
    at_sib = device_at(x, y, z, 1 - core)
    bit_b = z // 2
    shared = []

    keep = [
        pltpu.make_async_copy(w_hbm.at[:, h * 256 : (h + 1) * 256], wg.at[x, y_lo, core, h], own_sem.at[h])
        for h in range(2)
    ]
    load_qm = pltpu.make_async_copy(qm_hbm, qm, qm_sem.at[0])
    for copy in keep + [load_qm]:
        copy.start()
    greet((at_y, at_xp, at_xo, at_ze, at_zo, at_far, at_sib))

    def share(xs, ys, h, *targets):
        slot = wg.at[xs, ys, core, h]
        for target in targets:
            copy = pltpu.make_async_remote_copy(
                src_ref=slot,
                dst_ref=slot,
                send_sem=w_send.at[len(shared)],
                recv_sem=w_recv.at[xs, ys, core, h],
                device_id=target,
                device_id_type=MESH,
            )
            copy.start()
            shared.append(copy)

    def arrived(xs, ys, cs, h):
        slot = wg.at[xs, ys, cs, h]
        pltpu.make_async_remote_copy(
            src_ref=slot,
            dst_ref=slot,
            send_sem=w_send.at[0],
            recv_sem=w_recv.at[xs, ys, cs, h],
            device_id=at_sib,
            device_id_type=MESH,
        ).wait_recv()

    def pass_on(xs, ys, h, *targets):
        arrived(xs, ys, core, h)
        share(xs, ys, h, *targets)

    def prepare():
        packed[0:128, :] = pw_ref[...]
        parts = split_in_three(time_ref[...]) + split_in_three(norm_ref[...])
        packed[128:256, :] = jnp.concatenate(parts + [jnp.zeros((122, W), BF16)], 0)

        def body(i, carry):
            rows = pl.ds(pl.multiple_of(i * 256, 256), 256)
            value = nt_dot(one_hot_rows(i * 256, 256), packed[...])
            pwt[rows, :] = value[:, :128].astype(BF16)
            col[rows, :] = value[:, 128:]
            return carry

        lax.fori_loop(0, GRAD_ROWS // 256, body, 0)

    def prelude(c):
        t = (step_ref[0].astype(F32) + 0.5) / NT
        rows = pl.ds(c * TOKENS, TOKENS)
        noisy = ((1.0 - t) * lat_ref[rows, :].astype(F32) + t * noise_ref[rows, :].astype(F32)).astype(BF16)
        hidden = nn_dot(noisy, pw_ref[...]) + t * time_ref[...]
        scale = lax.rsqrt(jnp.mean(hidden * hidden, -1, keepdims=True) + eps)
        normed = (hidden * scale * norm_ref[...]).astype(BF16)
        hv_ref[rows, :] = nn_dot(hidden.astype(BF16), vhw_ref[...])
        q_out[...] = nn_dot(normed, qm[...]).astype(BF16)
        time_col = col[:, 0:1] + col[:, 1:2] + col[:, 2:3]
        norm_col = col[:, 3:4] + col[:, 4:5] + col[:, 5:6]
        ht = nt_dot(pwt[...], noisy) + t * time_col
        scale_t = lax.rsqrt(jnp.sum(ht * ht, 0, keepdims=True) / W + eps)
        nt_out[...] = (ht * scale_t * norm_col).astype(BF16)
        copies = (
            pltpu.make_async_copy(q_out, q_hbm.at[c * TOKENS : (c + 1) * TOKENS, :], out_sem.at[c, 0]),
            pltpu.make_async_copy(nt_out, nt_hbm.at[:, c * TOKENS : (c + 1) * TOKENS], out_sem.at[c, 1]),
        )
        for copy in copies:
            copy.start()
        return copies

    def prompts(start, end):
        def body(m, carry):
            attend(m, owner_ref, len_ref, q_ref, pk_ref, pv_ref, ok_ref, ov_ref, att)
            return carry

        lax.fori_loop(start, end, body, 0)

    first_chip = (x // 2, 1 - x // 2)
    chips = ((x, xp), (xo, xf))
    subs = ((core, 0), (1 - core, 0), (core, 1), (1 - core, 1))
    mine = bit_b

    def row_of(batch):
        return y_lo if batch < 2 else 1 - y_lo

    def passing(batch):
        return batch % 2

    def at_end(batch):
        return z % 2 == row_of(batch)

    def between(batch):
        return z % 2 != row_of(batch)

    def remote(s, which, source, landing, device):
        return pltpu.make_async_remote_copy(
            src_ref=source,
            dst_ref=landing,
            send_sem=r_send.at[s, which],
            recv_sem=r_recv.at[s, which],
            device_id=device,
            device_id_type=MESH,
        )

    def out_block(s):
        return (mine + z + row_of(s // 4) + 1) % 2

    def first(s, part):
        block = out_block(s) if part == 0 else 1 - mine
        return remote(s, part, terms.at[s, part, block], land_first.at[s, part], at_ze if part == 0 else at_zo)

    def second(s, part):
        block = 1 - mine if part == 0 else mine
        landing = land_second.at[passing(s // 4), s % 4, part]
        return remote(s, 2 + part, terms.at[s, part, block], landing, at_zo if part == 0 else at_ze)

    def multiply(s):
        batch = s // 4
        cs, h = subs[s % 4]

        def body(u, carry):
            value = nn_dot(att[...], wg[2 * first_chip[passing(batch)] + u, row_of(batch), cs, h]).astype(BF16)
            terms[s, 0, u] = value[:256]
            terms[s, 1, u] = value[256:]
            return carry

        lax.fori_loop(0, 2, body, 0)
        for part in range(2):
            first(s, part).start()

    def halve(s):
        for part in range(2):
            first(s, part).wait_recv()
            block = 1 - out_block(s) if part == 0 else mine
            total = terms[s, part, block].astype(F32) + land_first[s, part].astype(F32)
            terms[s, part, block] = total.astype(BF16)

        @pl.when(between(s // 4))
        def _():
            for part in range(2):
                second(s, part).start()

    def finish(s):
        batch = s // 4

        @pl.when(at_end(batch))
        def _():
            for part in range(2):
                second(s, part).wait_recv()
                landing = land_second[passing(batch), s % 4, part]
                total = terms[s, part, mine].astype(F32) + landing.astype(F32)
                zsum[passing(batch), s % 4, part * 256 : (part + 1) * 256] = total.astype(BF16)

    def across(p, i):
        return pltpu.make_async_remote_copy(
            src_ref=zsum.at[p, i],
            dst_ref=landy.at[i],
            send_sem=y_send.at[i],
            recv_sem=y_recv.at[i],
            device_id=at_far,
            device_id_type=MESH,
        )

    def cross(p, i):
        @pl.when((y_hi != x // 2) if p == 0 else (y_hi == x // 2))
        def _():
            across(p, i).start()

    def close(i):
        across(0, i).wait_recv()
        kept = (x // 2 + y_hi) % 2
        cs, h = subs[i]
        columns = pl.ds(pl.multiple_of(cs * 512 + h * 256, 256), 256)
        gain = gain_ref[:, columns]

        def body(m, carry):
            rows = pl.ds(pl.multiple_of(m * NQ, NQ), NQ)
            value = res_ref[owner_ref[0, m], :, columns].astype(F32)
            value = value + (zsum[kept, i, rows, :].astype(F32) + landy[i, rows, :].astype(F32))
            scaled_ref[rows, columns] = (value * gain).astype(BF16)
            square = value * value
            square = square[:, :128] + square[:, 128:]
            sq_ref[rows, :] = square if i == 0 else sq_ref[rows, :] + square
            return carry

        lax.fori_loop(0, 8, body, 0)

    def steps(batch, h):
        for s in (4 * batch + 2 * h, 4 * batch + 2 * h + 1):
            if s % 2 == 1:
                for xs in chips[passing(batch)]:
                    arrived(xs, row_of(batch), 1 - core, h)
            multiply(s)
            done.append(s)
            if len(done) > 4:
                halve(done[-5])
            if len(done) > 8:
                settle(done[-9])

    done = []

    def settle(s):
        finish(s)
        if 8 <= s < 12:
            cross(0, s - 8)
        if s >= 12:
            cross(1, s - 12)

    for h in range(2):
        keep[h].wait()
        share(x, y_lo, h, at_xp, at_xo, at_y, at_sib)
    prompts(0, 8)
    pass_on(xo, y_lo, 0, at_xp, at_sib)
    pass_on(xp, y_lo, 0, at_sib)
    steps(0, 0)
    pass_on(x, 1 - y_lo, 0, at_xp, at_xo, at_sib)
    pass_on(xp, y_lo, 1, at_xo, at_sib)
    pass_on(xo, y_lo, 1, at_sib)
    steps(0, 1)
    pass_on(x, 1 - y_lo, 1, at_xp, at_xo, at_sib)
    prepare()
    load_qm.wait()
    stores = prelude(0)
    pass_on(xf, y_lo, 0, at_y, at_sib)
    pass_on(xf, y_lo, 1, at_y, at_sib)
    pass_on(xp, 1 - y_lo, 0, at_sib)
    steps(2, 0)
    for copy in stores:
        copy.wait()
    stores = prelude(1)
    pass_on(xp, 1 - y_lo, 1, at_sib)
    steps(2, 1)
    steps(1, 0)
    for copy in stores:
        copy.wait()
    stores = prelude(2)
    pass_on(xo, 1 - y_lo, 0, at_sib)
    pass_on(xf, 1 - y_lo, 0, at_sib)
    steps(1, 1)
    for copy in stores:
        copy.wait()
    stores = prelude(3)
    steps(3, 0)
    pass_on(xo, 1 - y_lo, 1, at_sib)
    pass_on(xf, 1 - y_lo, 1, at_sib)
    steps(3, 1)
    for i in range(4):
        settle(4 + i)
        halve(12 + i)
    for i in range(4):
        settle(12 + i)
        if i > 0:
            close(i - 1)
    close(3)
    for copy in stores:
        copy.wait()
    for copy in shared:
        copy.wait_send()
    for s in range(16):
        for part in range(2):
            first(s, part).wait_send()

        @pl.when(between(s // 4))
        def _():
            for part in range(2):
                second(s, part).wait_send()

    for i in range(4):
        across(0, i).wait_send()


def projected(
    owner,
    lengths,
    timesteps,
    query_states,
    prompt_keys,
    prompt_values,
    query_keys,
    query_values,
    residual,
    gain,
    latents,
    noise,
    patch_weight,
    time_embedding,
    norm_gain,
    vhw,
    weight,
    qm,
):
    rows = query_states.shape[0] * NQ
    tokens = latents.shape[0]
    vmem, smem = pl.BlockSpec(memory_space=pltpu.VMEM), pl.BlockSpec(memory_space=pltpu.SMEM)
    anywhere = pl.BlockSpec(memory_space=pl.ANY)
    return pl.pallas_call(
        project_kernel,
        out_shape=[
            jax.ShapeDtypeStruct((rows, 1024), BF16),
            jax.ShapeDtypeStruct((rows, 128), F32),
            jax.ShapeDtypeStruct((tokens, 128), F32),
            jax.ShapeDtypeStruct((tokens, W), BF16),
            jax.ShapeDtypeStruct((GRAD_ROWS, tokens), BF16),
        ],
        in_specs=[smem] * 3 + [vmem] * 13 + [anywhere] * 2,
        out_specs=[vmem] * 3 + [anywhere] * 2,
        scratch_shapes=[
            pltpu.VMEM((rows, 1024), BF16),
            pltpu.VMEM((4, 2, 2, 2, 1024, 256), BF16),
            pltpu.VMEM((16, 2, 2, 256, 256), BF16),
            pltpu.VMEM((16, 2, 256, 256), BF16),
            pltpu.VMEM((2, 4, 2, 256, 256), BF16),
            pltpu.VMEM((2, 4, rows, 256), BF16),
            pltpu.VMEM((4, rows, 256), BF16),
            pltpu.VMEM(qm.shape, BF16),
            pltpu.VMEM((256, W), BF16),
            pltpu.VMEM((GRAD_ROWS, 128), BF16),
            pltpu.VMEM((GRAD_ROWS, 128), F32),
            pltpu.VMEM((TOKENS, W), BF16),
            pltpu.VMEM((GRAD_ROWS, TOKENS), BF16),
            pltpu.SemaphoreType.DMA((2,)),
            pltpu.SemaphoreType.DMA((1,)),
            pltpu.SemaphoreType.DMA((4, 2)),
            pltpu.SemaphoreType.DMA((32,)),
            pltpu.SemaphoreType.DMA((4, 2, 2, 2)),
            pltpu.SemaphoreType.DMA((16, 4)),
            pltpu.SemaphoreType.DMA((16, 4)),
            pltpu.SemaphoreType.DMA((4,)),
            pltpu.SemaphoreType.DMA((4,)),
        ],
        compiler_params=pltpu.CompilerParams(
            collective_id=2, has_side_effects=True, vmem_limit_bytes=62 << 20
        ),
        name="attend_project",
    )(
        owner,
        lengths,
        timesteps,
        query_states,
        prompt_keys,
        prompt_values,
        query_keys,
        query_values,
        residual,
        gain.reshape(1, -1),
        latents,
        noise,
        patch_weight,
        time_embedding.reshape(1, -1),
        norm_gain.reshape(1, -1),
        vhw,
        weight,
        qm,
    )


COLUMNS = 256
CHUNKS = 2 * W // COLUMNS


def connect_kernel(
    scaled_ref,
    sq_ref,
    conn_hbm,
    cond_ref,
    conn,
    buf,
    land1,
    land2,
    land3,
    sqb,
    sq1,
    sq2,
    sq3,
    load_sem,
    send_sem,
    recv_sem,
):
    x, y, z, core = places()
    y_hi = y // 2
    at_ze, at_zo = device_at(x, y, z + 1 - 2 * (z % 2), core), device_at(x, y, 3 - z, core)
    at_far = device_at(x, (y + 2) % 4, z, core)
    bit_a, bit_b = gray_bits(z)
    loads = [
        pltpu.make_async_copy(
            conn_hbm.at[:, part * 512 : (part + 1) * 512], conn.at[:, part * 512 : (part + 1) * 512], load_sem.at[part]
        )
        for part in range(7)
    ]
    for copy in loads:
        copy.start()

    greet((at_ze, at_zo, at_far))

    sent = []
    flying = {}

    def send(j, phase):
        if j == CHUNKS:
            block, landing = sqb, (sq1, sq2, sq3)[phase]
        else:
            block, landing = buf.at[j], (land1, land2, land3)[phase].at[j]
        if phase == 0:
            source = block.at[:, 1 - bit_a] if j % 2 == 0 else block.at[:, :, 1 - bit_b]
        elif phase == 1:
            source = block.at[:, bit_a, 1 - bit_b] if j % 2 == 0 else block.at[:, 1 - bit_a, bit_b]
        else:
            source = block.at[1 - y_hi, bit_a, bit_b]
        copy = pltpu.make_async_remote_copy(
            src_ref=source,
            dst_ref=landing,
            send_sem=send_sem.at[j, phase],
            recv_sem=recv_sem.at[j, phase],
            device_id=at_far if phase == 2 else at_ze if phase == j % 2 else at_zo,
            device_id_type=MESH,
        )
        copy.start()
        sent.append(copy)
        flying[j] = copy

    def settle(j, phase):
        flying[j].wait_recv()
        if phase == 0:
            index = (slice(None), bit_a) if j % 2 == 0 else (slice(None), slice(None), bit_b)
        else:
            index = (slice(None), bit_a, bit_b)
        if j == CHUNKS:
            sqb[index] = sqb[index] + (sq1, sq2)[phase][...]
        else:
            index = (j,) + index
            total = buf[index].astype(F32) + (land1, land2)[phase][j].astype(F32)
            buf[index] = total.astype(BF16)
        send(j, phase + 1)

    def spread(block, value):
        for m in range(8):
            a, b = gray_bits(m % 4)
            block[m // 4, a, b] = value[m * NQ : (m + 1) * NQ]

    chunks = [CHUNKS] + list(range(CHUNKS))
    for n in range(CHUNKS + 1 + 10):
        if n == 0:
            spread(sqb, sq_ref[...])
            send(CHUNKS, 0)
        elif n <= CHUNKS:
            j = chunks[n]
            if j % 2 == 0:
                loads[j // 2].wait()
            value = nn_dot(scaled_ref[...], conn[:, j * COLUMNS : (j + 1) * COLUMNS])
            spread(buf.at[j], value.astype(BF16))
            send(j, 0)
        if 0 <= n - 6 <= CHUNKS:
            settle(chunks[n - 6], 0)
        if 0 <= n - 10 <= CHUNKS:
            settle(chunks[n - 10], 1)
    flying[CHUNKS].wait_recv()
    squares = sqb[y_hi, bit_a, bit_b] + sq3[...]
    factor = lax.rsqrt(jnp.sum(squares, -1, keepdims=True) / D + eps)
    for j in range(CHUNKS):
        flying[j].wait_recv()
        total = buf[j, y_hi, bit_a, bit_b].astype(F32) + land3[j].astype(F32)
        cond_ref[:, j * COLUMNS : (j + 1) * COLUMNS] = (total * factor).astype(BF16)
    for copy in sent:
        copy.wait_send()


def connected(scaled, squares, conn_weight):
    vmem = pl.BlockSpec(memory_space=pltpu.VMEM)
    return pl.pallas_call(
        connect_kernel,
        out_shape=jax.ShapeDtypeStruct((NQ, 2 * W), BF16),
        in_specs=[vmem, vmem, pl.BlockSpec(memory_space=pl.ANY)],
        out_specs=vmem,
        scratch_shapes=[
            pltpu.VMEM(conn_weight.shape, BF16),
            pltpu.VMEM((CHUNKS, 2, 2, 2, NQ, COLUMNS), BF16),
            pltpu.VMEM((CHUNKS, 2, 2, NQ, COLUMNS), BF16),
            pltpu.VMEM((CHUNKS, 2, NQ, COLUMNS), BF16),
            pltpu.VMEM((CHUNKS, NQ, COLUMNS), BF16),
            pltpu.VMEM((2, 2, 2, NQ, 128), F32),
            pltpu.VMEM((2, 2, NQ, 128), F32),
            pltpu.VMEM((2, NQ, 128), F32),
            pltpu.VMEM((NQ, 128), F32),
            pltpu.SemaphoreType.DMA((7,)),
            pltpu.SemaphoreType.DMA((CHUNKS + 1, 3)),
            pltpu.SemaphoreType.DMA((CHUNKS + 1, 3)),
        ],
        compiler_params=pltpu.CompilerParams(
            collective_id=3, has_side_effects=True, vmem_limit_bytes=58 << 20
        ),
        name="connect",
    )(scaled, squares, conn_weight)


def on_device(
    prompt_keys,
    prompt_values,
    query_states,
    query_keys,
    query_values,
    lengths,
    residual,
    out_weight,
    final_gain,
    conn_weight,
    owner,
    latents,
    noise,
    timesteps,
    patch_weight,
    time_embedding,
    image_norm_gain,
    query_matrix,
    velocity_head_weight,
):
    count_of_rows = lax.axis_size("dp") * lax.axis_size("tensor") * latents.shape[1]
    scaled, squares, hv, q, normed_t = projected(
        owner,
        lengths,
        timesteps,
        query_states,
        prompt_keys,
        prompt_values,
        query_keys,
        query_values,
        residual,
        final_gain,
        latents[0],
        noise[0],
        patch_weight,
        time_embedding,
        image_norm_gain,
        velocity_head_weight,
        out_weight,
        query_matrix,
    )
    cond = connected(scaled, squares, conn_weight)
    velocity, dq = step(
        q, hv, latents[0], noise[0], cond, velocity_head_weight, grad_gain / math.sqrt(count_of_rows)
    )
    return (velocity[None], summed_gradient(normed_t, dq))


def solution(mesh):
    return jax.shard_map(
        on_device,
        mesh=mesh,
        in_specs=(
            P("dp", None, "tensor"),
            P("dp", None, "tensor"),
            P("dp", None, "tensor"),
            P("dp", None, "tensor"),
            P("dp", None, "tensor"),
            P("dp"),
            P("dp", None, "tensor"),
            P("tensor", "dp"),
            P("tensor"),
            P("tensor", None),
            P("dp", None),
            P(("dp", "tensor"), None, None),
            P(("dp", "tensor"), None, None),
            P(("dp", "tensor")),
            P(),
            P(),
            P(),
            P(),
            P(),
        ),
        out_specs=(P(("dp", "tensor"), None, None), P(("dp", "tensor"), None)),
        check_vma=False,
    )
```

```python
import math

import jax
import jax.numpy as jnp
from jax import lax
from jax.experimental import pallas as pl
from jax.experimental.pallas import tpu as pltpu
from jax.sharding import PartitionSpec as P

D = 8192
HEAD = 128
NQ = 64
DHEAD = 112
NT = 1000
W = 1792
IMG_HEADS = 16
F32 = jnp.float32
BF16 = jnp.bfloat16
MESH = pl.DeviceIdType.MESH

eps = 1e-06
grad_gain = 16.0

ROWS_BLOCK = 14
ROWS_PAD = 16
PIECES = (384, 384, 256, 256, 256, 256)
STARTS = (0, 384, 768, 1024, 1280, 1536)
KEY_WINDOWS = (0, 384, 896, 1280)
SCORE_WINDOWS = (0, 128, 256, 384, 512, 640, 768)


def nt_dot(a, b):
    return lax.dot_general(a, b, (((1,), (1,)), ((), ())), preferred_element_type=F32)


def nn_dot(a, b):
    return jnp.dot(a, b, preferred_element_type=F32)


def head_mask(rows, width, head, base):
    lane = lax.broadcasted_iota(jnp.int32, (rows, width), 1) + base
    return (lane >= head * DHEAD) & (lane < (head + 1) * DHEAD)


def only_head(block, head, base):
    return jnp.where(head_mask(*block.shape, head, base), block.astype(F32), 0.0).astype(BF16)


def step_kernel(
    gain, q_ref, hv_ref, lat_ref, noise_ref, cond_ref, vhw_ref, vel_ref, dq_ref, kbd, kflat, vw, ones, probs, dsc
):
    scale = 1.0 / DHEAD**0.5
    keys = cond_ref.shape[0]

    @pl.when(pl.program_id(0) == 0)
    def _():
        for g, base in enumerate(KEY_WINDOWS):
            vals = []
            for n in range(4):
                window = cond_ref[:, base : base + 512]
                kbd[g, n * keys : (n + 1) * keys, :] = only_head(window, 4 * g + n, base)
                window = cond_ref[:, W + base : W + base + 512]
                vals.append(only_head(window, 4 * g + n, base))
            vw[g] = nn_dot(jnp.concatenate(vals, 0), vhw_ref[base : base + 512, :]).astype(BF16)
        for tile, first in enumerate(SCORE_WINDOWS):
            for n in range(4):
                window = cond_ref[:, tile * 256 : (tile + 1) * 256]
                kflat[tile, n * keys : (n + 1) * keys, :] = only_head(window, first // keys + n, tile * 256)
        row = lax.broadcasted_iota(jnp.int32, (256, 256), 0) // keys
        column = lax.broadcasted_iota(jnp.int32, (256, 256), 1) // keys
        ones[...] = jnp.where(row == column, 1.0, 0.0).astype(BF16)

    velocity = hv_ref[...]
    for g, base in enumerate(KEY_WINDOWS):
        expo = jnp.exp(nt_dot(q_ref[:, base : base + 512], kbd[g]) * scale)
        total = nn_dot(jnp.minimum(expo, 3.38e38).astype(BF16), ones[...])
        p = expo / total
        probs[:, g * 256 : (g + 1) * 256] = p
        velocity = velocity + nn_dot(p.astype(BF16), vw[g])
    vel_ref[...] = velocity
    target = noise_ref[...].astype(F32) - lat_ref[...].astype(F32)
    dvel = ((velocity - target) * gain).astype(BF16)
    for g in range(4):
        p = probs[:, g * 256 : (g + 1) * 256]
        dprob = nt_dot(dvel, vw[g])
        both = p * dprob
        high = both.astype(BF16)
        low = (both - high.astype(F32)).astype(BF16)
        shift = nn_dot(high, ones[...]) + nn_dot(low, ones[...])
        dsc[:, g * 256 : (g + 1) * 256] = (p * (dprob - shift) * scale).astype(BF16)
    for tile, first in enumerate(SCORE_WINDOWS):
        dq_ref[:, tile * 256 : (tile + 1) * 256] = nn_dot(dsc[:, first : first + 256], kflat[tile]).astype(BF16)


def step(q, hv, latents, noise, cond, vhw, gain):
    tokens = q.shape[0]
    block = 256
    keys = cond.shape[0]
    whole = lambda a: pl.BlockSpec(a.shape, lambda i: (0,) * a.ndim)
    rows = lambda width: pl.BlockSpec((block, width), lambda i: (i, 0))
    return pl.pallas_call(
        lambda *refs: step_kernel(gain, *refs),
        grid=(tokens // block,),
        in_specs=[rows(W), rows(128), rows(128), rows(128), whole(cond), whole(vhw)],
        out_specs=[rows(128), rows(W)],
        out_shape=[jax.ShapeDtypeStruct((tokens, 128), F32), jax.ShapeDtypeStruct((tokens, W), BF16)],
        scratch_shapes=[
            pltpu.VMEM((4, 4 * keys, 512), BF16),
            pltpu.VMEM((7, 4 * keys, 256), BF16),
            pltpu.VMEM((4, 4 * keys, 128), BF16),
            pltpu.VMEM((256, 256), BF16),
            pltpu.VMEM((block, 1024), F32),
            pltpu.VMEM((block, 1024), BF16),
        ],
        compiler_params=pltpu.CompilerParams(vmem_limit_bytes=48 << 20),
        cost_estimate=pl.CostEstimate(flops=6 * 10**9, bytes_accessed=10 * 10**6, transcendentals=10**6),
        name="flow_step",
    )(q, hv, latents, noise, cond, vhw)


def places():
    dp, tensor = lax.axis_index("dp"), lax.axis_index("tensor")
    return dp // 4, (tensor // 4) * 2 + (dp // 2) % 2, tensor % 4, dp % 2


def device_at(x, y, z, core):
    return (x * 4 + (y % 2) * 2 + core, (y // 2) * 4 + z)


def link_partners(x, y, z, core):
    pair = lambda i: i + 1 - 2 * (i % 2)
    other = lambda i: 3 - i
    return (
        device_at(pair(x), y, z, core),
        device_at(other(x), y, z, core),
        device_at(x, pair(y), z, core),
        device_at(x, other(y), z, core),
        device_at(x, y, pair(z), core),
        device_at(x, y, other(z), core),
    )


def gray_bits(i):
    return (i + i // 2) % 2, i // 2


def grad_kernel(nt_ref, dq_ref, out_ref, *scratch):
    mine, away, sibling_part = scratch[0:6], scratch[6:12], scratch[12:18]
    landing = [scratch[18 + 6 * p : 24 + 6 * p] for p in range(6)]
    core_send, core_recv, send_sem, recv_sem = scratch[54:58]
    x, y, z, core = places()
    partners = link_partners(x, y, z, core)
    sibling = device_at(x, y, z, 1 - core)
    bits = gray_bits(x) + gray_bits(y) + gray_bits(z)

    barrier = pltpu.get_barrier_semaphore()
    for device in partners + (sibling,):
        pl.semaphore_signal(barrier, inc=1, device_id=device, device_id_type=MESH)
    pl.semaphore_wait(barrier, 7)

    def product(p, which, target):
        columns = pl.ds(STARTS[p], PIECES[p])

        def part(i, carry):
            rows = nt_ref[which, pl.ds(pl.multiple_of(i * 512, 512), 512), :]
            value = nn_dot(rows, dq_ref[:, columns]).astype(BF16)
            target[i] = value.reshape(2, 2, 2, 2, 2, ROWS_PAD, PIECES[p])
            return carry

        lax.fori_loop(0, 2, part, 0)

    def region(p, k, bit):
        index = []
        for dim in range(6):
            age = (dim - p) % 6
            index.append(bits[dim] if age < k else bit if age == k else slice(None))
        return tuple(index)

    def to_sibling(p):
        return pltpu.make_async_remote_copy(
            src_ref=away[p],
            dst_ref=sibling_part[p],
            send_sem=core_send.at[p],
            recv_sem=core_recv.at[p],
            device_id=sibling,
            device_id_type=MESH,
        )

    def exchange(p, k):
        dim = (p + k) % 6
        return pltpu.make_async_remote_copy(
            src_ref=mine[p].at[region(p, k, 1 - bits[dim])],
            dst_ref=landing[p][k],
            send_sem=send_sem.at[p, k],
            recv_sem=recv_sem.at[p, k],
            device_id=partners[dim],
            device_id_type=MESH,
        )

    sent = []
    flying = {}

    def send(p, copy):
        copy.start()
        flying[p] = copy
        sent.append(copy)

    def settle(p, k):
        flying[p].wait_recv()
        if k == 0:
            index = (slice(None),) * 6
            arrived = sibling_part[p]
        else:
            index = region(p, k - 1, bits[(p + k - 1) % 6])
            arrived = landing[p][k - 1]
        total = mine[p][index].astype(F32) + arrived[...].astype(F32)
        if k == 6:
            out_ref[:, STARTS[p] : STARTS[p] + PIECES[p]] = total
        else:
            mine[p][index] = total.astype(BF16)
            send(p, exchange(p, k))

    for p in range(7):
        if p < 6:
            product(p, 1 - core, away[p])
            send(p, to_sibling(p))
            product(p, core, mine[p])
        if p > 0:
            settle(p - 1, 0)
    for k in range(1, 7):
        for p in range(6):
            settle(p, k)
    for copy in sent:
        copy.wait_send()


def summed_gradient(normed_t, dq):
    tokens = dq.shape[0]
    full = [pltpu.VMEM((2,) * 6 + (ROWS_PAD, c), BF16) for c in PIECES]
    parts = [pltpu.VMEM((2,) * (5 - k) + (ROWS_PAD, c), BF16) for c in PIECES for k in range(6)]
    out = pl.pallas_call(
        grad_kernel,
        out_shape=jax.ShapeDtypeStruct((ROWS_PAD, W), F32),
        in_specs=[pl.BlockSpec(memory_space=pltpu.VMEM)] * 2,
        out_specs=pl.BlockSpec(memory_space=pltpu.VMEM),
        scratch_shapes=full
        + full
        + full
        + parts
        + [
            pltpu.SemaphoreType.DMA((6,)),
            pltpu.SemaphoreType.DMA((6,)),
            pltpu.SemaphoreType.DMA((6, 6)),
            pltpu.SemaphoreType.DMA((6, 6)),
        ],
        compiler_params=pltpu.CompilerParams(
            collective_id=1, has_side_effects=True, vmem_limit_bytes=48 << 20
        ),
        name="grad_sum",
    )(normed_t.reshape(2, -1, tokens), dq)
    return out[:ROWS_BLOCK]


def attend(m, owner_ref, len_ref, q_ref, pk_ref, pv_ref, ok_ref, ov_ref, att):
    prompt = owner_ref[0, m]
    length = len_ref[prompt]
    scale = 1.0 / HEAD**0.5
    own_k, own_v = ok_ref[prompt], ov_ref[prompt]
    keys, values = pk_ref[prompt], pv_ref[prompt]
    states = q_ref[prompt]
    heads = states.shape[1] // HEAD
    rows = jnp.concatenate([states[:, j * HEAD : (j + 1) * HEAD] for j in range(heads)], 0)
    first = nt_dot(rows, keys) * scale
    second = nt_dot(rows, own_k) * scale
    column = lax.broadcasted_iota(jnp.int32, first.shape, 1)
    first = jnp.where(column < length, first, -jnp.inf)
    row = lax.broadcasted_iota(jnp.int32, second.shape, 0) % NQ
    column = lax.broadcasted_iota(jnp.int32, second.shape, 1)
    second = jnp.where(column <= row, second, -jnp.inf)
    top = jnp.maximum(jnp.max(first, -1, keepdims=True), jnp.max(second, -1, keepdims=True))
    first, second = jnp.exp(first - top), jnp.exp(second - top)
    total = jnp.sum(first, -1, keepdims=True) + jnp.sum(second, -1, keepdims=True)
    out = nn_dot(first.astype(BF16), values) + nn_dot(second.astype(BF16), own_v)
    out = (out / total).astype(BF16)
    rows_at = pl.ds(pl.multiple_of(m * NQ, NQ), NQ)
    for j in range(heads):
        att[rows_at, j * HEAD : (j + 1) * HEAD] = out[j * NQ : (j + 1) * NQ]


def greet(devices):
    barrier = pltpu.get_barrier_semaphore()
    for device in devices:
        pl.semaphore_signal(barrier, inc=1, device_id=device, device_id_type=MESH)
    pl.semaphore_wait(barrier, len(devices))


TOKENS = 256
GRAD_ROWS = 2048


def one_hot_rows(start, rows):
    row = lax.broadcasted_iota(jnp.int32, (rows, 1), 0) + start
    bit = lambda n: row // (ROWS_PAD << n) % 2
    at = lambda n: 2 * bit(n) + (bit(n) + bit(n + 1)) % 2
    z, y, x, core = at(0), at(2), at(4), bit(6)
    natural = ((x * 2 + y % 2) * 2 + core) * 8 + y // 2 * 4 + z
    inside = row % ROWS_PAD
    source = jnp.where(inside < ROWS_BLOCK, natural * ROWS_BLOCK + inside, -1)
    lane = lax.broadcasted_iota(jnp.int32, (rows, W), 1)
    return jnp.where(lane == source, 1.0, 0.0).astype(BF16)


def split_in_three(value):
    parts = []
    for _ in range(3):
        part = value.astype(BF16)
        parts.append(part)
        value = value - part.astype(F32)
    return parts


def project_kernel(
    owner_ref,
    len_ref,
    step_ref,
    q_ref,
    pk_ref,
    pv_ref,
    ok_ref,
    ov_ref,
    res_ref,
    gain_ref,
    lat_ref,
    noise_ref,
    pw_ref,
    time_ref,
    norm_ref,
    vhw_ref,
    w_hbm,
    qm_hbm,
    scaled_ref,
    sq_ref,
    hv_ref,
    q_hbm,
    nt_hbm,
    att,
    wg,
    terms,
    land_first,
    land_second,
    zsum,
    landy,
    qm,
    packed,
    pwt,
    col,
    q_out,
    nt_out,
    own_sem,
    qm_sem,
    out_sem,
    w_send,
    w_recv,
    r_send,
    r_recv,
    y_send,
    y_recv,
):
    x, y, z, core = places()
    y_lo, y_hi = y % 2, y // 2
    xp, xo, xf = x + 1 - 2 * (x % 2), 3 - x, (x + 2) % 4
    at_y = device_at(x, y + 1 - 2 * y_lo, z, core)
    at_xp, at_xo = device_at(xp, y, z, core), device_at(xo, y, z, core)
    at_ze, at_zo = device_at(x, y, z + 1 - 2 * (z % 2), core), device_at(x, y, 3 - z, core)
    at_far = device_at(x, (y + 2) % 4, z, core)
    at_sib = device_at(x, y, z, 1 - core)
    bit_b = z // 2
    shared = []

    keep = [
        pltpu.make_async_copy(w_hbm.at[:, h * 256 : (h + 1) * 256], wg.at[x, y_lo, core, h], own_sem.at[h])
        for h in range(2)
    ]
    load_qm = pltpu.make_async_copy(qm_hbm, qm, qm_sem.at[0])
    for copy in keep + [load_qm]:
        copy.start()
    greet((at_y, at_xp, at_xo, at_ze, at_zo, at_far, at_sib))

    def share(xs, ys, h, *targets):
        slot = wg.at[xs, ys, core, h]
        for target in targets:
            copy = pltpu.make_async_remote_copy(
                src_ref=slot,
                dst_ref=slot,
                send_sem=w_send.at[len(shared)],
                recv_sem=w_recv.at[xs, ys, core, h],
                device_id=target,
                device_id_type=MESH,
            )
            copy.start()
            shared.append(copy)

    def arrived(xs, ys, cs, h):
        slot = wg.at[xs, ys, cs, h]
        pltpu.make_async_remote_copy(
            src_ref=slot,
            dst_ref=slot,
            send_sem=w_send.at[0],
            recv_sem=w_recv.at[xs, ys, cs, h],
            device_id=at_sib,
            device_id_type=MESH,
        ).wait_recv()

    def pass_on(xs, ys, h, *targets):
        arrived(xs, ys, core, h)
        share(xs, ys, h, *targets)

    def prepare():
        packed[0:128, :] = pw_ref[...]
        parts = split_in_three(time_ref[...].reshape(1, W)) + split_in_three(norm_ref[...].reshape(1, W))
        packed[128:256, :] = jnp.concatenate(parts + [jnp.zeros((122, W), BF16)], 0)

        def body(i, carry):
            rows = pl.ds(pl.multiple_of(i * 256, 256), 256)
            value = nt_dot(one_hot_rows(i * 256, 256), packed[...])
            pwt[rows, :] = value[:, :128].astype(BF16)
            col[rows, :] = value[:, 128:]
            return carry

        lax.fori_loop(0, GRAD_ROWS // 256, body, 0)

    def prelude(c):
        t = (step_ref[0].astype(F32) + 0.5) / NT
        rows = pl.ds(c * TOKENS, TOKENS)
        noisy = ((1.0 - t) * lat_ref[rows, :].astype(F32) + t * noise_ref[rows, :].astype(F32)).astype(BF16)
        hidden = nn_dot(noisy, pw_ref[...]) + t * time_ref[...].reshape(1, W)
        scale = lax.rsqrt(jnp.mean(hidden * hidden, -1, keepdims=True) + eps)
        normed = (hidden * scale * norm_ref[...].reshape(1, W)).astype(BF16)
        hv_ref[rows, :] = nn_dot(hidden.astype(BF16), vhw_ref[...])
        q_out[...] = nn_dot(normed, qm[...]).astype(BF16)
        time_col = col[:, 0:1] + col[:, 1:2] + col[:, 2:3]
        norm_col = col[:, 3:4] + col[:, 4:5] + col[:, 5:6]
        ht = nt_dot(pwt[...], noisy) + t * time_col
        scale_t = lax.rsqrt(jnp.sum(ht * ht, 0, keepdims=True) / W + eps)
        nt_out[...] = (ht * scale_t * norm_col).astype(BF16)
        copies = (
            pltpu.make_async_copy(q_out, q_hbm.at[c * TOKENS : (c + 1) * TOKENS, :], out_sem.at[c, 0]),
            pltpu.make_async_copy(nt_out, nt_hbm.at[:, c * TOKENS : (c + 1) * TOKENS], out_sem.at[c, 1]),
        )
        for copy in copies:
            copy.start()
        return copies

    def prompts(start, end):
        def body(m, carry):
            attend(m, owner_ref, len_ref, q_ref, pk_ref, pv_ref, ok_ref, ov_ref, att)
            return carry

        lax.fori_loop(start, end, body, 0)

    first_chip = (x // 2, 1 - x // 2)
    chips = ((x, xp), (xo, xf))
    subs = ((core, 0), (1 - core, 0), (core, 1), (1 - core, 1))
    mine = bit_b

    def row_of(batch):
        return y_lo if batch < 2 else 1 - y_lo

    def passing(batch):
        return batch % 2

    def at_end(batch):
        return z % 2 == row_of(batch)

    def between(batch):
        return z % 2 != row_of(batch)

    def remote(s, which, source, landing, device):
        return pltpu.make_async_remote_copy(
            src_ref=source,
            dst_ref=landing,
            send_sem=r_send.at[s, which],
            recv_sem=r_recv.at[s, which],
            device_id=device,
            device_id_type=MESH,
        )

    def out_block(s):
        return (mine + z + row_of(s // 4) + 1) % 2

    def first(s, part):
        block = out_block(s) if part == 0 else 1 - mine
        return remote(s, part, terms.at[s, part, block], land_first.at[s, part], at_ze if part == 0 else at_zo)

    def second(s, part):
        block = 1 - mine if part == 0 else mine
        landing = land_second.at[passing(s // 4), s % 4, part]
        return remote(s, 2 + part, terms.at[s, part, block], landing, at_zo if part == 0 else at_ze)

    def multiply(s):
        batch = s // 4
        cs, h = subs[s % 4]

        def body(u, carry):
            value = nn_dot(att[...], wg[2 * first_chip[passing(batch)] + u, row_of(batch), cs, h]).astype(BF16)
            terms[s, 0, u] = value[:256]
            terms[s, 1, u] = value[256:]
            return carry

        lax.fori_loop(0, 2, body, 0)
        for part in range(2):
            first(s, part).start()

    def halve(s):
        for part in range(2):
            first(s, part).wait_recv()
            block = 1 - out_block(s) if part == 0 else mine
            total = terms[s, part, block].astype(F32) + land_first[s, part].astype(F32)
            terms[s, part, block] = total.astype(BF16)

        @pl.when(between(s // 4))
        def _():
            for part in range(2):
                second(s, part).start()

    def finish(s):
        batch = s // 4

        @pl.when(at_end(batch))
        def _():
            for part in range(2):
                second(s, part).wait_recv()
                landing = land_second[passing(batch), s % 4, part]
                total = terms[s, part, mine].astype(F32) + landing.astype(F32)
                zsum[passing(batch), s % 4, part * 256 : (part + 1) * 256] = total.astype(BF16)

    def across(p, i):
        return pltpu.make_async_remote_copy(
            src_ref=zsum.at[p, i],
            dst_ref=landy.at[i],
            send_sem=y_send.at[i],
            recv_sem=y_recv.at[i],
            device_id=at_far,
            device_id_type=MESH,
        )

    def cross(p, i):
        @pl.when((y_hi != x // 2) if p == 0 else (y_hi == x // 2))
        def _():
            across(p, i).start()

    first_closed = []

    def close(i):
        first_closed.append(i)
        across(0, i).wait_recv()
        kept = (x // 2 + y_hi) % 2
        cs, h = subs[i]
        columns = pl.ds(pl.multiple_of(cs * 512 + h * 256, 256), 256)
        gain = gain_ref[:, columns]

        def body(m, carry):
            rows = pl.ds(pl.multiple_of(m * NQ, NQ), NQ)
            value = res_ref[owner_ref[0, m], :, columns].astype(F32)
            value = value + (zsum[kept, i, rows, :].astype(F32) + landy[i, rows, :].astype(F32))
            scaled_ref[rows, columns] = (value * gain).astype(BF16)
            square = value * value
            square = square[:, :128] + square[:, 128:]
            sq_ref[rows, :] = square if i == first_closed[0] else sq_ref[rows, :] + square
            return carry

        lax.fori_loop(0, 8, body, 0)

    done = []

    def steps(batch, h):
        for s in (4 * batch + 2 * h, 4 * batch + 2 * h + 1):
            if s % 2 == 1:
                for xs in chips[passing(batch)]:
                    arrived(xs, row_of(batch), 1 - core, h)
            multiply(s)
            done.append(s)
            if len(done) > 2:
                halve(done[-3])
            if len(done) > 6:
                settle(done[-7])

    ready = {}

    def settle(s):
        finish(s)
        key = (passing(s // 4), s % 4)
        ready[key] = ready.get(key, 0) + 1
        if ready[key] == 2:
            cross(*key)
            if ready.get((1 - key[0], key[1]), 0) == 2:
                open_columns.append(key[1])

    open_columns = []

    keep[0].wait()
    share(x, y_lo, 0, at_xp, at_xo, at_y, at_sib)
    prompts(0, 8)
    keep[1].wait()
    pass_on(xo, y_lo, 0, at_xp)
    share(x, y_lo, 1, at_xo, at_y)
    share(xo, y_lo, 0, at_sib)
    pass_on(xp, y_lo, 0, at_sib)
    share(x, y_lo, 1, at_sib)
    steps(0, 0)
    pass_on(x, 1 - y_lo, 0, at_sib)
    prepare()
    load_qm.wait()
    stores = prelude(0)
    pass_on(xo, y_lo, 1)
    share(x, y_lo, 1, at_xp)
    share(x, 1 - y_lo, 0, at_xo)
    pass_on(xf, y_lo, 0, at_y, at_sib)
    share(xo, y_lo, 1, at_sib)
    pass_on(x, 1 - y_lo, 1, at_sib)
    steps(1, 0)
    for copy in stores:
        copy.wait()
    stores = prelude(1)
    pass_on(xp, y_lo, 1, at_xo)
    share(x, 1 - y_lo, 0, at_xp)
    share(xp, y_lo, 1, at_sib)
    pass_on(xo, 1 - y_lo, 0, at_sib)
    steps(0, 1)
    pass_on(xf, 1 - y_lo, 0, at_sib)
    steps(3, 0)
    for copy in stores:
        copy.wait()
    stores = prelude(2)
    pass_on(xf, y_lo, 1, at_y)
    share(x, 1 - y_lo, 1, at_xp, at_xo)
    share(xf, y_lo, 1, at_sib)
    steps(1, 1)
    pass_on(xp, 1 - y_lo, 0, at_sib)
    steps(2, 0)
    for copy in stores:
        copy.wait()
    stores = prelude(3)
    pass_on(xp, 1 - y_lo, 1, at_sib)
    steps(2, 1)
    pass_on(xo, 1 - y_lo, 1, at_sib)
    pass_on(xf, 1 - y_lo, 1, at_sib)
    steps(3, 1)
    halve(done[-2])
    halve(done[-1])
    for s in done[-6:]:
        settle(s)
        while len(open_columns) > 1:
            close(open_columns.pop(0))
    while open_columns:
        close(open_columns.pop(0))
    for copy in stores:
        copy.wait()
    for copy in shared:
        copy.wait_send()
    for s in range(16):
        for part in range(2):
            first(s, part).wait_send()

        @pl.when(between(s // 4))
        def _():
            for part in range(2):
                second(s, part).wait_send()

    for i in range(4):
        across(0, i).wait_send()


def projected(
    owner,
    lengths,
    timesteps,
    query_states,
    prompt_keys,
    prompt_values,
    query_keys,
    query_values,
    residual,
    gain,
    latents,
    noise,
    patch_weight,
    time_embedding,
    norm_gain,
    vhw,
    weight,
    qm,
):
    rows = query_states.shape[0] * NQ
    tokens = latents.shape[0]
    vmem, smem = pl.BlockSpec(memory_space=pltpu.VMEM), pl.BlockSpec(memory_space=pltpu.SMEM)
    anywhere = pl.BlockSpec(memory_space=pl.ANY)
    return pl.pallas_call(
        project_kernel,
        out_shape=[
            jax.ShapeDtypeStruct((rows, 1024), BF16),
            jax.ShapeDtypeStruct((rows, 128), F32),
            jax.ShapeDtypeStruct((tokens, 128), F32),
            jax.ShapeDtypeStruct((tokens, W), BF16),
            jax.ShapeDtypeStruct((GRAD_ROWS, tokens), BF16),
        ],
        in_specs=[smem] * 3 + [vmem] * 13 + [anywhere] * 2,
        out_specs=[vmem] * 3 + [anywhere] * 2,
        scratch_shapes=[
            pltpu.VMEM((rows, 1024), BF16),
            pltpu.VMEM((4, 2, 2, 2, 1024, 256), BF16),
            pltpu.VMEM((16, 2, 2, 256, 256), BF16),
            pltpu.VMEM((16, 2, 256, 256), BF16),
            pltpu.VMEM((2, 4, 2, 256, 256), BF16),
            pltpu.VMEM((2, 4, rows, 256), BF16),
            pltpu.VMEM((4, rows, 256), BF16),
            pltpu.VMEM(qm.shape, BF16),
            pltpu.VMEM((256, W), BF16),
            pltpu.VMEM((GRAD_ROWS, 128), BF16),
            pltpu.VMEM((GRAD_ROWS, 128), F32),
            pltpu.VMEM((TOKENS, W), BF16),
            pltpu.VMEM((GRAD_ROWS, TOKENS), BF16),
            pltpu.SemaphoreType.DMA((2,)),
            pltpu.SemaphoreType.DMA((1,)),
            pltpu.SemaphoreType.DMA((4, 2)),
            pltpu.SemaphoreType.DMA((32,)),
            pltpu.SemaphoreType.DMA((4, 2, 2, 2)),
            pltpu.SemaphoreType.DMA((16, 4)),
            pltpu.SemaphoreType.DMA((16, 4)),
            pltpu.SemaphoreType.DMA((4,)),
            pltpu.SemaphoreType.DMA((4,)),
        ],
        compiler_params=pltpu.CompilerParams(
            collective_id=2, has_side_effects=True, vmem_limit_bytes=62 << 20
        ),
        name="attend_project",
    )(
        owner,
        lengths,
        timesteps,
        query_states,
        prompt_keys,
        prompt_values,
        query_keys,
        query_values,
        residual,
        gain.reshape(1, -1),
        latents,
        noise,
        patch_weight,
        time_embedding,
        norm_gain,
        vhw,
        weight,
        qm,
    )


COLUMNS = 256
CHUNKS = 2 * W // COLUMNS


def connect_kernel(
    scaled_ref,
    sq_ref,
    conn_hbm,
    cond_ref,
    conn,
    buf,
    land1,
    land2,
    land3,
    sqb,
    sq1,
    sq2,
    sq3,
    load_sem,
    send_sem,
    recv_sem,
):
    x, y, z, core = places()
    y_hi = y // 2
    at_ze, at_zo = device_at(x, y, z + 1 - 2 * (z % 2), core), device_at(x, y, 3 - z, core)
    at_far = device_at(x, (y + 2) % 4, z, core)
    bit_a, bit_b = gray_bits(z)
    loads = [
        pltpu.make_async_copy(
            conn_hbm.at[:, part * 512 : (part + 1) * 512], conn.at[:, part * 512 : (part + 1) * 512], load_sem.at[part]
        )
        for part in range(7)
    ]
    for copy in loads:
        copy.start()

    greet((at_ze, at_zo, at_far))

    sent = []
    flying = {}

    def send(j, phase):
        if j == CHUNKS:
            block, landing = sqb, (sq1, sq2, sq3)[phase]
        else:
            block, landing = buf.at[j], (land1, land2, land3)[phase].at[j]
        if phase == 0:
            source = block.at[:, 1 - bit_a] if j % 2 == 0 else block.at[:, :, 1 - bit_b]
        elif phase == 1:
            source = block.at[:, bit_a, 1 - bit_b] if j % 2 == 0 else block.at[:, 1 - bit_a, bit_b]
        else:
            source = block.at[1 - y_hi, bit_a, bit_b]
        copy = pltpu.make_async_remote_copy(
            src_ref=source,
            dst_ref=landing,
            send_sem=send_sem.at[j, phase],
            recv_sem=recv_sem.at[j, phase],
            device_id=at_far if phase == 2 else at_ze if phase == j % 2 else at_zo,
            device_id_type=MESH,
        )
        copy.start()
        sent.append(copy)
        flying[j] = copy

    def settle(j, phase):
        flying[j].wait_recv()
        if phase == 0:
            index = (slice(None), bit_a) if j % 2 == 0 else (slice(None), slice(None), bit_b)
        else:
            index = (slice(None), bit_a, bit_b)
        if j == CHUNKS:
            sqb[index] = sqb[index] + (sq1, sq2)[phase][...]
        else:
            index = (j,) + index
            total = buf[index].astype(F32) + (land1, land2)[phase][j].astype(F32)
            buf[index] = total.astype(BF16)
        send(j, phase + 1)

    def spread(block, value):
        for m in range(8):
            a, b = gray_bits(m % 4)
            block[m // 4, a, b] = value[m * NQ : (m + 1) * NQ]

    chunks = [CHUNKS] + list(range(CHUNKS))
    for n in range(CHUNKS + 1 + 10):
        if n == 0:
            spread(sqb, sq_ref[...])
            send(CHUNKS, 0)
        elif n <= CHUNKS:
            j = chunks[n]
            if j % 2 == 0:
                loads[j // 2].wait()
            value = nn_dot(scaled_ref[...], conn[:, j * COLUMNS : (j + 1) * COLUMNS])
            spread(buf.at[j], value.astype(BF16))
            send(j, 0)
        if 0 <= n - 6 <= CHUNKS:
            settle(chunks[n - 6], 0)
        if 0 <= n - 10 <= CHUNKS:
            settle(chunks[n - 10], 1)
    flying[CHUNKS].wait_recv()
    squares = sqb[y_hi, bit_a, bit_b] + sq3[...]
    factor = lax.rsqrt(jnp.sum(squares, -1, keepdims=True) / D + eps)
    for j in range(CHUNKS):
        flying[j].wait_recv()
        total = buf[j, y_hi, bit_a, bit_b].astype(F32) + land3[j].astype(F32)
        cond_ref[:, j * COLUMNS : (j + 1) * COLUMNS] = (total * factor).astype(BF16)
    for copy in sent:
        copy.wait_send()


def connected(scaled, squares, conn_weight):
    vmem = pl.BlockSpec(memory_space=pltpu.VMEM)
    return pl.pallas_call(
        connect_kernel,
        out_shape=jax.ShapeDtypeStruct((NQ, 2 * W), BF16),
        in_specs=[vmem, vmem, pl.BlockSpec(memory_space=pl.ANY)],
        out_specs=vmem,
        scratch_shapes=[
            pltpu.VMEM(conn_weight.shape, BF16),
            pltpu.VMEM((CHUNKS, 2, 2, 2, NQ, COLUMNS), BF16),
            pltpu.VMEM((CHUNKS, 2, 2, NQ, COLUMNS), BF16),
            pltpu.VMEM((CHUNKS, 2, NQ, COLUMNS), BF16),
            pltpu.VMEM((CHUNKS, NQ, COLUMNS), BF16),
            pltpu.VMEM((2, 2, 2, NQ, 128), F32),
            pltpu.VMEM((2, 2, NQ, 128), F32),
            pltpu.VMEM((2, NQ, 128), F32),
            pltpu.VMEM((NQ, 128), F32),
            pltpu.SemaphoreType.DMA((7,)),
            pltpu.SemaphoreType.DMA((CHUNKS + 1, 3)),
            pltpu.SemaphoreType.DMA((CHUNKS + 1, 3)),
        ],
        compiler_params=pltpu.CompilerParams(
            collective_id=3, has_side_effects=True, vmem_limit_bytes=58 << 20
        ),
        name="connect",
    )(scaled, squares, conn_weight)


def on_device(
    prompt_keys,
    prompt_values,
    query_states,
    query_keys,
    query_values,
    lengths,
    residual,
    out_weight,
    final_gain,
    conn_weight,
    owner,
    latents,
    noise,
    timesteps,
    patch_weight,
    time_embedding,
    image_norm_gain,
    query_matrix,
    velocity_head_weight,
):
    count_of_rows = lax.axis_size("dp") * lax.axis_size("tensor") * latents.shape[1]
    scaled, squares, hv, q, normed_t = projected(
        owner,
        lengths,
        timesteps,
        query_states,
        prompt_keys,
        prompt_values,
        query_keys,
        query_values,
        residual,
        final_gain,
        latents[0],
        noise[0],
        patch_weight,
        time_embedding,
        image_norm_gain,
        velocity_head_weight,
        out_weight,
        query_matrix,
    )
    cond = connected(scaled, squares, conn_weight)
    velocity, dq = step(
        q, hv, latents[0], noise[0], cond, velocity_head_weight, grad_gain / math.sqrt(count_of_rows)
    )
    return (velocity[None], summed_gradient(normed_t, dq))


def solution(mesh):
    return jax.shard_map(
        on_device,
        mesh=mesh,
        in_specs=(
            P("dp", None, "tensor"),
            P("dp", None, "tensor"),
            P("dp", None, "tensor"),
            P("dp", None, "tensor"),
            P("dp", None, "tensor"),
            P("dp"),
            P("dp", None, "tensor"),
            P("tensor", "dp"),
            P("tensor"),
            P("tensor", None),
            P("dp", None),
            P(("dp", "tensor"), None, None),
            P(("dp", "tensor"), None, None),
            P(("dp", "tensor")),
            P(),
            P(),
            P(),
            P(),
            P(),
        ),
        out_specs=(P(("dp", "tensor"), None, None), P(("dp", "tensor"), None)),
        check_vma=False,
    )
```

```python
import math

import jax
import jax.numpy as jnp
from jax import lax
from jax.experimental import pallas as pl
from jax.experimental.pallas import tpu as pltpu
from jax.sharding import PartitionSpec as P

D = 8192
HEAD = 128
NQ = 64
DHEAD = 112
NT = 1000
W = 1792
IMG_HEADS = 16
F32 = jnp.float32
BF16 = jnp.bfloat16
MESH = pl.DeviceIdType.MESH

eps = 1e-06
grad_gain = 16.0

ROWS_BLOCK = 14
ROWS_PAD = 16
PIECES = (384, 384, 256, 256, 256, 256)
STARTS = (0, 384, 768, 1024, 1280, 1536)
KEY_WINDOWS = (0, 384, 896, 1280)
SCORE_WINDOWS = (0, 128, 256, 384, 512, 640, 768)


def nt_dot(a, b):
    return lax.dot_general(a, b, (((1,), (1,)), ((), ())), preferred_element_type=F32)


def nn_dot(a, b):
    return jnp.dot(a, b, preferred_element_type=F32)


def head_mask(rows, width, head, base):
    lane = lax.broadcasted_iota(jnp.int32, (rows, width), 1) + base
    return (lane >= head * DHEAD) & (lane < (head + 1) * DHEAD)


def only_head(block, head, base):
    return jnp.where(head_mask(*block.shape, head, base), block.astype(F32), 0.0).astype(BF16)


def step_kernel(
    gain, q_ref, hv_ref, lat_ref, noise_ref, cond_ref, vhw_ref, vel_ref, dq_ref, kbd, kflat, vw, ones, probs, dsc
):
    scale = 1.0 / DHEAD**0.5
    keys = cond_ref.shape[0]

    @pl.when(pl.program_id(0) == 0)
    def _():
        for g, base in enumerate(KEY_WINDOWS):
            vals = []
            for n in range(4):
                window = cond_ref[:, base : base + 512]
                kbd[g, n * keys : (n + 1) * keys, :] = only_head(window, 4 * g + n, base)
                window = cond_ref[:, W + base : W + base + 512]
                vals.append(only_head(window, 4 * g + n, base))
            vw[g] = nn_dot(jnp.concatenate(vals, 0), vhw_ref[base : base + 512, :]).astype(BF16)
        for tile, first in enumerate(SCORE_WINDOWS):
            for n in range(4):
                window = cond_ref[:, tile * 256 : (tile + 1) * 256]
                kflat[tile, n * keys : (n + 1) * keys, :] = only_head(window, first // keys + n, tile * 256)
        row = lax.broadcasted_iota(jnp.int32, (256, 256), 0) // keys
        column = lax.broadcasted_iota(jnp.int32, (256, 256), 1) // keys
        ones[...] = jnp.where(row == column, 1.0, 0.0).astype(BF16)

    velocity = hv_ref[...]
    for g, base in enumerate(KEY_WINDOWS):
        expo = jnp.exp(nt_dot(q_ref[:, base : base + 512], kbd[g]) * scale)
        total = nn_dot(jnp.minimum(expo, 3.38e38).astype(BF16), ones[...])
        p = expo / total
        probs[:, g * 256 : (g + 1) * 256] = p
        velocity = velocity + nn_dot(p.astype(BF16), vw[g])
    vel_ref[...] = velocity
    target = noise_ref[...].astype(F32) - lat_ref[...].astype(F32)
    dvel = ((velocity - target) * gain).astype(BF16)
    for g in range(4):
        p = probs[:, g * 256 : (g + 1) * 256]
        dprob = nt_dot(dvel, vw[g])
        both = p * dprob
        high = both.astype(BF16)
        low = (both - high.astype(F32)).astype(BF16)
        shift = nn_dot(high, ones[...]) + nn_dot(low, ones[...])
        dsc[:, g * 256 : (g + 1) * 256] = (p * (dprob - shift) * scale).astype(BF16)
    for tile, first in enumerate(SCORE_WINDOWS):
        dq_ref[:, tile * 256 : (tile + 1) * 256] = nn_dot(dsc[:, first : first + 256], kflat[tile]).astype(BF16)


def step(q, hv, latents, noise, cond, vhw, gain):
    tokens = q.shape[0]
    block = 256
    keys = cond.shape[0]
    whole = lambda a: pl.BlockSpec(a.shape, lambda i: (0,) * a.ndim)
    rows = lambda width: pl.BlockSpec((block, width), lambda i: (i, 0))
    return pl.pallas_call(
        lambda *refs: step_kernel(gain, *refs),
        grid=(tokens // block,),
        in_specs=[rows(W), rows(128), rows(128), rows(128), whole(cond), whole(vhw)],
        out_specs=[rows(128), rows(W)],
        out_shape=[jax.ShapeDtypeStruct((tokens, 128), F32), jax.ShapeDtypeStruct((tokens, W), BF16)],
        scratch_shapes=[
            pltpu.VMEM((4, 4 * keys, 512), BF16),
            pltpu.VMEM((7, 4 * keys, 256), BF16),
            pltpu.VMEM((4, 4 * keys, 128), BF16),
            pltpu.VMEM((256, 256), BF16),
            pltpu.VMEM((block, 1024), F32),
            pltpu.VMEM((block, 1024), BF16),
        ],
        compiler_params=pltpu.CompilerParams(vmem_limit_bytes=48 << 20),
        cost_estimate=pl.CostEstimate(flops=6 * 10**9, bytes_accessed=10 * 10**6, transcendentals=10**6),
        name="flow_step",
    )(q, hv, latents, noise, cond, vhw)


def places():
    dp, tensor = lax.axis_index("dp"), lax.axis_index("tensor")
    return dp // 4, (tensor // 4) * 2 + (dp // 2) % 2, tensor % 4, dp % 2


def device_at(x, y, z, core):
    return (x * 4 + (y % 2) * 2 + core, (y // 2) * 4 + z)


def link_partners(x, y, z, core):
    pair = lambda i: i + 1 - 2 * (i % 2)
    other = lambda i: 3 - i
    return (
        device_at(pair(x), y, z, core),
        device_at(other(x), y, z, core),
        device_at(x, pair(y), z, core),
        device_at(x, other(y), z, core),
        device_at(x, y, pair(z), core),
        device_at(x, y, other(z), core),
    )


def gray_bits(i):
    return (i + i // 2) % 2, i // 2


def grad_kernel(nt_ref, dq_ref, out_ref, *scratch):
    mine, away, sibling_part = scratch[0:6], scratch[6:12], scratch[12:18]
    landing = [scratch[18 + 6 * p : 24 + 6 * p] for p in range(6)]
    core_send, core_recv, send_sem, recv_sem = scratch[54:58]
    x, y, z, core = places()
    partners = link_partners(x, y, z, core)
    sibling = device_at(x, y, z, 1 - core)
    bits = gray_bits(x) + gray_bits(y) + gray_bits(z)

    barrier = pltpu.get_barrier_semaphore()
    for device in partners + (sibling,):
        pl.semaphore_signal(barrier, inc=1, device_id=device, device_id_type=MESH)
    pl.semaphore_wait(barrier, 7)

    def product(p, which, target):
        columns = pl.ds(STARTS[p], PIECES[p])

        def part(i, carry):
            rows = nt_ref[which, pl.ds(pl.multiple_of(i * 512, 512), 512), :]
            value = nn_dot(rows, dq_ref[:, columns]).astype(BF16)
            target[i] = value.reshape(2, 2, 2, 2, 2, ROWS_PAD, PIECES[p])
            return carry

        lax.fori_loop(0, 2, part, 0)

    def region(p, k, bit):
        index = []
        for dim in range(6):
            age = (dim - p) % 6
            index.append(bits[dim] if age < k else bit if age == k else slice(None))
        return tuple(index)

    def to_sibling(p):
        return pltpu.make_async_remote_copy(
            src_ref=away[p],
            dst_ref=sibling_part[p],
            send_sem=core_send.at[p],
            recv_sem=core_recv.at[p],
            device_id=sibling,
            device_id_type=MESH,
        )

    def exchange(p, k):
        dim = (p + k) % 6
        return pltpu.make_async_remote_copy(
            src_ref=mine[p].at[region(p, k, 1 - bits[dim])],
            dst_ref=landing[p][k],
            send_sem=send_sem.at[p, k],
            recv_sem=recv_sem.at[p, k],
            device_id=partners[dim],
            device_id_type=MESH,
        )

    sent = []
    flying = {}

    def send(p, copy):
        copy.start()
        flying[p] = copy
        sent.append(copy)

    def settle(p, k):
        flying[p].wait_recv()
        if k == 0:
            index = (slice(None),) * 6
            arrived = sibling_part[p]
        else:
            index = region(p, k - 1, bits[(p + k - 1) % 6])
            arrived = landing[p][k - 1]
        total = mine[p][index].astype(F32) + arrived[...].astype(F32)
        if k == 6:
            out_ref[:, STARTS[p] : STARTS[p] + PIECES[p]] = total
        else:
            mine[p][index] = total.astype(BF16)
            send(p, exchange(p, k))

    for p in range(7):
        if p < 6:
            product(p, 1 - core, away[p])
            send(p, to_sibling(p))
            product(p, core, mine[p])
        if p > 0:
            settle(p - 1, 0)
    for k in range(1, 7):
        for p in range(6):
            settle(p, k)
    for copy in sent:
        copy.wait_send()


def summed_gradient(normed_t, dq):
    tokens = dq.shape[0]
    full = [pltpu.VMEM((2,) * 6 + (ROWS_PAD, c), BF16) for c in PIECES]
    parts = [pltpu.VMEM((2,) * (5 - k) + (ROWS_PAD, c), BF16) for c in PIECES for k in range(6)]
    out = pl.pallas_call(
        grad_kernel,
        out_shape=jax.ShapeDtypeStruct((ROWS_PAD, W), F32),
        in_specs=[pl.BlockSpec(memory_space=pltpu.VMEM)] * 2,
        out_specs=pl.BlockSpec(memory_space=pltpu.VMEM),
        scratch_shapes=full
        + full
        + full
        + parts
        + [
            pltpu.SemaphoreType.DMA((6,)),
            pltpu.SemaphoreType.DMA((6,)),
            pltpu.SemaphoreType.DMA((6, 6)),
            pltpu.SemaphoreType.DMA((6, 6)),
        ],
        compiler_params=pltpu.CompilerParams(
            collective_id=1, has_side_effects=True, vmem_limit_bytes=48 << 20
        ),
        name="grad_sum",
    )(normed_t.reshape(2, -1, tokens), dq)
    return out[:ROWS_BLOCK]


def attend(m, owner_ref, len_ref, q_ref, pk_ref, pv_ref, ok_ref, ov_ref, att):
    prompt = owner_ref[0, m]
    length = len_ref[prompt]
    scale = 1.0 / HEAD**0.5
    own_k, own_v = ok_ref[prompt], ov_ref[prompt]
    keys, values = pk_ref[prompt], pv_ref[prompt]
    states = q_ref[prompt]
    heads = states.shape[1] // HEAD
    rows = jnp.concatenate([states[:, j * HEAD : (j + 1) * HEAD] for j in range(heads)], 0)
    first = nt_dot(rows, keys) * scale
    second = nt_dot(rows, own_k) * scale
    column = lax.broadcasted_iota(jnp.int32, first.shape, 1)
    first = jnp.where(column < length, first, -jnp.inf)
    row = lax.broadcasted_iota(jnp.int32, second.shape, 0) % NQ
    column = lax.broadcasted_iota(jnp.int32, second.shape, 1)
    second = jnp.where(column <= row, second, -jnp.inf)
    top = jnp.maximum(jnp.max(first, -1, keepdims=True), jnp.max(second, -1, keepdims=True))
    first, second = jnp.exp(first - top), jnp.exp(second - top)
    total = jnp.sum(first, -1, keepdims=True) + jnp.sum(second, -1, keepdims=True)
    out = nn_dot(first.astype(BF16), values) + nn_dot(second.astype(BF16), own_v)
    out = (out / total).astype(BF16)
    rows_at = pl.ds(pl.multiple_of(m * NQ, NQ), NQ)
    for j in range(heads):
        att[rows_at, j * HEAD : (j + 1) * HEAD] = out[j * NQ : (j + 1) * NQ]


def greet(devices):
    barrier = pltpu.get_barrier_semaphore()
    for device in devices:
        pl.semaphore_signal(barrier, inc=1, device_id=device, device_id_type=MESH)
    pl.semaphore_wait(barrier, len(devices))


TOKENS = 256
GRAD_ROWS = 2048


def one_hot_rows(start, rows):
    row = lax.broadcasted_iota(jnp.int32, (rows, 1), 0) + start
    bit = lambda n: row // (ROWS_PAD << n) % 2
    at = lambda n: 2 * bit(n) + (bit(n) + bit(n + 1)) % 2
    z, y, x, core = at(0), at(2), at(4), bit(6)
    natural = ((x * 2 + y % 2) * 2 + core) * 8 + y // 2 * 4 + z
    inside = row % ROWS_PAD
    source = jnp.where(inside < ROWS_BLOCK, natural * ROWS_BLOCK + inside, -1)
    lane = lax.broadcasted_iota(jnp.int32, (rows, W), 1)
    return jnp.where(lane == source, 1.0, 0.0).astype(BF16)


def split_in_three(value):
    parts = []
    for _ in range(3):
        part = value.astype(BF16)
        parts.append(part)
        value = value - part.astype(F32)
    return parts


def project_kernel(
    owner_ref,
    len_ref,
    step_ref,
    q_ref,
    pk_ref,
    pv_ref,
    ok_ref,
    ov_ref,
    res_ref,
    gain_ref,
    lat_ref,
    noise_ref,
    pw_ref,
    time_ref,
    norm_ref,
    vhw_ref,
    w_hbm,
    qm_hbm,
    scaled_ref,
    sq_ref,
    hv_ref,
    q_hbm,
    nt_hbm,
    att,
    wg,
    terms,
    land_first,
    land_second,
    zsum,
    relay,
    landy,
    qm,
    packed,
    pwt,
    col,
    q_out,
    nt_out,
    own_sem,
    qm_sem,
    out_sem,
    w_send,
    w_recv,
    r_send,
    r_recv,
    y_send,
    y_recv,
):
    x, y, z, core = places()
    y_lo, y_hi = y % 2, y // 2
    xp, xo, xf = x + 1 - 2 * (x % 2), 3 - x, (x + 2) % 4
    at_y = device_at(x, y + 1 - 2 * y_lo, z, core)
    at_xp, at_xo = device_at(xp, y, z, core), device_at(xo, y, z, core)
    at_ze, at_zo = device_at(x, y, z + 1 - 2 * (z % 2), core), device_at(x, y, 3 - z, core)
    at_yo = device_at(x, 3 - y, z, core)
    at_sib = device_at(x, y, z, 1 - core)
    bit_b = z // 2
    shared = []

    keep = [
        pltpu.make_async_copy(w_hbm.at[:, h * 256 : (h + 1) * 256], wg.at[x, y_lo, core, h], own_sem.at[h])
        for h in range(2)
    ]
    load_qm = pltpu.make_async_copy(qm_hbm, qm, qm_sem.at[0])
    for copy in keep + [load_qm]:
        copy.start()
    greet((at_y, at_yo, at_xp, at_xo, at_ze, at_zo, at_sib))

    def share(xs, ys, h, *targets):
        slot = wg.at[xs, ys, core, h]
        for target in targets:
            copy = pltpu.make_async_remote_copy(
                src_ref=slot,
                dst_ref=slot,
                send_sem=w_send.at[len(shared)],
                recv_sem=w_recv.at[xs, ys, core, h],
                device_id=target,
                device_id_type=MESH,
            )
            copy.start()
            shared.append(copy)

    def arrived(xs, ys, cs, h):
        slot = wg.at[xs, ys, cs, h]
        pltpu.make_async_remote_copy(
            src_ref=slot,
            dst_ref=slot,
            send_sem=w_send.at[0],
            recv_sem=w_recv.at[xs, ys, cs, h],
            device_id=at_sib,
            device_id_type=MESH,
        ).wait_recv()

    def pass_on(xs, ys, h, *targets):
        arrived(xs, ys, core, h)
        share(xs, ys, h, *targets)

    def prepare():
        packed[0:128, :] = pw_ref[...]
        parts = split_in_three(time_ref[...].reshape(1, W)) + split_in_three(norm_ref[...].reshape(1, W))
        packed[128:256, :] = jnp.concatenate(parts + [jnp.zeros((122, W), BF16)], 0)

        def body(i, carry):
            rows = pl.ds(pl.multiple_of(i * 256, 256), 256)
            value = nt_dot(one_hot_rows(i * 256, 256), packed[...])
            pwt[rows, :] = value[:, :128].astype(BF16)
            col[rows, :] = value[:, 128:]
            return carry

        lax.fori_loop(0, GRAD_ROWS // 256, body, 0)

    def prelude(c):
        t = (step_ref[0].astype(F32) + 0.5) / NT
        rows = pl.ds(c * TOKENS, TOKENS)
        noisy = ((1.0 - t) * lat_ref[rows, :].astype(F32) + t * noise_ref[rows, :].astype(F32)).astype(BF16)
        hidden = nn_dot(noisy, pw_ref[...]) + t * time_ref[...].reshape(1, W)
        scale = lax.rsqrt(jnp.mean(hidden * hidden, -1, keepdims=True) + eps)
        normed = (hidden * scale * norm_ref[...].reshape(1, W)).astype(BF16)
        hv_ref[rows, :] = nn_dot(hidden.astype(BF16), vhw_ref[...])
        q_out[...] = nn_dot(normed, qm[...]).astype(BF16)
        time_col = col[:, 0:1] + col[:, 1:2] + col[:, 2:3]
        norm_col = col[:, 3:4] + col[:, 4:5] + col[:, 5:6]
        ht = nt_dot(pwt[...], noisy) + t * time_col
        scale_t = lax.rsqrt(jnp.sum(ht * ht, 0, keepdims=True) / W + eps)
        nt_out[...] = (ht * scale_t * norm_col).astype(BF16)
        copies = (
            pltpu.make_async_copy(q_out, q_hbm.at[c * TOKENS : (c + 1) * TOKENS, :], out_sem.at[c, 0]),
            pltpu.make_async_copy(nt_out, nt_hbm.at[:, c * TOKENS : (c + 1) * TOKENS], out_sem.at[c, 1]),
        )
        for copy in copies:
            copy.start()
        return copies

    def prompts(start, end):
        def body(m, carry):
            attend(m, owner_ref, len_ref, q_ref, pk_ref, pv_ref, ok_ref, ov_ref, att)
            return carry

        lax.fori_loop(start, end, body, 0)

    first_chip = (x // 2, 1 - x // 2)
    chips = ((x, xp), (xo, xf))
    subs = ((core, 0), (1 - core, 0), (core, 1), (1 - core, 1))
    mine = bit_b

    def row_of(batch):
        return y_lo if batch < 2 else 1 - y_lo

    def passing(batch):
        return batch % 2

    def at_end(batch):
        return z % 2 == row_of(batch)

    def between(batch):
        return z % 2 != row_of(batch)

    def remote(s, which, source, landing, device):
        return pltpu.make_async_remote_copy(
            src_ref=source,
            dst_ref=landing,
            send_sem=r_send.at[s, which],
            recv_sem=r_recv.at[s, which],
            device_id=device,
            device_id_type=MESH,
        )

    def out_block(s):
        return (mine + z + row_of(s // 4) + 1) % 2

    def first(s, part):
        block = out_block(s) if part == 0 else 1 - mine
        return remote(s, part, terms.at[s, part, block], land_first.at[s, part], at_ze if part == 0 else at_zo)

    def second(s, part):
        block = 1 - mine if part == 0 else mine
        landing = land_second.at[passing(s // 4), s % 4, part]
        return remote(s, 2 + part, terms.at[s, part, block], landing, at_zo if part == 0 else at_ze)

    def multiply(s):
        batch = s // 4
        cs, h = subs[s % 4]

        def body(u, carry):
            value = nn_dot(att[...], wg[2 * first_chip[passing(batch)] + u, row_of(batch), cs, h]).astype(BF16)
            terms[s, 0, u] = value[:256]
            terms[s, 1, u] = value[256:]
            return carry

        lax.fori_loop(0, 2, body, 0)
        for part in range(2):
            first(s, part).start()

    def halve(s):
        for part in range(2):
            first(s, part).wait_recv()
            block = 1 - out_block(s) if part == 0 else mine
            total = terms[s, part, block].astype(F32) + land_first[s, part].astype(F32)
            terms[s, part, block] = total.astype(BF16)

        @pl.when(between(s // 4))
        def _():
            for part in range(2):
                second(s, part).start()

    def finish(s):
        batch = s // 4

        @pl.when(at_end(batch))
        def _():
            for part in range(2):
                second(s, part).wait_recv()
                landing = land_second[passing(batch), s % 4, part]
                total = terms[s, part, mine].astype(F32) + landing.astype(F32)
                zsum[passing(batch), s % 4, part * 256 : (part + 1) * 256] = total.astype(BF16)

    kept = (x // 2 + y_hi) % 2

    def across(i, leg):
        part = leg % 2
        if leg < 2:
            source, landing = zsum.at[1 - kept, i, part * 256 : (part + 1) * 256], relay.at[i, part]
        else:
            source, landing = relay.at[i, part], landy.at[i, part]
        return pltpu.make_async_remote_copy(
            src_ref=source,
            dst_ref=landing,
            send_sem=y_send.at[i, leg],
            recv_sem=y_recv.at[i, leg],
            device_id=at_y if leg in (0, 3) else at_yo,
            device_id_type=MESH,
        )

    def cross(i):
        across(i, 0).start()
        across(i, 1).start()

    def relay_on(i):
        for part in range(2):
            across(i, part).wait_recv()
            across(i, 2 + part).start()

    def close(i):
        for part in range(2):
            across(i, 2 + part).wait_recv()
        cs, h = subs[i]
        columns = pl.ds(pl.multiple_of(cs * 512 + h * 256, 256), 256)
        gain = gain_ref[:, columns]

        def body(m, carry):
            rows = pl.ds(pl.multiple_of(m * NQ, NQ), NQ)
            part, inside = m // 4, pl.ds(pl.multiple_of(m % 4 * NQ, NQ), NQ)
            value = res_ref[owner_ref[0, m], :, columns].astype(F32)
            value = value + (zsum[kept, i, rows, :].astype(F32) + landy[i, part, inside, :].astype(F32))
            scaled_ref[rows, columns] = (value * gain).astype(BF16)
            square = value * value
            square = square[:, :128] + square[:, 128:]
            sq_ref[rows, :] = square if i == 0 else sq_ref[rows, :] + square
            return carry

        lax.fori_loop(0, 8, body, 0)

    def steps(batch, h):
        for s in (4 * batch + 2 * h, 4 * batch + 2 * h + 1):
            if s % 2 == 1:
                for xs in chips[passing(batch)]:
                    arrived(xs, row_of(batch), 1 - core, h)
            multiply(s)

    def each(do, *numbers):
        for s in numbers:
            do(s)

    keep[0].wait()
    share(x, y_lo, 0, at_xp, at_xo, at_y, at_sib)
    prompts(0, 4)
    keep[1].wait()
    pass_on(xo, y_lo, 0, at_xp)
    share(x, y_lo, 1, at_xo, at_y)
    share(xo, y_lo, 0, at_sib)
    pass_on(xp, y_lo, 0, at_sib)
    share(x, y_lo, 1, at_sib)
    prompts(4, 8)
    steps(0, 0)
    pass_on(x, 1 - y_lo, 0, at_sib)
    prepare()
    load_qm.wait()
    stores = prelude(0)
    each(halve, 0, 1)

    pass_on(xo, y_lo, 1)
    share(x, y_lo, 1, at_xp)
    share(x, 1 - y_lo, 0, at_xo)
    pass_on(xf, y_lo, 0, at_y, at_sib)
    share(xo, y_lo, 1, at_sib)
    pass_on(x, 1 - y_lo, 1, at_sib)
    steps(1, 0)
    for copy in stores:
        copy.wait()
    stores = prelude(1)
    each(halve, 4, 5)
    each(finish, 0, 1)

    pass_on(xp, y_lo, 1, at_xo)
    share(x, 1 - y_lo, 0, at_xp)
    share(xp, y_lo, 1, at_sib)
    pass_on(xo, 1 - y_lo, 0, at_sib)
    steps(0, 1)
    pass_on(xf, 1 - y_lo, 0, at_sib)
    steps(3, 0)
    for copy in stores:
        copy.wait()
    stores = prelude(2)
    each(halve, 2, 3)
    each(finish, 4, 5)

    pass_on(xf, y_lo, 1, at_y)
    share(x, 1 - y_lo, 1, at_xp, at_xo)
    share(xf, y_lo, 1, at_sib)
    pass_on(xp, 1 - y_lo, 0, at_sib)
    steps(2, 0)
    steps(1, 1)
    each(halve, 12, 13)
    for copy in stores:
        copy.wait()
    stores = prelude(3)
    each(halve, 8, 9)
    each(finish, 2, 3)

    pass_on(xp, 1 - y_lo, 1, at_sib)
    steps(2, 1)
    pass_on(xo, 1 - y_lo, 1, at_sib)
    pass_on(xf, 1 - y_lo, 1, at_sib)
    steps(3, 1)
    each(halve, 6, 7)
    each(finish, 12, 8)
    cross(0)
    each(finish, 13, 9)
    cross(1)
    each(halve, 10, 11)
    relay_on(0)
    each(halve, 14, 15)
    relay_on(1)
    each(finish, 6, 10, 14)
    cross(2)
    each(finish, 7, 11, 15)
    cross(3)
    close(0)
    close(1)
    relay_on(2)
    relay_on(3)
    close(2)
    close(3)
    for copy in stores:
        copy.wait()
    for copy in shared:
        copy.wait_send()
    for s in range(16):
        for part in range(2):
            first(s, part).wait_send()

        @pl.when(between(s // 4))
        def _():
            for part in range(2):
                second(s, part).wait_send()

    for i in range(4):
        for leg in range(4):
            across(i, leg).wait_send()


def projected(
    owner,
    lengths,
    timesteps,
    query_states,
    prompt_keys,
    prompt_values,
    query_keys,
    query_values,
    residual,
    gain,
    latents,
    noise,
    patch_weight,
    time_embedding,
    norm_gain,
    vhw,
    weight,
    qm,
):
    rows = query_states.shape[0] * NQ
    tokens = latents.shape[0]
    vmem, smem = pl.BlockSpec(memory_space=pltpu.VMEM), pl.BlockSpec(memory_space=pltpu.SMEM)
    anywhere = pl.BlockSpec(memory_space=pl.ANY)
    return pl.pallas_call(
        project_kernel,
        out_shape=[
            jax.ShapeDtypeStruct((rows, 1024), BF16),
            jax.ShapeDtypeStruct((rows, 128), F32),
            jax.ShapeDtypeStruct((tokens, 128), F32),
            jax.ShapeDtypeStruct((tokens, W), BF16),
            jax.ShapeDtypeStruct((GRAD_ROWS, tokens), BF16),
        ],
        in_specs=[smem] * 3 + [vmem] * 13 + [anywhere] * 2,
        out_specs=[vmem] * 3 + [anywhere] * 2,
        scratch_shapes=[
            pltpu.VMEM((rows, 1024), BF16),
            pltpu.VMEM((4, 2, 2, 2, 1024, 256), BF16),
            pltpu.VMEM((16, 2, 2, 256, 256), BF16),
            pltpu.VMEM((16, 2, 256, 256), BF16),
            pltpu.VMEM((2, 4, 2, 256, 256), BF16),
            pltpu.VMEM((2, 4, rows, 256), BF16),
            pltpu.VMEM((4, 2, 256, 256), BF16),
            pltpu.VMEM((4, 2, 256, 256), BF16),
            pltpu.VMEM(qm.shape, BF16),
            pltpu.VMEM((256, W), BF16),
            pltpu.VMEM((GRAD_ROWS, 128), BF16),
            pltpu.VMEM((GRAD_ROWS, 128), F32),
            pltpu.VMEM((TOKENS, W), BF16),
            pltpu.VMEM((GRAD_ROWS, TOKENS), BF16),
            pltpu.SemaphoreType.DMA((2,)),
            pltpu.SemaphoreType.DMA((1,)),
            pltpu.SemaphoreType.DMA((4, 2)),
            pltpu.SemaphoreType.DMA((32,)),
            pltpu.SemaphoreType.DMA((4, 2, 2, 2)),
            pltpu.SemaphoreType.DMA((16, 4)),
            pltpu.SemaphoreType.DMA((16, 4)),
            pltpu.SemaphoreType.DMA((4, 4)),
            pltpu.SemaphoreType.DMA((4, 4)),
        ],
        compiler_params=pltpu.CompilerParams(
            collective_id=2, has_side_effects=True, vmem_limit_bytes=62 << 20
        ),
        name="attend_project",
    )(
        owner,
        lengths,
        timesteps,
        query_states,
        prompt_keys,
        prompt_values,
        query_keys,
        query_values,
        residual,
        gain.reshape(1, -1),
        latents,
        noise,
        patch_weight,
        time_embedding,
        norm_gain,
        vhw,
        weight,
        qm,
    )


COLUMNS = 256
CHUNKS = 2 * W // COLUMNS


def connect_kernel(
    scaled_ref,
    sq_ref,
    conn_hbm,
    cond_ref,
    conn,
    buf,
    land1,
    land2,
    land3,
    sqb,
    sq1,
    sq2,
    sq3,
    load_sem,
    send_sem,
    recv_sem,
):
    x, y, z, core = places()
    y_hi = y // 2
    at_ze, at_zo = device_at(x, y, z + 1 - 2 * (z % 2), core), device_at(x, y, 3 - z, core)
    at_far = device_at(x, (y + 2) % 4, z, core)
    bit_a, bit_b = gray_bits(z)
    loads = [
        pltpu.make_async_copy(
            conn_hbm.at[:, part * 512 : (part + 1) * 512], conn.at[:, part * 512 : (part + 1) * 512], load_sem.at[part]
        )
        for part in range(7)
    ]
    for copy in loads:
        copy.start()

    greet((at_ze, at_zo, at_far))

    sent = []
    flying = {}

    def send(j, phase):
        if j == CHUNKS:
            block, landing = sqb, (sq1, sq2, sq3)[phase]
        else:
            block, landing = buf.at[j], (land1, land2, land3)[phase].at[j]
        if phase == 0:
            source = block.at[:, 1 - bit_a] if j % 2 == 0 else block.at[:, :, 1 - bit_b]
        elif phase == 1:
            source = block.at[:, bit_a, 1 - bit_b] if j % 2 == 0 else block.at[:, 1 - bit_a, bit_b]
        else:
            source = block.at[1 - y_hi, bit_a, bit_b]
        copy = pltpu.make_async_remote_copy(
            src_ref=source,
            dst_ref=landing,
            send_sem=send_sem.at[j, phase],
            recv_sem=recv_sem.at[j, phase],
            device_id=at_far if phase == 2 else at_ze if phase == j % 2 else at_zo,
            device_id_type=MESH,
        )
        copy.start()
        sent.append(copy)
        flying[j] = copy

    def settle(j, phase):
        flying[j].wait_recv()
        if phase == 0:
            index = (slice(None), bit_a) if j % 2 == 0 else (slice(None), slice(None), bit_b)
        else:
            index = (slice(None), bit_a, bit_b)
        if j == CHUNKS:
            sqb[index] = sqb[index] + (sq1, sq2)[phase][...]
        else:
            index = (j,) + index
            total = buf[index].astype(F32) + (land1, land2)[phase][j].astype(F32)
            buf[index] = total.astype(BF16)
        send(j, phase + 1)

    def spread(block, value):
        for m in range(8):
            a, b = gray_bits(m % 4)
            block[m // 4, a, b] = value[m * NQ : (m + 1) * NQ]

    chunks = [CHUNKS] + list(range(CHUNKS))
    for n in range(CHUNKS + 1 + 10):
        if n == 0:
            spread(sqb, sq_ref[...])
            send(CHUNKS, 0)
        elif n <= CHUNKS:
            j = chunks[n]
            if j % 2 == 0:
                loads[j // 2].wait()
            value = nn_dot(scaled_ref[...], conn[:, j * COLUMNS : (j + 1) * COLUMNS])
            spread(buf.at[j], value.astype(BF16))
            send(j, 0)
        if 0 <= n - 6 <= CHUNKS:
            settle(chunks[n - 6], 0)
        if 0 <= n - 10 <= CHUNKS:
            settle(chunks[n - 10], 1)
    flying[CHUNKS].wait_recv()
    squares = sqb[y_hi, bit_a, bit_b] + sq3[...]
    factor = lax.rsqrt(jnp.sum(squares, -1, keepdims=True) / D + eps)
    for j in range(CHUNKS):
        flying[j].wait_recv()
        total = buf[j, y_hi, bit_a, bit_b].astype(F32) + land3[j].astype(F32)
        cond_ref[:, j * COLUMNS : (j + 1) * COLUMNS] = (total * factor).astype(BF16)
    for copy in sent:
        copy.wait_send()


def connected(scaled, squares, conn_weight):
    vmem = pl.BlockSpec(memory_space=pltpu.VMEM)
    return pl.pallas_call(
        connect_kernel,
        out_shape=jax.ShapeDtypeStruct((NQ, 2 * W), BF16),
        in_specs=[vmem, vmem, pl.BlockSpec(memory_space=pl.ANY)],
        out_specs=vmem,
        scratch_shapes=[
            pltpu.VMEM(conn_weight.shape, BF16),
            pltpu.VMEM((CHUNKS, 2, 2, 2, NQ, COLUMNS), BF16),
            pltpu.VMEM((CHUNKS, 2, 2, NQ, COLUMNS), BF16),
            pltpu.VMEM((CHUNKS, 2, NQ, COLUMNS), BF16),
            pltpu.VMEM((CHUNKS, NQ, COLUMNS), BF16),
            pltpu.VMEM((2, 2, 2, NQ, 128), F32),
            pltpu.VMEM((2, 2, NQ, 128), F32),
            pltpu.VMEM((2, NQ, 128), F32),
            pltpu.VMEM((NQ, 128), F32),
            pltpu.SemaphoreType.DMA((7,)),
            pltpu.SemaphoreType.DMA((CHUNKS + 1, 3)),
            pltpu.SemaphoreType.DMA((CHUNKS + 1, 3)),
        ],
        compiler_params=pltpu.CompilerParams(
            collective_id=3, has_side_effects=True, vmem_limit_bytes=58 << 20
        ),
        name="connect",
    )(scaled, squares, conn_weight)


def on_device(
    prompt_keys,
    prompt_values,
    query_states,
    query_keys,
    query_values,
    lengths,
    residual,
    out_weight,
    final_gain,
    conn_weight,
    owner,
    latents,
    noise,
    timesteps,
    patch_weight,
    time_embedding,
    image_norm_gain,
    query_matrix,
    velocity_head_weight,
):
    count_of_rows = lax.axis_size("dp") * lax.axis_size("tensor") * latents.shape[1]
    scaled, squares, hv, q, normed_t = projected(
        owner,
        lengths,
        timesteps,
        query_states,
        prompt_keys,
        prompt_values,
        query_keys,
        query_values,
        residual,
        final_gain,
        latents[0],
        noise[0],
        patch_weight,
        time_embedding,
        image_norm_gain,
        velocity_head_weight,
        out_weight,
        query_matrix,
    )
    cond = connected(scaled, squares, conn_weight)
    velocity, dq = step(
        q, hv, latents[0], noise[0], cond, velocity_head_weight, grad_gain / math.sqrt(count_of_rows)
    )
    return (velocity[None], summed_gradient(normed_t, dq))


def solution(mesh):
    return jax.shard_map(
        on_device,
        mesh=mesh,
        in_specs=(
            P("dp", None, "tensor"),
            P("dp", None, "tensor"),
            P("dp", None, "tensor"),
            P("dp", None, "tensor"),
            P("dp", None, "tensor"),
            P("dp"),
            P("dp", None, "tensor"),
            P("tensor", "dp"),
            P("tensor"),
            P("tensor", None),
            P("dp", None),
            P(("dp", "tensor"), None, None),
            P(("dp", "tensor"), None, None),
            P(("dp", "tensor")),
            P(),
            P(),
            P(),
            P(),
            P(),
        ),
        out_specs=(P(("dp", "tensor"), None, None), P(("dp", "tensor"), None)),
        check_vma=False,
    )
```

```python
import math

import jax
import jax.numpy as jnp
from jax import lax
from jax.experimental import pallas as pl
from jax.experimental.pallas import tpu as pltpu
from jax.sharding import PartitionSpec as P

D = 8192
HEAD = 128
NQ = 64
DHEAD = 112
NT = 1000
W = 1792
IMG_HEADS = 16
F32 = jnp.float32
BF16 = jnp.bfloat16
MESH = pl.DeviceIdType.MESH

eps = 1e-06
grad_gain = 16.0

ROWS_BLOCK = 14
ROWS_PAD = 16
PIECES = (384, 384, 256, 256, 256, 256)
STARTS = (0, 384, 768, 1024, 1280, 1536)
KEY_WINDOWS = (0, 384, 896, 1280)
SCORE_WINDOWS = (0, 128, 256, 384, 512, 640, 768)


def nt_dot(a, b):
    return lax.dot_general(a, b, (((1,), (1,)), ((), ())), preferred_element_type=F32)


def nn_dot(a, b):
    return jnp.dot(a, b, preferred_element_type=F32)


def head_mask(rows, width, head, base):
    lane = lax.broadcasted_iota(jnp.int32, (rows, width), 1) + base
    return (lane >= head * DHEAD) & (lane < (head + 1) * DHEAD)


def only_head(block, head, base):
    return jnp.where(head_mask(*block.shape, head, base), block.astype(F32), 0.0).astype(BF16)


def places():
    dp, tensor = lax.axis_index("dp"), lax.axis_index("tensor")
    return dp // 4, (tensor // 4) * 2 + (dp // 2) % 2, tensor % 4, dp % 2


def device_at(x, y, z, core):
    return (x * 4 + (y % 2) * 2 + core, (y // 2) * 4 + z)


def link_partners(x, y, z, core):
    pair = lambda i: i + 1 - 2 * (i % 2)
    other = lambda i: 3 - i
    return (
        device_at(pair(x), y, z, core),
        device_at(other(x), y, z, core),
        device_at(x, pair(y), z, core),
        device_at(x, other(y), z, core),
        device_at(x, y, pair(z), core),
        device_at(x, y, other(z), core),
    )


def gray_bits(i):
    return (i + i // 2) % 2, i // 2


def attend(m, owner_ref, len_ref, q_ref, pk_ref, pv_ref, ok_ref, ov_ref, att):
    prompt = owner_ref[0, m]
    length = len_ref[prompt]
    scale = 1.0 / HEAD**0.5
    own_k, own_v = ok_ref[prompt], ov_ref[prompt]
    keys, values = pk_ref[prompt], pv_ref[prompt]
    states = q_ref[prompt]
    heads = states.shape[1] // HEAD
    rows = jnp.concatenate([states[:, j * HEAD : (j + 1) * HEAD] for j in range(heads)], 0)
    first = nt_dot(rows, keys) * scale
    second = nt_dot(rows, own_k) * scale
    column = lax.broadcasted_iota(jnp.int32, first.shape, 1)
    first = jnp.where(column < length, first, -jnp.inf)
    row = lax.broadcasted_iota(jnp.int32, second.shape, 0) % NQ
    column = lax.broadcasted_iota(jnp.int32, second.shape, 1)
    second = jnp.where(column <= row, second, -jnp.inf)
    top = jnp.maximum(jnp.max(first, -1, keepdims=True), jnp.max(second, -1, keepdims=True))
    first, second = jnp.exp(first - top), jnp.exp(second - top)
    total = jnp.sum(first, -1, keepdims=True) + jnp.sum(second, -1, keepdims=True)
    out = nn_dot(first.astype(BF16), values) + nn_dot(second.astype(BF16), own_v)
    out = (out / total).astype(BF16)
    rows_at = pl.ds(pl.multiple_of(m * NQ, NQ), NQ)
    for j in range(heads):
        att[rows_at, j * HEAD : (j + 1) * HEAD] = out[j * NQ : (j + 1) * NQ]


def greet(devices):
    barrier = pltpu.get_barrier_semaphore()
    for device in devices:
        pl.semaphore_signal(barrier, inc=1, device_id=device, device_id_type=MESH)
    pl.semaphore_wait(barrier, len(devices))


TOKENS = 256
GRAD_ROWS = 2048


def one_hot_rows(start, rows):
    row = lax.broadcasted_iota(jnp.int32, (rows, 1), 0) + start
    bit = lambda n: row // (ROWS_PAD << n) % 2
    at = lambda n: 2 * bit(n) + (bit(n) + bit(n + 1)) % 2
    z, y, x, core = at(0), at(2), at(4), bit(6)
    natural = ((x * 2 + y % 2) * 2 + core) * 8 + y // 2 * 4 + z
    inside = row % ROWS_PAD
    source = jnp.where(inside < ROWS_BLOCK, natural * ROWS_BLOCK + inside, -1)
    lane = lax.broadcasted_iota(jnp.int32, (rows, W), 1)
    return jnp.where(lane == source, 1.0, 0.0).astype(BF16)


def split_in_three(value):
    parts = []
    for _ in range(3):
        part = value.astype(BF16)
        parts.append(part)
        value = value - part.astype(F32)
    return parts


def project_kernel(
    owner_ref,
    len_ref,
    step_ref,
    q_ref,
    pk_ref,
    pv_ref,
    ok_ref,
    ov_ref,
    res_ref,
    gain_ref,
    lat_ref,
    noise_ref,
    pw_ref,
    time_ref,
    norm_ref,
    vhw_ref,
    w_hbm,
    qm_hbm,
    scaled_ref,
    sq_ref,
    hv_ref,
    q_hbm,
    nt_hbm,
    att,
    wg,
    terms,
    land_first,
    land_second,
    zsum,
    relay,
    landy,
    qm,
    packed,
    pwt,
    col,
    q_out,
    nt_out,
    own_sem,
    qm_sem,
    out_sem,
    w_send,
    w_recv,
    r_send,
    r_recv,
    y_send,
    y_recv,
):
    x, y, z, core = places()
    y_lo, y_hi = y % 2, y // 2
    xp, xo, xf = x + 1 - 2 * (x % 2), 3 - x, (x + 2) % 4
    at_y = device_at(x, y + 1 - 2 * y_lo, z, core)
    at_xp, at_xo = device_at(xp, y, z, core), device_at(xo, y, z, core)
    at_ze, at_zo = device_at(x, y, z + 1 - 2 * (z % 2), core), device_at(x, y, 3 - z, core)
    at_yo = device_at(x, 3 - y, z, core)
    at_sib = device_at(x, y, z, 1 - core)
    bit_b = z // 2
    shared = []

    keep = [
        pltpu.make_async_copy(w_hbm.at[:, h * 256 : (h + 1) * 256], wg.at[x, y_lo, core, h], own_sem.at[h])
        for h in range(2)
    ]
    load_qm = pltpu.make_async_copy(qm_hbm, qm, qm_sem.at[0])
    for copy in keep + [load_qm]:
        copy.start()
    greet((at_y, at_yo, at_xp, at_xo, at_ze, at_zo, at_sib))

    def share(xs, ys, h, *targets):
        slot = wg.at[xs, ys, core, h]
        for target in targets:
            copy = pltpu.make_async_remote_copy(
                src_ref=slot,
                dst_ref=slot,
                send_sem=w_send.at[len(shared)],
                recv_sem=w_recv.at[xs, ys, core, h],
                device_id=target,
                device_id_type=MESH,
            )
            copy.start()
            shared.append(copy)

    def arrived(xs, ys, cs, h):
        slot = wg.at[xs, ys, cs, h]
        pltpu.make_async_remote_copy(
            src_ref=slot,
            dst_ref=slot,
            send_sem=w_send.at[0],
            recv_sem=w_recv.at[xs, ys, cs, h],
            device_id=at_sib,
            device_id_type=MESH,
        ).wait_recv()

    def pass_on(xs, ys, h, *targets):
        arrived(xs, ys, core, h)
        share(xs, ys, h, *targets)

    def prepare():
        packed[0:128, :] = pw_ref[...]
        parts = split_in_three(time_ref[...].reshape(1, W)) + split_in_three(norm_ref[...].reshape(1, W))
        packed[128:256, :] = jnp.concatenate(parts + [jnp.zeros((122, W), BF16)], 0)

        def body(i, carry):
            rows = pl.ds(pl.multiple_of(i * 256, 256), 256)
            value = nt_dot(one_hot_rows(i * 256, 256), packed[...])
            pwt[rows, :] = value[:, :128].astype(BF16)
            col[rows, :] = value[:, 128:]
            return carry

        lax.fori_loop(0, GRAD_ROWS // 256, body, 0)

    def prelude(c):
        t = (step_ref[0].astype(F32) + 0.5) / NT
        rows = pl.ds(c * TOKENS, TOKENS)
        noisy = ((1.0 - t) * lat_ref[rows, :].astype(F32) + t * noise_ref[rows, :].astype(F32)).astype(BF16)
        hidden = nn_dot(noisy, pw_ref[...]) + t * time_ref[...].reshape(1, W)
        scale = lax.rsqrt(jnp.mean(hidden * hidden, -1, keepdims=True) + eps)
        normed = (hidden * scale * norm_ref[...].reshape(1, W)).astype(BF16)
        hv_ref[rows, :] = nn_dot(hidden.astype(BF16), vhw_ref[...])
        q_out[...] = nn_dot(normed, qm[...]).astype(BF16)
        time_col = col[:, 0:1] + col[:, 1:2] + col[:, 2:3]
        norm_col = col[:, 3:4] + col[:, 4:5] + col[:, 5:6]
        ht = nt_dot(pwt[...], noisy) + t * time_col
        scale_t = lax.rsqrt(jnp.sum(ht * ht, 0, keepdims=True) / W + eps)
        nt_out[...] = (ht * scale_t * norm_col).astype(BF16)
        copies = (
            pltpu.make_async_copy(q_out, q_hbm.at[c * TOKENS : (c + 1) * TOKENS, :], out_sem.at[c, 0]),
            pltpu.make_async_copy(nt_out, nt_hbm.at[:, c * TOKENS : (c + 1) * TOKENS], out_sem.at[c, 1]),
        )
        for copy in copies:
            copy.start()
        return copies

    def prompts(start, end):
        def body(m, carry):
            attend(m, owner_ref, len_ref, q_ref, pk_ref, pv_ref, ok_ref, ov_ref, att)
            return carry

        lax.fori_loop(start, end, body, 0)

    first_chip = (x // 2, 1 - x // 2)
    chips = ((x, xp), (xo, xf))
    subs = ((core, 0), (1 - core, 0), (core, 1), (1 - core, 1))
    mine = bit_b

    def row_of(batch):
        return y_lo if batch < 2 else 1 - y_lo

    def passing(batch):
        return batch % 2

    def at_end(batch):
        return z % 2 == row_of(batch)

    def between(batch):
        return z % 2 != row_of(batch)

    def remote(s, which, source, landing, device):
        return pltpu.make_async_remote_copy(
            src_ref=source,
            dst_ref=landing,
            send_sem=r_send.at[s, which],
            recv_sem=r_recv.at[s, which],
            device_id=device,
            device_id_type=MESH,
        )

    def out_block(s):
        return (mine + z + row_of(s // 4) + 1) % 2

    def first(s, part):
        block = out_block(s) if part == 0 else 1 - mine
        return remote(s, part, terms.at[s, part, block], land_first.at[s, part], at_ze if part == 0 else at_zo)

    def second(s, part):
        block = 1 - mine if part == 0 else mine
        landing = land_second.at[passing(s // 4), s % 4, part]
        return remote(s, 2 + part, terms.at[s, part, block], landing, at_zo if part == 0 else at_ze)

    def multiply(s):
        batch = s // 4
        cs, h = subs[s % 4]

        def body(u, carry):
            value = nn_dot(att[...], wg[2 * first_chip[passing(batch)] + u, row_of(batch), cs, h]).astype(BF16)
            terms[s, 0, u] = value[:256]
            terms[s, 1, u] = value[256:]
            return carry

        lax.fori_loop(0, 2, body, 0)
        for part in range(2):
            first(s, part).start()

    def halve(s):
        for part in range(2):
            first(s, part).wait_recv()
            block = 1 - out_block(s) if part == 0 else mine
            total = terms[s, part, block].astype(F32) + land_first[s, part].astype(F32)
            terms[s, part, block] = total.astype(BF16)

        @pl.when(between(s // 4))
        def _():
            for part in range(2):
                second(s, part).start()

    def finish(s):
        batch = s // 4

        @pl.when(at_end(batch))
        def _():
            for part in range(2):
                second(s, part).wait_recv()
                landing = land_second[passing(batch), s % 4, part]
                total = terms[s, part, mine].astype(F32) + landing.astype(F32)
                zsum[passing(batch), s % 4, part * 256 : (part + 1) * 256] = total.astype(BF16)

    kept = (x // 2 + y_hi) % 2

    def across(i, leg):
        part = leg % 2
        if leg < 2:
            source, landing = zsum.at[1 - kept, i, part * 256 : (part + 1) * 256], relay.at[i, part]
        else:
            source, landing = relay.at[i, part], landy.at[i, part]
        return pltpu.make_async_remote_copy(
            src_ref=source,
            dst_ref=landing,
            send_sem=y_send.at[i, leg],
            recv_sem=y_recv.at[i, leg],
            device_id=at_y if leg in (0, 3) else at_yo,
            device_id_type=MESH,
        )

    def cross(i):
        across(i, 0).start()
        across(i, 1).start()

    def relay_on(i):
        for part in range(2):
            across(i, part).wait_recv()
            across(i, 2 + part).start()

    def close(i):
        for part in range(2):
            across(i, 2 + part).wait_recv()
        cs, h = subs[i]
        columns = pl.ds(pl.multiple_of(cs * 512 + h * 256, 256), 256)
        gain = gain_ref[:, columns]

        def body(m, carry):
            rows = pl.ds(pl.multiple_of(m * NQ, NQ), NQ)
            part, inside = m // 4, pl.ds(pl.multiple_of(m % 4 * NQ, NQ), NQ)
            value = res_ref[owner_ref[0, m], :, columns].astype(F32)
            value = value + (zsum[kept, i, rows, :].astype(F32) + landy[i, part, inside, :].astype(F32))
            scaled_ref[rows, columns] = (value * gain).astype(BF16)
            square = value * value
            square = square[:, :128] + square[:, 128:]
            sq_ref[rows, :] = square if i == 0 else sq_ref[rows, :] + square
            return carry

        lax.fori_loop(0, 8, body, 0)

    def steps(batch, h):
        for s in (4 * batch + 2 * h, 4 * batch + 2 * h + 1):
            if s % 2 == 1:
                for xs in chips[passing(batch)]:
                    arrived(xs, row_of(batch), 1 - core, h)
            multiply(s)

    def each(do, *numbers):
        for s in numbers:
            do(s)

    keep[0].wait()
    share(x, y_lo, 0, at_xp, at_xo, at_y, at_sib)
    prompts(0, 4)
    keep[1].wait()
    pass_on(xo, y_lo, 0, at_xp)
    share(x, y_lo, 1, at_xo, at_y)
    share(xo, y_lo, 0, at_sib)
    pass_on(xp, y_lo, 0, at_sib)
    share(x, y_lo, 1, at_sib)
    prompts(4, 8)
    steps(0, 0)
    pass_on(x, 1 - y_lo, 0, at_sib)
    prepare()
    load_qm.wait()
    stores = prelude(0)
    each(halve, 0, 1)

    pass_on(xo, y_lo, 1)
    share(x, y_lo, 1, at_xp)
    share(x, 1 - y_lo, 0, at_xo)
    pass_on(xf, y_lo, 0, at_y, at_sib)
    share(xo, y_lo, 1, at_sib)
    pass_on(x, 1 - y_lo, 1, at_sib)
    steps(1, 0)
    for copy in stores:
        copy.wait()
    stores = prelude(1)
    each(halve, 4, 5)
    each(finish, 0, 1)

    pass_on(xp, y_lo, 1, at_xo)
    share(x, 1 - y_lo, 0, at_xp)
    share(xp, y_lo, 1, at_sib)
    pass_on(xo, 1 - y_lo, 0, at_sib)
    steps(0, 1)
    pass_on(xf, 1 - y_lo, 0, at_sib)
    steps(3, 0)
    for copy in stores:
        copy.wait()
    stores = prelude(2)
    each(halve, 2, 3)
    each(finish, 4, 5)

    pass_on(xf, y_lo, 1, at_y)
    share(x, 1 - y_lo, 1, at_xp, at_xo)
    share(xf, y_lo, 1, at_sib)
    pass_on(xp, 1 - y_lo, 0, at_sib)
    steps(2, 0)
    steps(1, 1)
    each(halve, 12, 13)
    for copy in stores:
        copy.wait()
    stores = prelude(3)
    each(halve, 8, 9)
    each(finish, 2, 3)

    pass_on(xp, 1 - y_lo, 1, at_sib)
    steps(2, 1)
    pass_on(xo, 1 - y_lo, 1, at_sib)
    pass_on(xf, 1 - y_lo, 1, at_sib)
    steps(3, 1)
    each(halve, 6, 7)
    each(finish, 12, 8)
    cross(0)
    each(finish, 13, 9)
    cross(1)
    each(halve, 10, 11)
    relay_on(0)
    each(halve, 14, 15)
    relay_on(1)
    each(finish, 6, 10, 14)
    cross(2)
    each(finish, 7, 11, 15)
    cross(3)
    close(0)
    close(1)
    relay_on(2)
    relay_on(3)
    close(2)
    close(3)
    for copy in stores:
        copy.wait()
    for copy in shared:
        copy.wait_send()
    for s in range(16):
        for part in range(2):
            first(s, part).wait_send()

        @pl.when(between(s // 4))
        def _():
            for part in range(2):
                second(s, part).wait_send()

    for i in range(4):
        for leg in range(4):
            across(i, leg).wait_send()


def projected(
    owner,
    lengths,
    timesteps,
    query_states,
    prompt_keys,
    prompt_values,
    query_keys,
    query_values,
    residual,
    gain,
    latents,
    noise,
    patch_weight,
    time_embedding,
    norm_gain,
    vhw,
    weight,
    qm,
):
    rows = query_states.shape[0] * NQ
    tokens = latents.shape[0]
    vmem, smem = pl.BlockSpec(memory_space=pltpu.VMEM), pl.BlockSpec(memory_space=pltpu.SMEM)
    anywhere = pl.BlockSpec(memory_space=pl.ANY)
    return pl.pallas_call(
        project_kernel,
        out_shape=[
            jax.ShapeDtypeStruct((rows, 1024), BF16),
            jax.ShapeDtypeStruct((rows, 128), F32),
            jax.ShapeDtypeStruct((tokens, 128), F32),
            jax.ShapeDtypeStruct((tokens, W), BF16),
            jax.ShapeDtypeStruct((GRAD_ROWS, tokens), BF16),
        ],
        in_specs=[smem] * 3 + [vmem] * 13 + [anywhere] * 2,
        out_specs=[vmem] * 3 + [anywhere] * 2,
        scratch_shapes=[
            pltpu.VMEM((rows, 1024), BF16),
            pltpu.VMEM((4, 2, 2, 2, 1024, 256), BF16),
            pltpu.VMEM((16, 2, 2, 256, 256), BF16),
            pltpu.VMEM((16, 2, 256, 256), BF16),
            pltpu.VMEM((2, 4, 2, 256, 256), BF16),
            pltpu.VMEM((2, 4, rows, 256), BF16),
            pltpu.VMEM((4, 2, 256, 256), BF16),
            pltpu.VMEM((4, 2, 256, 256), BF16),
            pltpu.VMEM(qm.shape, BF16),
            pltpu.VMEM((256, W), BF16),
            pltpu.VMEM((GRAD_ROWS, 128), BF16),
            pltpu.VMEM((GRAD_ROWS, 128), F32),
            pltpu.VMEM((TOKENS, W), BF16),
            pltpu.VMEM((GRAD_ROWS, TOKENS), BF16),
            pltpu.SemaphoreType.DMA((2,)),
            pltpu.SemaphoreType.DMA((1,)),
            pltpu.SemaphoreType.DMA((4, 2)),
            pltpu.SemaphoreType.DMA((32,)),
            pltpu.SemaphoreType.DMA((4, 2, 2, 2)),
            pltpu.SemaphoreType.DMA((16, 4)),
            pltpu.SemaphoreType.DMA((16, 4)),
            pltpu.SemaphoreType.DMA((4, 4)),
            pltpu.SemaphoreType.DMA((4, 4)),
        ],
        compiler_params=pltpu.CompilerParams(
            collective_id=2, has_side_effects=True, vmem_limit_bytes=62 << 20
        ),
        name="attend_project",
    )(
        owner,
        lengths,
        timesteps,
        query_states,
        prompt_keys,
        prompt_values,
        query_keys,
        query_values,
        residual,
        gain.reshape(1, -1),
        latents,
        noise,
        patch_weight,
        time_embedding,
        norm_gain,
        vhw,
        weight,
        qm,
    )


COLUMNS = 256
CHUNKS = 2 * W // COLUMNS


def finish_kernel(
    gain,
    scaled_ref,
    sq_ref,
    hv_ref,
    lat_ref,
    noise_ref,
    vhw_ref,
    conn_hbm,
    q_hbm,
    nt_hbm,
    vel_ref,
    out_ref,
    conn,
    q,
    nt,
    buf,
    land1,
    land2,
    land3,
    sqb,
    sq1,
    sq2,
    sq3,
    cond,
    kbd,
    kflat,
    vw,
    ones,
    probs,
    dsc,
    dq,
    load_sem,
    send_sem,
    recv_sem,
    core_send,
    core_recv,
    g_send,
    g_recv,
    *pieces,
):
    mine, away, sibling_part = pieces[0:6], pieces[6:12], pieces[12:18]
    landing = [pieces[18 + 6 * p : 24 + 6 * p] for p in range(6)]
    x, y, z, core = places()
    y_hi = y // 2
    partners = link_partners(x, y, z, core)
    at_ze, at_zo = partners[4], partners[5]
    at_far = device_at(x, (y + 2) % 4, z, core)
    sibling = device_at(x, y, z, 1 - core)
    bits = gray_bits(x) + gray_bits(y) + gray_bits(z)
    bit_a, bit_b = gray_bits(z)
    loads = [
        pltpu.make_async_copy(
            conn_hbm.at[:, part * 512 : (part + 1) * 512], conn.at[:, part * 512 : (part + 1) * 512], load_sem.at[part]
        )
        for part in range(7)
    ]
    loads.append(pltpu.make_async_copy(q_hbm, q, load_sem.at[7]))
    loads.append(pltpu.make_async_copy(nt_hbm, nt, load_sem.at[8]))
    for copy in loads:
        copy.start()
    greet(partners + (at_far, sibling))

    sent = []
    flying = {}

    def send(j, phase):
        if j == CHUNKS:
            block, target = sqb, (sq1, sq2, sq3)[phase]
        else:
            block, target = buf.at[j], (land1, land2, land3)[phase].at[j]
        if phase == 0:
            source = block.at[:, 1 - bit_a] if j % 2 == 0 else block.at[:, :, 1 - bit_b]
        elif phase == 1:
            source = block.at[:, bit_a, 1 - bit_b] if j % 2 == 0 else block.at[:, 1 - bit_a, bit_b]
        else:
            source = block.at[1 - y_hi, bit_a, bit_b]
        copy = pltpu.make_async_remote_copy(
            src_ref=source,
            dst_ref=target,
            send_sem=send_sem.at[j, phase],
            recv_sem=recv_sem.at[j, phase],
            device_id=at_far if phase == 2 else at_ze if phase == j % 2 else at_zo,
            device_id_type=MESH,
        )
        copy.start()
        sent.append(copy)
        flying[j] = copy

    def settle(j, phase):
        flying[j].wait_recv()
        if phase == 0:
            index = (slice(None), bit_a) if j % 2 == 0 else (slice(None), slice(None), bit_b)
        else:
            index = (slice(None), bit_a, bit_b)
        if j == CHUNKS:
            sqb[index] = sqb[index] + (sq1, sq2)[phase][...]
        else:
            index = (j,) + index
            total = buf[index].astype(F32) + (land1, land2)[phase][j].astype(F32)
            buf[index] = total.astype(BF16)
        send(j, phase + 1)

    def spread(block, value):
        for m in range(8):
            a, b = gray_bits(m % 4)
            block[m // 4, a, b] = value[m * NQ : (m + 1) * NQ]

    def condition(j, factor):
        flying[j].wait_recv()
        total = buf[j, y_hi, bit_a, bit_b].astype(F32) + land3[j].astype(F32)
        cond[:, j * COLUMNS : (j + 1) * COLUMNS] = (total * factor).astype(BF16)

    def norm_factor():
        flying[CHUNKS].wait_recv()
        squares = sqb[y_hi, bit_a, bit_b] + sq3[...]
        return lax.rsqrt(jnp.sum(squares, -1, keepdims=True) / D + eps)

    scale = 1.0 / DHEAD**0.5

    def place_keys():
        for g, base in enumerate(KEY_WINDOWS):
            for n in range(4):
                window = cond[:, base : base + 512]
                kbd[g, n * NQ : (n + 1) * NQ, :] = only_head(window, 4 * g + n, base)
        for tile, first in enumerate(SCORE_WINDOWS):
            for n in range(4):
                window = cond[:, tile * 256 : (tile + 1) * 256]
                kflat[tile, n * NQ : (n + 1) * NQ, :] = only_head(window, first // NQ + n, tile * 256)
        row = lax.broadcasted_iota(jnp.int32, (256, 256), 0) // NQ
        column = lax.broadcasted_iota(jnp.int32, (256, 256), 1) // NQ
        ones[...] = jnp.where(row == column, 1.0, 0.0).astype(BF16)

    def place_values():
        for g, base in enumerate(KEY_WINDOWS):
            window = cond[:, W + base : W + base + 512]
            vals = [only_head(window, 4 * g + n, base) for n in range(4)]
            vw[g] = nn_dot(jnp.concatenate(vals, 0), vhw_ref[base : base + 512, :]).astype(BF16)

    def softmax(c):
        rows = pl.ds(c * TOKENS, TOKENS)
        for g, base in enumerate(KEY_WINDOWS):
            expo = jnp.exp(nt_dot(q[rows, base : base + 512], kbd[g]) * scale)
            total = nn_dot(jnp.minimum(expo, 3.38e38).astype(BF16), ones[...])
            probs[rows, g * 256 : (g + 1) * 256] = expo / total

    def scores_back(c, carry):
        rows = pl.ds(pl.multiple_of(c * TOKENS, TOKENS), TOKENS)
        velocity = hv_ref[rows, :]
        for g in range(4):
            velocity = velocity + nn_dot(probs[rows, g * 256 : (g + 1) * 256].astype(BF16), vw[g])
        vel_ref[rows, :] = velocity
        target = noise_ref[rows, :].astype(F32) - lat_ref[rows, :].astype(F32)
        dvel = ((velocity - target) * gain).astype(BF16)
        for g in range(4):
            p = probs[rows, g * 256 : (g + 1) * 256]
            dprob = nt_dot(dvel, vw[g])
            both = p * dprob
            high = both.astype(BF16)
            low = (both - high.astype(F32)).astype(BF16)
            shift = nn_dot(high, ones[...]) + nn_dot(low, ones[...])
            dsc[:, g * 256 : (g + 1) * 256] = (p * (dprob - shift) * scale).astype(BF16)
        for tile, first in enumerate(SCORE_WINDOWS):
            dq[rows, tile * 256 : (tile + 1) * 256] = nn_dot(dsc[:, first : first + 256], kflat[tile]).astype(BF16)
        return carry

    def product(p, which, target):
        columns = pl.ds(STARTS[p], PIECES[p])

        def part(i, carry):
            rows = nt[pl.ds(pl.multiple_of(which * 1024 + i * 512, 512), 512), :]
            value = nn_dot(rows, dq[:, columns]).astype(BF16)
            target[i] = value.reshape(2, 2, 2, 2, 2, ROWS_PAD, PIECES[p])
            return carry

        lax.fori_loop(0, 2, part, 0)

    def region(p, k, bit):
        index = []
        for dim in range(6):
            age = (dim - p) % 6
            index.append(bits[dim] if age < k else bit if age == k else slice(None))
        return tuple(index)

    def to_sibling(p):
        return pltpu.make_async_remote_copy(
            src_ref=away[p],
            dst_ref=sibling_part[p],
            send_sem=core_send.at[p],
            recv_sem=core_recv.at[p],
            device_id=sibling,
            device_id_type=MESH,
        )

    def exchange(p, k):
        dim = (p + k) % 6
        return pltpu.make_async_remote_copy(
            src_ref=mine[p].at[region(p, k, 1 - bits[dim])],
            dst_ref=landing[p][k],
            send_sem=g_send.at[p, k],
            recv_sem=g_recv.at[p, k],
            device_id=partners[dim],
            device_id_type=MESH,
        )

    def launch(p, copy):
        copy.start()
        flying["grad", p] = copy
        sent.append(copy)

    def accumulate(p, k):
        flying["grad", p].wait_recv()
        if k == 0:
            index = (slice(None),) * 6
            arrived = sibling_part[p]
        else:
            index = region(p, k - 1, bits[(p + k - 1) % 6])
            arrived = landing[p][k - 1]
        total = mine[p][index].astype(F32) + arrived[...].astype(F32)
        if k == 6:
            out_ref[:, STARTS[p] : STARTS[p] + PIECES[p]] = total
        else:
            mine[p][index] = total.astype(BF16)
            launch(p, exchange(p, k))

    chunks = [CHUNKS] + list(range(CHUNKS))
    for n in range(CHUNKS + 1 + 10):
        if n == 0:
            spread(sqb, sq_ref[...])
            send(CHUNKS, 0)
        elif n <= CHUNKS:
            j = chunks[n]
            if j % 2 == 0:
                loads[j // 2].wait()
            value = nn_dot(scaled_ref[...], conn[:, j * COLUMNS : (j + 1) * COLUMNS])
            spread(buf.at[j], value.astype(BF16))
            send(j, 0)
        if 0 <= n - 6 <= CHUNKS:
            settle(chunks[n - 6], 0)
        if 0 <= n - 10 <= CHUNKS:
            settle(chunks[n - 10], 1)
        if n == 19:
            factor = norm_factor()
            for j in range(7):
                condition(j, factor)
            place_keys()
            loads[7].wait()
        if 20 <= n < 24:
            softmax(n - 20)
    for j in range(7, CHUNKS):
        condition(j, factor)
    place_values()
    lax.fori_loop(0, 4, scores_back, 0)
    loads[8].wait()
    for p in range(7):
        if p < 6:
            product(p, 1 - core, away[p])
            launch(p, to_sibling(p))
            product(p, core, mine[p])
        if p > 0:
            accumulate(p - 1, 0)
    for k in range(1, 7):
        for p in range(6):
            accumulate(p, k)
    for copy in sent:
        copy.wait_send()


def finished(scaled, squares, hv, latents, noise, vhw, conn_weight, q, normed_t, gain):
    tokens = latents.shape[0]
    vmem, anywhere = pl.BlockSpec(memory_space=pltpu.VMEM), pl.BlockSpec(memory_space=pl.ANY)
    full = [pltpu.VMEM((2,) * 6 + (ROWS_PAD, c), BF16) for c in PIECES]
    parts = [pltpu.VMEM((2,) * (5 - k) + (ROWS_PAD, c), BF16) for c in PIECES for k in range(6)]
    velocity, out = pl.pallas_call(
        lambda *refs: finish_kernel(gain, *refs),
        out_shape=[jax.ShapeDtypeStruct((tokens, 128), F32), jax.ShapeDtypeStruct((ROWS_PAD, W), F32)],
        in_specs=[vmem] * 6 + [anywhere] * 3,
        out_specs=[vmem] * 2,
        scratch_shapes=[
            pltpu.VMEM(conn_weight.shape, BF16),
            pltpu.VMEM(q.shape, BF16),
            pltpu.VMEM(normed_t.shape, BF16),
            pltpu.VMEM((CHUNKS, 2, 2, 2, NQ, COLUMNS), BF16),
            pltpu.VMEM((CHUNKS, 2, 2, NQ, COLUMNS), BF16),
            pltpu.VMEM((CHUNKS, 2, NQ, COLUMNS), BF16),
            pltpu.VMEM((CHUNKS, NQ, COLUMNS), BF16),
            pltpu.VMEM((2, 2, 2, NQ, 128), F32),
            pltpu.VMEM((2, 2, NQ, 128), F32),
            pltpu.VMEM((2, NQ, 128), F32),
            pltpu.VMEM((NQ, 128), F32),
            pltpu.VMEM((NQ, 2 * W), BF16),
            pltpu.VMEM((4, 4 * NQ, 512), BF16),
            pltpu.VMEM((7, 4 * NQ, 256), BF16),
            pltpu.VMEM((4, 4 * NQ, 128), BF16),
            pltpu.VMEM((256, 256), BF16),
            pltpu.VMEM((tokens, 1024), F32),
            pltpu.VMEM((TOKENS, 1024), BF16),
            pltpu.VMEM((tokens, W), BF16),
            pltpu.SemaphoreType.DMA((9,)),
            pltpu.SemaphoreType.DMA((CHUNKS + 1, 3)),
            pltpu.SemaphoreType.DMA((CHUNKS + 1, 3)),
            pltpu.SemaphoreType.DMA((6,)),
            pltpu.SemaphoreType.DMA((6,)),
            pltpu.SemaphoreType.DMA((6, 6)),
            pltpu.SemaphoreType.DMA((6, 6)),
        ]
        + full
        + full
        + full
        + parts,
        compiler_params=pltpu.CompilerParams(
            collective_id=3, has_side_effects=True, vmem_limit_bytes=62 << 20
        ),
        name="connect_step_grad",
    )(scaled, squares, hv, latents, noise, vhw, conn_weight, q, normed_t)
    return velocity, out[:ROWS_BLOCK]


def on_device(
    prompt_keys,
    prompt_values,
    query_states,
    query_keys,
    query_values,
    lengths,
    residual,
    out_weight,
    final_gain,
    conn_weight,
    owner,
    latents,
    noise,
    timesteps,
    patch_weight,
    time_embedding,
    image_norm_gain,
    query_matrix,
    velocity_head_weight,
):
    count_of_rows = lax.axis_size("dp") * lax.axis_size("tensor") * latents.shape[1]
    scaled, squares, hv, q, normed_t = projected(
        owner,
        lengths,
        timesteps,
        query_states,
        prompt_keys,
        prompt_values,
        query_keys,
        query_values,
        residual,
        final_gain,
        latents[0],
        noise[0],
        patch_weight,
        time_embedding,
        image_norm_gain,
        velocity_head_weight,
        out_weight,
        query_matrix,
    )
    velocity, query_grad = finished(
        scaled,
        squares,
        hv,
        latents[0],
        noise[0],
        velocity_head_weight,
        conn_weight,
        q,
        normed_t,
        grad_gain / math.sqrt(count_of_rows),
    )
    return (velocity[None], query_grad)


def solution(mesh):
    return jax.shard_map(
        on_device,
        mesh=mesh,
        in_specs=(
            P("dp", None, "tensor"),
            P("dp", None, "tensor"),
            P("dp", None, "tensor"),
            P("dp", None, "tensor"),
            P("dp", None, "tensor"),
            P("dp"),
            P("dp", None, "tensor"),
            P("tensor", "dp"),
            P("tensor"),
            P("tensor", None),
            P("dp", None),
            P(("dp", "tensor"), None, None),
            P(("dp", "tensor"), None, None),
            P(("dp", "tensor")),
            P(),
            P(),
            P(),
            P(),
            P(),
        ),
        out_specs=(P(("dp", "tensor"), None, None), P(("dp", "tensor"), None)),
        check_vma=False,
    )
```

```python
import math

import jax
import jax.numpy as jnp
from jax import lax
from jax.experimental import pallas as pl
from jax.experimental.pallas import tpu as pltpu
from jax.sharding import PartitionSpec as P

D = 8192
HEAD = 128
NQ = 64
DHEAD = 112
NT = 1000
W = 1792
IMG_HEADS = 16
F32 = jnp.float32
BF16 = jnp.bfloat16
MESH = pl.DeviceIdType.MESH

eps = 1e-06
grad_gain = 16.0

ROWS_BLOCK = 14
ROWS_PAD = 16
PIECES = (384, 384, 256, 256, 256, 256)
STARTS = (0, 384, 768, 1024, 1280, 1536)
KEY_WINDOWS = (0, 384, 896, 1280)
SCORE_WINDOWS = (0, 128, 256, 384, 512, 640, 768)


def nt_dot(a, b):
    return lax.dot_general(a, b, (((1,), (1,)), ((), ())), preferred_element_type=F32)


def nn_dot(a, b):
    return jnp.dot(a, b, preferred_element_type=F32)


def head_mask(rows, width, head, base):
    lane = lax.broadcasted_iota(jnp.int32, (rows, width), 1) + base
    return (lane >= head * DHEAD) & (lane < (head + 1) * DHEAD)


def only_head(block, head, base):
    return jnp.where(head_mask(*block.shape, head, base), block.astype(F32), 0.0).astype(BF16)


def places():
    dp, tensor = lax.axis_index("dp"), lax.axis_index("tensor")
    return dp // 4, (tensor // 4) * 2 + (dp // 2) % 2, tensor % 4, dp % 2


def device_at(x, y, z, core):
    return (x * 4 + (y % 2) * 2 + core, (y // 2) * 4 + z)


def link_partners(x, y, z, core):
    pair = lambda i: i + 1 - 2 * (i % 2)
    other = lambda i: 3 - i
    return (
        device_at(pair(x), y, z, core),
        device_at(other(x), y, z, core),
        device_at(x, pair(y), z, core),
        device_at(x, other(y), z, core),
        device_at(x, y, pair(z), core),
        device_at(x, y, other(z), core),
    )


def gray_bits(i):
    return (i + i // 2) % 2, i // 2


def attend(m, owner_ref, len_ref, q_ref, pk_ref, pv_ref, ok_ref, ov_ref, att):
    prompt = owner_ref[0, m]
    length = len_ref[prompt]
    scale = 1.0 / HEAD**0.5
    own_k, own_v = ok_ref[prompt], ov_ref[prompt]
    keys, values = pk_ref[prompt], pv_ref[prompt]
    states = q_ref[prompt]
    heads = states.shape[1] // HEAD
    rows = jnp.concatenate([states[:, j * HEAD : (j + 1) * HEAD] for j in range(heads)], 0)
    first = nt_dot(rows, keys) * scale
    second = nt_dot(rows, own_k) * scale
    column = lax.broadcasted_iota(jnp.int32, first.shape, 1)
    first = jnp.where(column < length, first, -jnp.inf)
    row = lax.broadcasted_iota(jnp.int32, second.shape, 0) % NQ
    column = lax.broadcasted_iota(jnp.int32, second.shape, 1)
    second = jnp.where(column <= row, second, -jnp.inf)
    top = jnp.maximum(jnp.max(first, -1, keepdims=True), jnp.max(second, -1, keepdims=True))
    first, second = jnp.exp(first - top), jnp.exp(second - top)
    total = jnp.sum(first, -1, keepdims=True) + jnp.sum(second, -1, keepdims=True)
    out = nn_dot(first.astype(BF16), values) + nn_dot(second.astype(BF16), own_v)
    out = (out / total).astype(BF16)
    rows_at = pl.ds(pl.multiple_of(m * NQ, NQ), NQ)
    for j in range(heads):
        att[rows_at, j * HEAD : (j + 1) * HEAD] = out[j * NQ : (j + 1) * NQ]


def greet(devices):
    barrier = pltpu.get_barrier_semaphore()
    for device in devices:
        pl.semaphore_signal(barrier, inc=1, device_id=device, device_id_type=MESH)
    pl.semaphore_wait(barrier, len(devices))


TOKENS = 256
GRAD_ROWS = 2048


def one_hot_rows(start, rows):
    row = lax.broadcasted_iota(jnp.int32, (rows, 1), 0) + start
    bit = lambda n: row // (ROWS_PAD << n) % 2
    at = lambda n: 2 * bit(n) + (bit(n) + bit(n + 1)) % 2
    z, y, x, core = at(0), at(2), at(4), bit(6)
    natural = ((x * 2 + y % 2) * 2 + core) * 8 + y // 2 * 4 + z
    inside = row % ROWS_PAD
    source = jnp.where(inside < ROWS_BLOCK, natural * ROWS_BLOCK + inside, -1)
    lane = lax.broadcasted_iota(jnp.int32, (rows, W), 1)
    return jnp.where(lane == source, 1.0, 0.0).astype(BF16)


def split_in_three(value):
    parts = []
    for _ in range(3):
        part = value.astype(BF16)
        parts.append(part)
        value = value - part.astype(F32)
    return parts


def project_kernel(
    owner_ref,
    len_ref,
    step_ref,
    ok_ref,
    ov_ref,
    gain_ref,
    lat_ref,
    noise_ref,
    pw_ref,
    time_ref,
    norm_ref,
    vhw_ref,
    w_hbm,
    q_in,
    pk_in,
    pv_in,
    res_in,
    qm_hbm,
    scaled_ref,
    sq_ref,
    hv_ref,
    q_hbm,
    nt_hbm,
    q_ref,
    pk_ref,
    pv_ref,
    res_ref,
    att,
    wg,
    terms,
    land_first,
    land_second,
    zsum,
    relay,
    landy,
    qm,
    packed,
    pwt,
    col,
    q_out,
    nt_out,
    own_sem,
    qm_sem,
    out_sem,
    w_send,
    w_recv,
    r_send,
    r_recv,
    y_send,
    y_recv,
):
    x, y, z, core = places()
    y_lo, y_hi = y % 2, y // 2
    xp, xo, xf = x + 1 - 2 * (x % 2), 3 - x, (x + 2) % 4
    at_y = device_at(x, y + 1 - 2 * y_lo, z, core)
    at_xp, at_xo = device_at(xp, y, z, core), device_at(xo, y, z, core)
    at_ze, at_zo = device_at(x, y, z + 1 - 2 * (z % 2), core), device_at(x, y, 3 - z, core)
    at_yo = device_at(x, 3 - y, z, core)
    at_sib = device_at(x, y, z, 1 - core)
    bit_b = z // 2
    shared = []

    keep = [
        pltpu.make_async_copy(w_hbm.at[:, h * 256 : (h + 1) * 256], wg.at[x, y_lo, core, h], own_sem.at[h])
        for h in range(2)
    ]
    inputs = [
        pltpu.make_async_copy(source, target, qm_sem.at[n])
        for n, (source, target) in enumerate(
            ((q_in, q_ref), (pk_in, pk_ref), (pv_in, pv_ref), (res_in, res_ref), (qm_hbm, qm))
        )
    ]
    load_qm = inputs[4]
    for copy in keep + inputs:
        copy.start()
    greet((at_y, at_yo, at_xp, at_xo, at_ze, at_zo, at_sib))

    def share(xs, ys, h, *targets):
        slot = wg.at[xs, ys, core, h]
        for target in targets:
            copy = pltpu.make_async_remote_copy(
                src_ref=slot,
                dst_ref=slot,
                send_sem=w_send.at[len(shared)],
                recv_sem=w_recv.at[xs, ys, core, h],
                device_id=target,
                device_id_type=MESH,
            )
            copy.start()
            shared.append(copy)

    def arrived(xs, ys, cs, h):
        slot = wg.at[xs, ys, cs, h]
        pltpu.make_async_remote_copy(
            src_ref=slot,
            dst_ref=slot,
            send_sem=w_send.at[0],
            recv_sem=w_recv.at[xs, ys, cs, h],
            device_id=at_sib,
            device_id_type=MESH,
        ).wait_recv()

    def pass_on(xs, ys, h, *targets):
        arrived(xs, ys, core, h)
        share(xs, ys, h, *targets)

    def prepare():
        packed[0:128, :] = pw_ref[...]
        parts = split_in_three(time_ref[...].reshape(1, W)) + split_in_three(norm_ref[...].reshape(1, W))
        packed[128:256, :] = jnp.concatenate(parts + [jnp.zeros((122, W), BF16)], 0)

        def body(i, carry):
            rows = pl.ds(pl.multiple_of(i * 256, 256), 256)
            value = nt_dot(one_hot_rows(i * 256, 256), packed[...])
            pwt[rows, :] = value[:, :128].astype(BF16)
            col[rows, :] = value[:, 128:]
            return carry

        lax.fori_loop(0, GRAD_ROWS // 256, body, 0)

    def prelude(c):
        t = (step_ref[0].astype(F32) + 0.5) / NT
        rows = pl.ds(c * TOKENS, TOKENS)
        noisy = ((1.0 - t) * lat_ref[rows, :].astype(F32) + t * noise_ref[rows, :].astype(F32)).astype(BF16)
        hidden = nn_dot(noisy, pw_ref[...]) + t * time_ref[...].reshape(1, W)
        scale = lax.rsqrt(jnp.mean(hidden * hidden, -1, keepdims=True) + eps)
        normed = (hidden * scale * norm_ref[...].reshape(1, W)).astype(BF16)
        hv_ref[rows, :] = nn_dot(hidden.astype(BF16), vhw_ref[...])
        q_out[...] = nn_dot(normed, qm[...]).astype(BF16)
        time_col = col[:, 0:1] + col[:, 1:2] + col[:, 2:3]
        norm_col = col[:, 3:4] + col[:, 4:5] + col[:, 5:6]
        ht = nt_dot(pwt[...], noisy) + t * time_col
        scale_t = lax.rsqrt(jnp.sum(ht * ht, 0, keepdims=True) / W + eps)
        nt_out[...] = (ht * scale_t * norm_col).astype(BF16)
        copies = (
            pltpu.make_async_copy(q_out, q_hbm.at[c * TOKENS : (c + 1) * TOKENS, :], out_sem.at[c, 0]),
            pltpu.make_async_copy(nt_out, nt_hbm.at[:, c * TOKENS : (c + 1) * TOKENS], out_sem.at[c, 1]),
        )
        for copy in copies:
            copy.start()
        return copies

    def prompts(start, end):
        def body(m, carry):
            attend(m, owner_ref, len_ref, q_ref, pk_ref, pv_ref, ok_ref, ov_ref, att)
            return carry

        lax.fori_loop(start, end, body, 0)

    first_chip = (x // 2, 1 - x // 2)
    chips = ((x, xp), (xo, xf))
    subs = ((core, 0), (1 - core, 0), (core, 1), (1 - core, 1))
    mine = bit_b

    def row_of(batch):
        return y_lo if batch < 2 else 1 - y_lo

    def passing(batch):
        return batch % 2

    def at_end(batch):
        return z % 2 == row_of(batch)

    def between(batch):
        return z % 2 != row_of(batch)

    def remote(s, which, source, landing, device):
        return pltpu.make_async_remote_copy(
            src_ref=source,
            dst_ref=landing,
            send_sem=r_send.at[s, which],
            recv_sem=r_recv.at[s, which],
            device_id=device,
            device_id_type=MESH,
        )

    def out_block(s):
        return (mine + z + row_of(s // 4) + 1) % 2

    def first(s, part):
        block = out_block(s) if part == 0 else 1 - mine
        return remote(s, part, terms.at[s, part, block], land_first.at[s, part], at_ze if part == 0 else at_zo)

    def second(s, part):
        block = 1 - mine if part == 0 else mine
        landing = land_second.at[passing(s // 4), s % 4, part]
        return remote(s, 2 + part, terms.at[s, part, block], landing, at_zo if part == 0 else at_ze)

    def multiply(s):
        batch = s // 4
        cs, h = subs[s % 4]

        def body(u, carry):
            value = nn_dot(att[...], wg[2 * first_chip[passing(batch)] + u, row_of(batch), cs, h]).astype(BF16)
            terms[s, 0, u] = value[:256]
            terms[s, 1, u] = value[256:]
            return carry

        lax.fori_loop(0, 2, body, 0)
        for part in range(2):
            first(s, part).start()

    def halve(s):
        for part in range(2):
            first(s, part).wait_recv()
            block = 1 - out_block(s) if part == 0 else mine
            total = terms[s, part, block].astype(F32) + land_first[s, part].astype(F32)
            terms[s, part, block] = total.astype(BF16)

        @pl.when(between(s // 4))
        def _():
            for part in range(2):
                second(s, part).start()

    def finish(s):
        batch = s // 4

        @pl.when(at_end(batch))
        def _():
            for part in range(2):
                second(s, part).wait_recv()
                landing = land_second[passing(batch), s % 4, part]
                total = terms[s, part, mine].astype(F32) + landing.astype(F32)
                zsum[passing(batch), s % 4, part * 256 : (part + 1) * 256] = total.astype(BF16)

    kept = (x // 2 + y_hi) % 2

    def across(i, leg):
        part = leg % 2
        if leg < 2:
            source, landing = zsum.at[1 - kept, i, part * 256 : (part + 1) * 256], relay.at[i, part]
        else:
            source, landing = relay.at[i, part], landy.at[i, part]
        return pltpu.make_async_remote_copy(
            src_ref=source,
            dst_ref=landing,
            send_sem=y_send.at[i, leg],
            recv_sem=y_recv.at[i, leg],
            device_id=at_y if leg in (0, 3) else at_yo,
            device_id_type=MESH,
        )

    def cross(i):
        across(i, 0).start()
        across(i, 1).start()

    def relay_on(i):
        for part in range(2):
            across(i, part).wait_recv()
            across(i, 2 + part).start()

    def close(i):
        for part in range(2):
            across(i, 2 + part).wait_recv()
        cs, h = subs[i]
        columns = pl.ds(pl.multiple_of(cs * 512 + h * 256, 256), 256)
        gain = gain_ref[:, columns]

        def body(m, carry):
            rows = pl.ds(pl.multiple_of(m * NQ, NQ), NQ)
            part, inside = m // 4, pl.ds(pl.multiple_of(m % 4 * NQ, NQ), NQ)
            value = res_ref[owner_ref[0, m], :, columns].astype(F32)
            value = value + (zsum[kept, i, rows, :].astype(F32) + landy[i, part, inside, :].astype(F32))
            scaled_ref[rows, columns] = (value * gain).astype(BF16)
            square = value * value
            square = square[:, :128] + square[:, 128:]
            sq_ref[rows, :] = square if i == 0 else sq_ref[rows, :] + square
            return carry

        lax.fori_loop(0, 8, body, 0)

    def steps(batch, h):
        for s in (4 * batch + 2 * h, 4 * batch + 2 * h + 1):
            if s % 2 == 1:
                for xs in chips[passing(batch)]:
                    arrived(xs, row_of(batch), 1 - core, h)
            multiply(s)

    def each(do, *numbers):
        for s in numbers:
            do(s)

    keep[0].wait()
    share(x, y_lo, 0, at_xp, at_xo, at_y, at_sib)
    for copy in inputs[:4]:
        copy.wait()
    prompts(0, 4)
    keep[1].wait()
    pass_on(xo, y_lo, 0, at_xp)
    share(x, y_lo, 1, at_xo, at_y)
    share(xo, y_lo, 0, at_sib)
    pass_on(xp, y_lo, 0, at_sib)
    share(x, y_lo, 1, at_sib)
    prompts(4, 8)
    steps(0, 0)
    pass_on(x, 1 - y_lo, 0, at_sib)
    prepare()
    each(halve, 0, 1)

    pass_on(xo, y_lo, 1)
    share(x, y_lo, 1, at_xp)
    share(x, 1 - y_lo, 0, at_xo)
    pass_on(xf, y_lo, 0, at_y, at_sib)
    share(xo, y_lo, 1, at_sib)
    pass_on(x, 1 - y_lo, 1, at_sib)
    steps(1, 0)
    load_qm.wait()
    stores = prelude(0)
    each(halve, 4, 5)
    each(finish, 0, 1)

    pass_on(xp, y_lo, 1, at_xo)
    share(x, 1 - y_lo, 0, at_xp)
    share(xp, y_lo, 1, at_sib)
    pass_on(xo, 1 - y_lo, 0, at_sib)
    steps(0, 1)
    pass_on(xf, 1 - y_lo, 0, at_sib)
    steps(3, 0)
    for copy in stores:
        copy.wait()
    stores = prelude(1)
    each(halve, 2, 3)
    each(finish, 4, 5)

    pass_on(xf, y_lo, 1, at_y)
    share(x, 1 - y_lo, 1, at_xp, at_xo)
    share(xf, y_lo, 1, at_sib)
    pass_on(xp, 1 - y_lo, 0, at_sib)
    steps(2, 0)
    steps(1, 1)
    each(halve, 12, 13)
    for copy in stores:
        copy.wait()
    stores = prelude(2)
    each(halve, 8, 9, 6, 7)
    each(finish, 2, 3)

    pass_on(xp, 1 - y_lo, 1, at_sib)
    multiply(10)
    pass_on(xo, 1 - y_lo, 1, at_sib)
    pass_on(xf, 1 - y_lo, 1, at_sib)
    multiply(14)
    for xs in (x, xp, xo, xf):
        arrived(xs, 1 - y_lo, 1 - core, 1)
    multiply(11)
    multiply(15)
    each(finish, 12, 8)
    cross(0)
    each(finish, 13, 9)
    cross(1)
    for copy in stores:
        copy.wait()
    stores = prelude(3)
    each(halve, 10, 14)
    relay_on(0)
    each(halve, 11, 15)
    relay_on(1)
    each(finish, 6, 10, 14)
    cross(2)
    close(0)
    each(finish, 7, 11, 15)
    cross(3)
    relay_on(2)
    close(1)
    relay_on(3)
    close(2)
    close(3)
    for copy in stores:
        copy.wait()
    for copy in shared:
        copy.wait_send()
    for s in range(16):
        for part in range(2):
            first(s, part).wait_send()

        @pl.when(between(s // 4))
        def _():
            for part in range(2):
                second(s, part).wait_send()

    for i in range(4):
        for leg in range(4):
            across(i, leg).wait_send()


def projected(
    owner,
    lengths,
    timesteps,
    query_states,
    prompt_keys,
    prompt_values,
    query_keys,
    query_values,
    residual,
    gain,
    latents,
    noise,
    patch_weight,
    time_embedding,
    norm_gain,
    vhw,
    weight,
    qm,
):
    rows = query_states.shape[0] * NQ
    tokens = latents.shape[0]
    vmem, smem = pl.BlockSpec(memory_space=pltpu.VMEM), pl.BlockSpec(memory_space=pltpu.SMEM)
    anywhere = pl.BlockSpec(memory_space=pl.ANY)
    return pl.pallas_call(
        project_kernel,
        out_shape=[
            jax.ShapeDtypeStruct((rows, 1024), BF16),
            jax.ShapeDtypeStruct((rows, 128), F32),
            jax.ShapeDtypeStruct((tokens, 128), F32),
            jax.ShapeDtypeStruct((tokens, W), BF16),
            jax.ShapeDtypeStruct((GRAD_ROWS, tokens), BF16),
        ],
        in_specs=[smem] * 3 + [vmem] * 9 + [anywhere] * 6,
        out_specs=[vmem] * 3 + [anywhere] * 2,
        scratch_shapes=[
            pltpu.VMEM(query_states.shape, BF16),
            pltpu.VMEM(prompt_keys.shape, BF16),
            pltpu.VMEM(prompt_values.shape, BF16),
            pltpu.VMEM(residual.shape, BF16),
            pltpu.VMEM((rows, 1024), BF16),
            pltpu.VMEM((4, 2, 2, 2, 1024, 256), BF16),
            pltpu.VMEM((16, 2, 2, 256, 256), BF16),
            pltpu.VMEM((16, 2, 256, 256), BF16),
            pltpu.VMEM((2, 4, 2, 256, 256), BF16),
            pltpu.VMEM((2, 4, rows, 256), BF16),
            pltpu.VMEM((4, 2, 256, 256), BF16),
            pltpu.VMEM((4, 2, 256, 256), BF16),
            pltpu.VMEM(qm.shape, BF16),
            pltpu.VMEM((256, W), BF16),
            pltpu.VMEM((GRAD_ROWS, 128), BF16),
            pltpu.VMEM((GRAD_ROWS, 128), F32),
            pltpu.VMEM((TOKENS, W), BF16),
            pltpu.VMEM((GRAD_ROWS, TOKENS), BF16),
            pltpu.SemaphoreType.DMA((2,)),
            pltpu.SemaphoreType.DMA((5,)),
            pltpu.SemaphoreType.DMA((4, 2)),
            pltpu.SemaphoreType.DMA((32,)),
            pltpu.SemaphoreType.DMA((4, 2, 2, 2)),
            pltpu.SemaphoreType.DMA((16, 4)),
            pltpu.SemaphoreType.DMA((16, 4)),
            pltpu.SemaphoreType.DMA((4, 4)),
            pltpu.SemaphoreType.DMA((4, 4)),
        ],
        compiler_params=pltpu.CompilerParams(
            collective_id=2, has_side_effects=True, vmem_limit_bytes=62 << 20
        ),
        name="attend_project",
    )(
        owner,
        lengths,
        timesteps,
        query_keys,
        query_values,
        gain.reshape(1, -1),
        latents,
        noise,
        patch_weight,
        time_embedding,
        norm_gain,
        vhw,
        weight,
        query_states,
        prompt_keys,
        prompt_values,
        residual,
        qm,
    )


COLUMNS = 256
CHUNKS = 2 * W // COLUMNS


def finish_kernel(
    gain,
    scaled_ref,
    sq_ref,
    hv_ref,
    lat_ref,
    noise_ref,
    vhw_ref,
    conn_hbm,
    q_hbm,
    nt_hbm,
    vel_ref,
    out_ref,
    conn,
    q,
    nt,
    buf,
    land1,
    land2,
    land3,
    sqb,
    sq1,
    sq2,
    sq3,
    cond,
    kbd,
    kflat,
    vw,
    ones,
    probs,
    dsc,
    dq,
    load_sem,
    send_sem,
    recv_sem,
    core_send,
    core_recv,
    g_send,
    g_recv,
    *pieces,
):
    mine, away, sibling_part = pieces[0:6], pieces[6:12], pieces[12:18]
    landing = [pieces[18 + 6 * p : 24 + 6 * p] for p in range(6)]
    x, y, z, core = places()
    y_hi = y // 2
    partners = link_partners(x, y, z, core)
    at_ze, at_zo = partners[4], partners[5]
    at_far = device_at(x, (y + 2) % 4, z, core)
    sibling = device_at(x, y, z, 1 - core)
    bits = gray_bits(x) + gray_bits(y) + gray_bits(z)
    bit_a, bit_b = gray_bits(z)
    loads = [
        pltpu.make_async_copy(
            conn_hbm.at[:, part * 512 : (part + 1) * 512], conn.at[:, part * 512 : (part + 1) * 512], load_sem.at[part]
        )
        for part in range(7)
    ]
    loads.append(pltpu.make_async_copy(q_hbm, q, load_sem.at[7]))
    loads.append(pltpu.make_async_copy(nt_hbm, nt, load_sem.at[8]))
    for copy in loads:
        copy.start()
    greet(partners + (at_far, sibling))

    sent = []
    flying = {}

    def send(j, phase):
        if j == CHUNKS:
            block, target = sqb, (sq1, sq2, sq3)[phase]
        else:
            block, target = buf.at[j], (land1, land2, land3)[phase].at[j]
        if phase == 0:
            source = block.at[:, 1 - bit_a] if j % 2 == 0 else block.at[:, :, 1 - bit_b]
        elif phase == 1:
            source = block.at[:, bit_a, 1 - bit_b] if j % 2 == 0 else block.at[:, 1 - bit_a, bit_b]
        else:
            source = block.at[1 - y_hi, bit_a, bit_b]
        copy = pltpu.make_async_remote_copy(
            src_ref=source,
            dst_ref=target,
            send_sem=send_sem.at[j, phase],
            recv_sem=recv_sem.at[j, phase],
            device_id=at_far if phase == 2 else at_ze if phase == j % 2 else at_zo,
            device_id_type=MESH,
        )
        copy.start()
        sent.append(copy)
        flying[j] = copy

    def settle(j, phase):
        flying[j].wait_recv()
        if phase == 0:
            index = (slice(None), bit_a) if j % 2 == 0 else (slice(None), slice(None), bit_b)
        else:
            index = (slice(None), bit_a, bit_b)
        if j == CHUNKS:
            sqb[index] = sqb[index] + (sq1, sq2)[phase][...]
        else:
            index = (j,) + index
            total = buf[index].astype(F32) + (land1, land2)[phase][j].astype(F32)
            buf[index] = total.astype(BF16)
        send(j, phase + 1)

    def spread(block, value):
        for m in range(8):
            a, b = gray_bits(m % 4)
            block[m // 4, a, b] = value[m * NQ : (m + 1) * NQ]

    def condition(j, factor):
        flying[j].wait_recv()
        total = buf[j, y_hi, bit_a, bit_b].astype(F32) + land3[j].astype(F32)
        cond[:, j * COLUMNS : (j + 1) * COLUMNS] = (total * factor).astype(BF16)

    def norm_factor():
        flying[CHUNKS].wait_recv()
        squares = sqb[y_hi, bit_a, bit_b] + sq3[...]
        return lax.rsqrt(jnp.sum(squares, -1, keepdims=True) / D + eps)

    scale = 1.0 / DHEAD**0.5

    def place_keys():
        for g, base in enumerate(KEY_WINDOWS):
            for n in range(4):
                window = cond[:, base : base + 512]
                kbd[g, n * NQ : (n + 1) * NQ, :] = only_head(window, 4 * g + n, base)
        for tile, first in enumerate(SCORE_WINDOWS):
            for n in range(4):
                window = cond[:, tile * 256 : (tile + 1) * 256]
                kflat[tile, n * NQ : (n + 1) * NQ, :] = only_head(window, first // NQ + n, tile * 256)
        row = lax.broadcasted_iota(jnp.int32, (256, 256), 0) // NQ
        column = lax.broadcasted_iota(jnp.int32, (256, 256), 1) // NQ
        ones[...] = jnp.where(row == column, 1.0, 0.0).astype(BF16)

    def place_values():
        for g, base in enumerate(KEY_WINDOWS):
            window = cond[:, W + base : W + base + 512]
            vals = [only_head(window, 4 * g + n, base) for n in range(4)]
            vw[g] = nn_dot(jnp.concatenate(vals, 0), vhw_ref[base : base + 512, :]).astype(BF16)

    def softmax(c):
        rows = pl.ds(c * TOKENS, TOKENS)
        for g, base in enumerate(KEY_WINDOWS):
            expo = jnp.exp(nt_dot(q[rows, base : base + 512], kbd[g]) * scale)
            total = nn_dot(jnp.minimum(expo, 3.38e38).astype(BF16), ones[...])
            probs[rows, g * 256 : (g + 1) * 256] = expo / total

    def scores_back(c, carry):
        rows = pl.ds(pl.multiple_of(c * TOKENS, TOKENS), TOKENS)
        velocity = hv_ref[rows, :]
        for g in range(4):
            velocity = velocity + nn_dot(probs[rows, g * 256 : (g + 1) * 256].astype(BF16), vw[g])
        vel_ref[rows, :] = velocity
        target = noise_ref[rows, :].astype(F32) - lat_ref[rows, :].astype(F32)
        dvel = ((velocity - target) * gain).astype(BF16)
        for g in range(4):
            p = probs[rows, g * 256 : (g + 1) * 256]
            dprob = nt_dot(dvel, vw[g])
            both = p * dprob
            high = both.astype(BF16)
            low = (both - high.astype(F32)).astype(BF16)
            shift = nn_dot(high, ones[...]) + nn_dot(low, ones[...])
            dsc[:, g * 256 : (g + 1) * 256] = (p * (dprob - shift) * scale).astype(BF16)
        for tile, first in enumerate(SCORE_WINDOWS):
            dq[rows, tile * 256 : (tile + 1) * 256] = nn_dot(dsc[:, first : first + 256], kflat[tile]).astype(BF16)
        return carry

    def product(p, which, target):
        columns = pl.ds(STARTS[p], PIECES[p])

        def part(i, carry):
            rows = nt[pl.ds(pl.multiple_of(which * 1024 + i * 512, 512), 512), :]
            value = nn_dot(rows, dq[:, columns]).astype(BF16)
            target[i] = value.reshape(2, 2, 2, 2, 2, ROWS_PAD, PIECES[p])
            return carry

        lax.fori_loop(0, 2, part, 0)

    def region(p, k, bit):
        index = []
        for dim in range(6):
            age = (dim - p) % 6
            index.append(bits[dim] if age < k else bit if age == k else slice(None))
        return tuple(index)

    def to_sibling(p):
        return pltpu.make_async_remote_copy(
            src_ref=away[p],
            dst_ref=sibling_part[p],
            send_sem=core_send.at[p],
            recv_sem=core_recv.at[p],
            device_id=sibling,
            device_id_type=MESH,
        )

    def exchange(p, k):
        dim = (p + k) % 6
        return pltpu.make_async_remote_copy(
            src_ref=mine[p].at[region(p, k, 1 - bits[dim])],
            dst_ref=landing[p][k],
            send_sem=g_send.at[p, k],
            recv_sem=g_recv.at[p, k],
            device_id=partners[dim],
            device_id_type=MESH,
        )

    def launch(p, copy):
        copy.start()
        flying["grad", p] = copy
        sent.append(copy)

    def accumulate(p, k):
        flying["grad", p].wait_recv()
        if k == 0:
            index = (slice(None),) * 6
            arrived = sibling_part[p]
        else:
            index = region(p, k - 1, bits[(p + k - 1) % 6])
            arrived = landing[p][k - 1]
        total = mine[p][index].astype(F32) + arrived[...].astype(F32)
        if k == 6:
            out_ref[:, STARTS[p] : STARTS[p] + PIECES[p]] = total
        else:
            mine[p][index] = total.astype(BF16)
            launch(p, exchange(p, k))

    chunks = [CHUNKS] + list(range(CHUNKS))
    for n in range(CHUNKS + 1 + 10):
        if n == 0:
            spread(sqb, sq_ref[...])
            send(CHUNKS, 0)
        elif n <= CHUNKS:
            j = chunks[n]
            if j % 2 == 0:
                loads[j // 2].wait()
            value = nn_dot(scaled_ref[...], conn[:, j * COLUMNS : (j + 1) * COLUMNS])
            spread(buf.at[j], value.astype(BF16))
            send(j, 0)
        if 0 <= n - 6 <= CHUNKS:
            settle(chunks[n - 6], 0)
        if 0 <= n - 10 <= CHUNKS:
            settle(chunks[n - 10], 1)
        if n == 19:
            factor = norm_factor()
            for j in range(7):
                condition(j, factor)
            place_keys()
            loads[7].wait()
        if 20 <= n < 24:
            softmax(n - 20)
    for j in range(7, CHUNKS):
        condition(j, factor)
    place_values()
    lax.fori_loop(0, 4, scores_back, 0)
    loads[8].wait()
    for p in range(7):
        if p < 6:
            product(p, 1 - core, away[p])
            launch(p, to_sibling(p))
            product(p, core, mine[p])
        if p > 0:
            accumulate(p - 1, 0)
    for k in range(1, 7):
        for p in range(6):
            accumulate(p, k)
    for copy in sent:
        copy.wait_send()


def finished(scaled, squares, hv, latents, noise, vhw, conn_weight, q, normed_t, gain):
    tokens = latents.shape[0]
    vmem, anywhere = pl.BlockSpec(memory_space=pltpu.VMEM), pl.BlockSpec(memory_space=pl.ANY)
    full = [pltpu.VMEM((2,) * 6 + (ROWS_PAD, c), BF16) for c in PIECES]
    parts = [pltpu.VMEM((2,) * (5 - k) + (ROWS_PAD, c), BF16) for c in PIECES for k in range(6)]
    velocity, out = pl.pallas_call(
        lambda *refs: finish_kernel(gain, *refs),
        out_shape=[jax.ShapeDtypeStruct((tokens, 128), F32), jax.ShapeDtypeStruct((ROWS_PAD, W), F32)],
        in_specs=[vmem] * 6 + [anywhere] * 3,
        out_specs=[vmem] * 2,
        scratch_shapes=[
            pltpu.VMEM(conn_weight.shape, BF16),
            pltpu.VMEM(q.shape, BF16),
            pltpu.VMEM(normed_t.shape, BF16),
            pltpu.VMEM((CHUNKS, 2, 2, 2, NQ, COLUMNS), BF16),
            pltpu.VMEM((CHUNKS, 2, 2, NQ, COLUMNS), BF16),
            pltpu.VMEM((CHUNKS, 2, NQ, COLUMNS), BF16),
            pltpu.VMEM((CHUNKS, NQ, COLUMNS), BF16),
            pltpu.VMEM((2, 2, 2, NQ, 128), F32),
            pltpu.VMEM((2, 2, NQ, 128), F32),
            pltpu.VMEM((2, NQ, 128), F32),
            pltpu.VMEM((NQ, 128), F32),
            pltpu.VMEM((NQ, 2 * W), BF16),
            pltpu.VMEM((4, 4 * NQ, 512), BF16),
            pltpu.VMEM((7, 4 * NQ, 256), BF16),
            pltpu.VMEM((4, 4 * NQ, 128), BF16),
            pltpu.VMEM((256, 256), BF16),
            pltpu.VMEM((tokens, 1024), F32),
            pltpu.VMEM((TOKENS, 1024), BF16),
            pltpu.VMEM((tokens, W), BF16),
            pltpu.SemaphoreType.DMA((9,)),
            pltpu.SemaphoreType.DMA((CHUNKS + 1, 3)),
            pltpu.SemaphoreType.DMA((CHUNKS + 1, 3)),
            pltpu.SemaphoreType.DMA((6,)),
            pltpu.SemaphoreType.DMA((6,)),
            pltpu.SemaphoreType.DMA((6, 6)),
            pltpu.SemaphoreType.DMA((6, 6)),
        ]
        + full
        + full
        + full
        + parts,
        compiler_params=pltpu.CompilerParams(
            collective_id=3, has_side_effects=True, vmem_limit_bytes=62 << 20
        ),
        name="connect_step_grad",
    )(scaled, squares, hv, latents, noise, vhw, conn_weight, q, normed_t)
    return velocity, out[:ROWS_BLOCK]


def on_device(
    prompt_keys,
    prompt_values,
    query_states,
    query_keys,
    query_values,
    lengths,
    residual,
    out_weight,
    final_gain,
    conn_weight,
    owner,
    latents,
    noise,
    timesteps,
    patch_weight,
    time_embedding,
    image_norm_gain,
    query_matrix,
    velocity_head_weight,
):
    count_of_rows = lax.axis_size("dp") * lax.axis_size("tensor") * latents.shape[1]
    scaled, squares, hv, q, normed_t = projected(
        owner,
        lengths,
        timesteps,
        query_states,
        prompt_keys,
        prompt_values,
        query_keys,
        query_values,
        residual,
        final_gain,
        latents[0],
        noise[0],
        patch_weight,
        time_embedding,
        image_norm_gain,
        velocity_head_weight,
        out_weight,
        query_matrix,
    )
    velocity, query_grad = finished(
        scaled,
        squares,
        hv,
        latents[0],
        noise[0],
        velocity_head_weight,
        conn_weight,
        q,
        normed_t,
        grad_gain / math.sqrt(count_of_rows),
    )
    return (velocity[None], query_grad)


def solution(mesh):
    return jax.shard_map(
        on_device,
        mesh=mesh,
        in_specs=(
            P("dp", None, "tensor"),
            P("dp", None, "tensor"),
            P("dp", None, "tensor"),
            P("dp", None, "tensor"),
            P("dp", None, "tensor"),
            P("dp"),
            P("dp", None, "tensor"),
            P("tensor", "dp"),
            P("tensor"),
            P("tensor", None),
            P("dp", None),
            P(("dp", "tensor"), None, None),
            P(("dp", "tensor"), None, None),
            P(("dp", "tensor")),
            P(),
            P(),
            P(),
            P(),
            P(),
        ),
        out_specs=(P(("dp", "tensor"), None, None), P(("dp", "tensor"), None)),
        check_vma=False,
    )
```

```python
import math

import jax
import jax.numpy as jnp
from jax import lax
from jax.experimental import pallas as pl
from jax.experimental.pallas import tpu as pltpu
from jax.sharding import PartitionSpec as P

D = 8192
HEAD = 128
NQ = 64
DHEAD = 112
NT = 1000
W = 1792
IMG_HEADS = 16
F32 = jnp.float32
BF16 = jnp.bfloat16
MESH = pl.DeviceIdType.MESH

eps = 1e-06
grad_gain = 16.0

ROWS_BLOCK = 14
ROWS_PAD = 16
PIECES = (384, 384, 256, 256, 256, 256)
STARTS = (0, 384, 768, 1024, 1280, 1536)
KEY_WINDOWS = (0, 384, 896, 1280)
SCORE_WINDOWS = (0, 128, 256, 384, 512, 640, 768)


def nt_dot(a, b):
    return lax.dot_general(a, b, (((1,), (1,)), ((), ())), preferred_element_type=F32)


def nn_dot(a, b):
    return jnp.dot(a, b, preferred_element_type=F32)


def head_mask(rows, width, head, base):
    lane = lax.broadcasted_iota(jnp.int32, (rows, width), 1) + base
    return (lane >= head * DHEAD) & (lane < (head + 1) * DHEAD)


def only_head(block, head, base):
    return jnp.where(head_mask(*block.shape, head, base), block.astype(F32), 0.0).astype(BF16)


def places():
    dp, tensor = lax.axis_index("dp"), lax.axis_index("tensor")
    return dp // 4, (tensor // 4) * 2 + (dp // 2) % 2, tensor % 4, dp % 2


def device_at(x, y, z, core):
    return (x * 4 + (y % 2) * 2 + core, (y // 2) * 4 + z)


def link_partners(x, y, z, core):
    pair = lambda i: i + 1 - 2 * (i % 2)
    other = lambda i: 3 - i
    return (
        device_at(pair(x), y, z, core),
        device_at(other(x), y, z, core),
        device_at(x, pair(y), z, core),
        device_at(x, other(y), z, core),
        device_at(x, y, pair(z), core),
        device_at(x, y, other(z), core),
    )


def gray_bits(i):
    return (i + i // 2) % 2, i // 2


def attend(m, owner_ref, len_ref, q_ref, pk_ref, pv_ref, ok_ref, ov_ref, att):
    prompt = owner_ref[0, m]
    length = len_ref[prompt]
    scale = 1.0 / HEAD**0.5
    own_k, own_v = ok_ref[prompt], ov_ref[prompt]
    keys, values = pk_ref[prompt], pv_ref[prompt]
    states = q_ref[prompt]
    heads = states.shape[1] // HEAD
    rows = jnp.concatenate([states[:, j * HEAD : (j + 1) * HEAD] for j in range(heads)], 0)
    first = nt_dot(rows, keys) * scale
    second = nt_dot(rows, own_k) * scale
    column = lax.broadcasted_iota(jnp.int32, first.shape, 1)
    first = jnp.where(column < length, first, -jnp.inf)
    row = lax.broadcasted_iota(jnp.int32, second.shape, 0) % NQ
    column = lax.broadcasted_iota(jnp.int32, second.shape, 1)
    second = jnp.where(column <= row, second, -jnp.inf)
    top = jnp.maximum(jnp.max(first, -1, keepdims=True), jnp.max(second, -1, keepdims=True))
    first, second = jnp.exp(first - top), jnp.exp(second - top)
    total = jnp.sum(first, -1, keepdims=True) + jnp.sum(second, -1, keepdims=True)
    out = nn_dot(first.astype(BF16), values) + nn_dot(second.astype(BF16), own_v)
    out = (out / total).astype(BF16)
    rows_at = pl.ds(pl.multiple_of(m * NQ, NQ), NQ)
    for j in range(heads):
        att[rows_at, j * HEAD : (j + 1) * HEAD] = out[j * NQ : (j + 1) * NQ]


def greet(devices):
    barrier = pltpu.get_barrier_semaphore()
    for device in devices:
        pl.semaphore_signal(barrier, inc=1, device_id=device, device_id_type=MESH)
    pl.semaphore_wait(barrier, len(devices))


TOKENS = 256
GRAD_ROWS = 2048


def one_hot_rows(start, rows):
    row = lax.broadcasted_iota(jnp.int32, (rows, 1), 0) + start
    bit = lambda n: row // (ROWS_PAD << n) % 2
    at = lambda n: 2 * bit(n) + (bit(n) + bit(n + 1)) % 2
    z, y, x, core = at(0), at(2), at(4), bit(6)
    natural = ((x * 2 + y % 2) * 2 + core) * 8 + y // 2 * 4 + z
    inside = row % ROWS_PAD
    source = jnp.where(inside < ROWS_BLOCK, natural * ROWS_BLOCK + inside, -1)
    lane = lax.broadcasted_iota(jnp.int32, (rows, W), 1)
    return jnp.where(lane == source, 1.0, 0.0).astype(BF16)


def split_in_three(value):
    parts = []
    for _ in range(3):
        part = value.astype(BF16)
        parts.append(part)
        value = value - part.astype(F32)
    return parts


def project_kernel(
    owner_ref,
    len_ref,
    step_ref,
    ok_ref,
    ov_ref,
    gain_ref,
    lat_ref,
    noise_ref,
    pw_ref,
    time_ref,
    norm_ref,
    vhw_ref,
    w_hbm,
    q_in,
    pk_in,
    pv_in,
    res_in,
    qm_hbm,
    scaled_ref,
    sq_ref,
    hv_ref,
    q_hbm,
    nt_hbm,
    q_ref,
    pk_ref,
    pv_ref,
    res_ref,
    att,
    wg,
    terms,
    land_first,
    land_second,
    zsum,
    relay,
    landy,
    qm,
    packed,
    pwt,
    col,
    q_out,
    nt_out,
    own_sem,
    qm_sem,
    out_sem,
    w_send,
    w_recv,
    r_send,
    r_recv,
    y_send,
    y_recv,
):
    x, y, z, core = places()
    y_lo, y_hi = y % 2, y // 2
    xp, xo, xf = x + 1 - 2 * (x % 2), 3 - x, (x + 2) % 4
    at_y = device_at(x, y + 1 - 2 * y_lo, z, core)
    at_xp, at_xo = device_at(xp, y, z, core), device_at(xo, y, z, core)
    at_ze, at_zo = device_at(x, y, z + 1 - 2 * (z % 2), core), device_at(x, y, 3 - z, core)
    at_yo = device_at(x, 3 - y, z, core)
    at_sib = device_at(x, y, z, 1 - core)
    bit_b = z // 2
    shared = []

    keep = [
        pltpu.make_async_copy(w_hbm.at[:, h * 256 : (h + 1) * 256], wg.at[x, y_lo, core, h], own_sem.at[h])
        for h in range(2)
    ]
    inputs = [
        pltpu.make_async_copy(source, target, qm_sem.at[n])
        for n, (source, target) in enumerate(
            ((q_in, q_ref), (pk_in, pk_ref), (pv_in, pv_ref), (res_in, res_ref), (qm_hbm, qm))
        )
    ]
    load_qm = inputs[4]
    for copy in keep + inputs:
        copy.start()
    greet((at_y, at_yo, at_xp, at_xo, at_ze, at_zo, at_sib))

    def piece(part):
        return pl.ds(0, 256) if part is None else pl.ds(part * 128, 128)

    def share(xs, ys, h, *targets, part=None):
        slot = wg.at[xs, ys, core, h, :, piece(part)]
        for target in targets:
            copy = pltpu.make_async_remote_copy(
                src_ref=slot,
                dst_ref=slot,
                send_sem=w_send.at[len(shared)],
                recv_sem=w_recv.at[xs, ys, core, h, part or 0],
                device_id=target,
                device_id_type=MESH,
            )
            copy.start()
            shared.append(copy)

    def arrived(xs, ys, cs, h, part=None):
        slot = wg.at[xs, ys, cs, h, :, piece(part)]
        pltpu.make_async_remote_copy(
            src_ref=slot,
            dst_ref=slot,
            send_sem=w_send.at[0],
            recv_sem=w_recv.at[xs, ys, cs, h, part or 0],
            device_id=at_sib,
            device_id_type=MESH,
        ).wait_recv()

    def pass_on(xs, ys, h, *targets, part=None):
        arrived(xs, ys, core, h, part)
        share(xs, ys, h, *targets, part=part)

    def prepare():
        packed[0:128, :] = pw_ref[...]
        parts = split_in_three(time_ref[...].reshape(1, W)) + split_in_three(norm_ref[...].reshape(1, W))
        packed[128:256, :] = jnp.concatenate(parts + [jnp.zeros((122, W), BF16)], 0)

        def body(i, carry):
            rows = pl.ds(pl.multiple_of(i * 256, 256), 256)
            value = nt_dot(one_hot_rows(i * 256, 256), packed[...])
            pwt[rows, :] = value[:, :128].astype(BF16)
            col[rows, :] = value[:, 128:]
            return carry

        lax.fori_loop(0, GRAD_ROWS // 256, body, 0)

    def prelude(c):
        t = (step_ref[0].astype(F32) + 0.5) / NT
        rows = pl.ds(c * TOKENS, TOKENS)
        noisy = ((1.0 - t) * lat_ref[rows, :].astype(F32) + t * noise_ref[rows, :].astype(F32)).astype(BF16)
        hidden = nn_dot(noisy, pw_ref[...]) + t * time_ref[...].reshape(1, W)
        scale = lax.rsqrt(jnp.mean(hidden * hidden, -1, keepdims=True) + eps)
        normed = (hidden * scale * norm_ref[...].reshape(1, W)).astype(BF16)
        hv_ref[rows, :] = nn_dot(hidden.astype(BF16), vhw_ref[...])
        q_out[...] = nn_dot(normed, qm[...]).astype(BF16)
        time_col = col[:, 0:1] + col[:, 1:2] + col[:, 2:3]
        norm_col = col[:, 3:4] + col[:, 4:5] + col[:, 5:6]
        ht = nt_dot(pwt[...], noisy) + t * time_col
        scale_t = lax.rsqrt(jnp.sum(ht * ht, 0, keepdims=True) / W + eps)
        nt_out[...] = (ht * scale_t * norm_col).astype(BF16)
        copies = (
            pltpu.make_async_copy(q_out, q_hbm.at[c * TOKENS : (c + 1) * TOKENS, :], out_sem.at[c, 0]),
            pltpu.make_async_copy(nt_out, nt_hbm.at[:, c * TOKENS : (c + 1) * TOKENS], out_sem.at[c, 1]),
        )
        for copy in copies:
            copy.start()
        return copies

    def prompts(start, end):
        def body(m, carry):
            attend(m, owner_ref, len_ref, q_ref, pk_ref, pv_ref, ok_ref, ov_ref, att)
            return carry

        lax.fori_loop(start, end, body, 0)

    first_chip = (x // 2, 1 - x // 2)
    chips = ((x, xp), (xo, xf))
    subs = ((core, 0), (1 - core, 0), (core, 1), (1 - core, 1))
    mine = bit_b

    def row_of(batch):
        return y_lo if batch < 2 else 1 - y_lo

    def passing(batch):
        return batch % 2

    def at_end(batch):
        return z % 2 == row_of(batch)

    def between(batch):
        return z % 2 != row_of(batch)

    def remote(s, which, part, source, landing, device):
        return pltpu.make_async_remote_copy(
            src_ref=source,
            dst_ref=landing,
            send_sem=r_send.at[s, which, part or 0],
            recv_sem=r_recv.at[s, which, part or 0],
            device_id=device,
            device_id_type=MESH,
        )

    def out_block(s):
        return (mine + z + row_of(s // 4) + 1) % 2

    def first(s, rows, part):
        block = out_block(s) if rows == 0 else 1 - mine
        source, landing = terms.at[s, rows, block, :, piece(part)], land_first.at[s, rows, :, piece(part)]
        return remote(s, rows, part, source, landing, at_ze if rows == 0 else at_zo)

    def second(s, rows, part):
        block = 1 - mine if rows == 0 else mine
        landing = land_second.at[passing(s // 4), s % 4, rows, :, piece(part)]
        return remote(s, 2 + rows, part, terms.at[s, rows, block, :, piece(part)], landing, at_zo if rows == 0 else at_ze)

    def multiply(s, part=None):
        batch = s // 4
        cs, h = subs[s % 4]

        def body(u, carry):
            weight = wg[2 * first_chip[passing(batch)] + u, row_of(batch), cs, h, :, piece(part)]
            value = nn_dot(att[...], weight).astype(BF16)
            terms[s, 0, u, :, piece(part)] = value[:256]
            terms[s, 1, u, :, piece(part)] = value[256:]
            return carry

        lax.fori_loop(0, 2, body, 0)
        for rows in range(2):
            first(s, rows, part).start()

    def halve(s, part=None):
        columns = piece(part)
        for rows in range(2):
            first(s, rows, part).wait_recv()
            block = 1 - out_block(s) if rows == 0 else mine
            total = terms[s, rows, block, :, columns].astype(F32) + land_first[s, rows, :, columns].astype(F32)
            terms[s, rows, block, :, columns] = total.astype(BF16)

        @pl.when(between(s // 4))
        def _():
            for rows in range(2):
                second(s, rows, part).start()

    def finish(s, part=None):
        batch = s // 4
        columns = piece(part)

        @pl.when(at_end(batch))
        def _():
            for rows in range(2):
                second(s, rows, part).wait_recv()
                landing = land_second[passing(batch), s % 4, rows, :, columns]
                total = terms[s, rows, mine, :, columns].astype(F32) + landing.astype(F32)
                zsum[passing(batch), s % 4, rows * 256 : (rows + 1) * 256, columns] = total.astype(BF16)

    kept = (x // 2 + y_hi) % 2

    def across(i, leg):
        part = leg % 2
        if leg < 2:
            source, landing = zsum.at[1 - kept, i, part * 256 : (part + 1) * 256], relay.at[i, part]
        else:
            source, landing = relay.at[i, part], landy.at[i, part]
        return pltpu.make_async_remote_copy(
            src_ref=source,
            dst_ref=landing,
            send_sem=y_send.at[i, leg],
            recv_sem=y_recv.at[i, leg],
            device_id=at_y if leg in (0, 3) else at_yo,
            device_id_type=MESH,
        )

    def cross(i):
        across(i, 0).start()
        across(i, 1).start()

    def relay_on(i):
        for part in range(2):
            across(i, part).wait_recv()
            across(i, 2 + part).start()

    def close(i):
        for part in range(2):
            across(i, 2 + part).wait_recv()
        cs, h = subs[i]
        columns = pl.ds(pl.multiple_of(cs * 512 + h * 256, 256), 256)
        gain = gain_ref[:, columns]

        def body(m, carry):
            rows = pl.ds(pl.multiple_of(m * NQ, NQ), NQ)
            part, inside = m // 4, pl.ds(pl.multiple_of(m % 4 * NQ, NQ), NQ)
            value = res_ref[owner_ref[0, m], :, columns].astype(F32)
            value = value + (zsum[kept, i, rows, :].astype(F32) + landy[i, part, inside, :].astype(F32))
            scaled_ref[rows, columns] = (value * gain).astype(BF16)
            square = value * value
            square = square[:, :128] + square[:, 128:]
            sq_ref[rows, :] = square if i == 0 else sq_ref[rows, :] + square
            return carry

        lax.fori_loop(0, 8, body, 0)

    def steps(batch, h):
        for s in (4 * batch + 2 * h, 4 * batch + 2 * h + 1):
            if s % 2 == 1:
                for xs in chips[passing(batch)]:
                    arrived(xs, row_of(batch), 1 - core, h)
            multiply(s)

    def each(do, *numbers, part=None):
        for s in numbers:
            do(s, part)

    keep[0].wait()
    share(x, y_lo, 0, at_xp, at_xo, at_y, at_sib)
    for copy in inputs[:4]:
        copy.wait()
    prompts(0, 4)
    keep[1].wait()
    pass_on(xo, y_lo, 0, at_xp)
    share(x, y_lo, 1, at_xo, at_y)
    share(xo, y_lo, 0, at_sib)
    pass_on(xp, y_lo, 0, at_sib)
    share(x, y_lo, 1, at_sib)
    prompts(4, 8)
    steps(0, 0)
    pass_on(x, 1 - y_lo, 0, at_sib)
    prepare()
    each(halve, 0, 1)

    pass_on(xo, y_lo, 1)
    share(x, y_lo, 1, at_xp)
    share(x, 1 - y_lo, 0, at_xo)
    pass_on(xf, y_lo, 0, at_y, at_sib)
    share(xo, y_lo, 1, at_sib)
    pass_on(x, 1 - y_lo, 1, at_sib)
    steps(1, 0)
    load_qm.wait()
    stores = prelude(0)
    each(halve, 4, 5)
    each(finish, 0, 1)

    pass_on(xp, y_lo, 1, at_xo)
    share(x, 1 - y_lo, 0, at_xp)
    share(xp, y_lo, 1, at_sib)
    pass_on(xo, 1 - y_lo, 0, at_sib)
    steps(0, 1)
    pass_on(xf, 1 - y_lo, 0, at_sib)
    steps(3, 0)
    for copy in stores:
        copy.wait()
    stores = prelude(1)
    each(halve, 2, 3)
    each(finish, 4, 5)

    arrived(xf, y_lo, core, 1)
    for part in range(2):
        share(xf, y_lo, 1, at_y, part=part)
        share(x, 1 - y_lo, 1, at_xp, at_xo, part=part)
    share(xf, y_lo, 1, at_sib)
    pass_on(xp, 1 - y_lo, 0, at_sib)
    steps(2, 0)
    steps(1, 1)
    each(halve, 12, 13)
    for copy in stores:
        copy.wait()
    stores = prelude(2)
    each(halve, 8, 9, 6, 7)
    each(finish, 2, 3)

    for part in range(2):
        pass_on(xp, 1 - y_lo, 1, at_sib, part=part)
        multiply(10, part)
        pass_on(xo, 1 - y_lo, 1, at_sib, part=part)
        pass_on(xf, 1 - y_lo, 1, at_sib, part=part)
        multiply(14, part)
        if part == 0:
            arrived(x, 1 - y_lo, 1 - core, 1)
        for xs in (xp, xo, xf):
            arrived(xs, 1 - y_lo, 1 - core, 1, part)
        multiply(11, part)
        multiply(15, part)
        if part == 0:
            each(finish, 12, 8)
            cross(0)
            each(finish, 13, 9)
            cross(1)
    each(halve, 10, 14, 11, 15, part=0)
    relay_on(0)
    for copy in stores:
        copy.wait()
    stores = prelude(3)
    each(halve, 10, 14, part=1)
    relay_on(1)
    each(halve, 11, 15, part=1)
    close(0)
    finish(6)
    each(finish, 10, 14, part=0)
    each(finish, 10, 14, part=1)
    cross(2)
    finish(7)
    each(finish, 11, 15, part=0)
    each(finish, 11, 15, part=1)
    cross(3)
    relay_on(2)
    close(1)
    relay_on(3)
    close(2)
    close(3)
    for copy in stores:
        copy.wait()
    for copy in shared:
        copy.wait_send()
    for s in range(16):
        parts = (0, 1) if s in (10, 11, 14, 15) else (None,)
        for part in parts:
            for rows in range(2):
                first(s, rows, part).wait_send()

        @pl.when(between(s // 4))
        def _():
            for part in parts:
                for rows in range(2):
                    second(s, rows, part).wait_send()

    for i in range(4):
        for leg in range(4):
            across(i, leg).wait_send()


def projected(
    owner,
    lengths,
    timesteps,
    query_states,
    prompt_keys,
    prompt_values,
    query_keys,
    query_values,
    residual,
    gain,
    latents,
    noise,
    patch_weight,
    time_embedding,
    norm_gain,
    vhw,
    weight,
    qm,
):
    rows = query_states.shape[0] * NQ
    tokens = latents.shape[0]
    vmem, smem = pl.BlockSpec(memory_space=pltpu.VMEM), pl.BlockSpec(memory_space=pltpu.SMEM)
    anywhere = pl.BlockSpec(memory_space=pl.ANY)
    return pl.pallas_call(
        project_kernel,
        out_shape=[
            jax.ShapeDtypeStruct((rows, 1024), BF16),
            jax.ShapeDtypeStruct((rows, 128), F32),
            jax.ShapeDtypeStruct((tokens, 128), F32),
            jax.ShapeDtypeStruct((tokens, W), BF16),
            jax.ShapeDtypeStruct((GRAD_ROWS, tokens), BF16),
        ],
        in_specs=[smem] * 3 + [vmem] * 9 + [anywhere] * 6,
        out_specs=[vmem] * 3 + [anywhere] * 2,
        scratch_shapes=[
            pltpu.VMEM(query_states.shape, BF16),
            pltpu.VMEM(prompt_keys.shape, BF16),
            pltpu.VMEM(prompt_values.shape, BF16),
            pltpu.VMEM(residual.shape, BF16),
            pltpu.VMEM((rows, 1024), BF16),
            pltpu.VMEM((4, 2, 2, 2, 1024, 256), BF16),
            pltpu.VMEM((16, 2, 2, 256, 256), BF16),
            pltpu.VMEM((16, 2, 256, 256), BF16),
            pltpu.VMEM((2, 4, 2, 256, 256), BF16),
            pltpu.VMEM((2, 4, rows, 256), BF16),
            pltpu.VMEM((4, 2, 256, 256), BF16),
            pltpu.VMEM((4, 2, 256, 256), BF16),
            pltpu.VMEM(qm.shape, BF16),
            pltpu.VMEM((256, W), BF16),
            pltpu.VMEM((GRAD_ROWS, 128), BF16),
            pltpu.VMEM((GRAD_ROWS, 128), F32),
            pltpu.VMEM((TOKENS, W), BF16),
            pltpu.VMEM((GRAD_ROWS, TOKENS), BF16),
            pltpu.SemaphoreType.DMA((2,)),
            pltpu.SemaphoreType.DMA((5,)),
            pltpu.SemaphoreType.DMA((4, 2)),
            pltpu.SemaphoreType.DMA((40,)),
            pltpu.SemaphoreType.DMA((4, 2, 2, 2, 2)),
            pltpu.SemaphoreType.DMA((16, 4, 2)),
            pltpu.SemaphoreType.DMA((16, 4, 2)),
            pltpu.SemaphoreType.DMA((4, 4)),
            pltpu.SemaphoreType.DMA((4, 4)),
        ],
        compiler_params=pltpu.CompilerParams(
            collective_id=2, has_side_effects=True, vmem_limit_bytes=62 << 20
        ),
        name="attend_project",
    )(
        owner,
        lengths,
        timesteps,
        query_keys,
        query_values,
        gain.reshape(1, -1),
        latents,
        noise,
        patch_weight,
        time_embedding,
        norm_gain,
        vhw,
        weight,
        query_states,
        prompt_keys,
        prompt_values,
        residual,
        qm,
    )


COLUMNS = 256
CHUNKS = 2 * W // COLUMNS


def finish_kernel(
    gain,
    scaled_ref,
    sq_ref,
    hv_ref,
    lat_ref,
    noise_ref,
    vhw_ref,
    conn_hbm,
    q_hbm,
    nt_hbm,
    vel_ref,
    out_ref,
    conn,
    q,
    nt,
    buf,
    land1,
    land2,
    land3,
    sqb,
    sq1,
    sq2,
    sq3,
    cond,
    kbd,
    kflat,
    vw,
    ones,
    probs,
    dsc,
    dq,
    load_sem,
    send_sem,
    recv_sem,
    core_send,
    core_recv,
    g_send,
    g_recv,
    *pieces,
):
    mine, away, sibling_part = pieces[0:6], pieces[6:12], pieces[12:18]
    landing = [pieces[18 + 6 * p : 24 + 6 * p] for p in range(6)]
    x, y, z, core = places()
    y_hi = y // 2
    partners = link_partners(x, y, z, core)
    at_ze, at_zo = partners[4], partners[5]
    at_far = device_at(x, (y + 2) % 4, z, core)
    sibling = device_at(x, y, z, 1 - core)
    bits = gray_bits(x) + gray_bits(y) + gray_bits(z)
    bit_a, bit_b = gray_bits(z)
    loads = [
        pltpu.make_async_copy(
            conn_hbm.at[:, part * 512 : (part + 1) * 512], conn.at[:, part * 512 : (part + 1) * 512], load_sem.at[part]
        )
        for part in range(7)
    ]
    loads.append(pltpu.make_async_copy(q_hbm, q, load_sem.at[7]))
    loads.append(pltpu.make_async_copy(nt_hbm, nt, load_sem.at[8]))
    for copy in loads:
        copy.start()
    greet(partners + (at_far, sibling))

    sent = []
    flying = {}

    def send(j, phase):
        if j == CHUNKS:
            block, target = sqb, (sq1, sq2, sq3)[phase]
        else:
            block, target = buf.at[j], (land1, land2, land3)[phase].at[j]
        if phase == 0:
            source = block.at[:, 1 - bit_a] if j % 2 == 0 else block.at[:, :, 1 - bit_b]
        elif phase == 1:
            source = block.at[:, bit_a, 1 - bit_b] if j % 2 == 0 else block.at[:, 1 - bit_a, bit_b]
        else:
            source = block.at[1 - y_hi, bit_a, bit_b]
        copy = pltpu.make_async_remote_copy(
            src_ref=source,
            dst_ref=target,
            send_sem=send_sem.at[j, phase],
            recv_sem=recv_sem.at[j, phase],
            device_id=at_far if phase == 2 else at_ze if phase == j % 2 else at_zo,
            device_id_type=MESH,
        )
        copy.start()
        sent.append(copy)
        flying[j] = copy

    def settle(j, phase):
        flying[j].wait_recv()
        if phase == 0:
            index = (slice(None), bit_a) if j % 2 == 0 else (slice(None), slice(None), bit_b)
        else:
            index = (slice(None), bit_a, bit_b)
        if j == CHUNKS:
            sqb[index] = sqb[index] + (sq1, sq2)[phase][...]
        else:
            index = (j,) + index
            total = buf[index].astype(F32) + (land1, land2)[phase][j].astype(F32)
            buf[index] = total.astype(BF16)
        send(j, phase + 1)

    def spread(block, value):
        for m in range(8):
            a, b = gray_bits(m % 4)
            block[m // 4, a, b] = value[m * NQ : (m + 1) * NQ]

    def condition(j, factor):
        flying[j].wait_recv()
        total = buf[j, y_hi, bit_a, bit_b].astype(F32) + land3[j].astype(F32)
        cond[:, j * COLUMNS : (j + 1) * COLUMNS] = (total * factor).astype(BF16)

    def norm_factor():
        flying[CHUNKS].wait_recv()
        squares = sqb[y_hi, bit_a, bit_b] + sq3[...]
        return lax.rsqrt(jnp.sum(squares, -1, keepdims=True) / D + eps)

    scale = 1.0 / DHEAD**0.5

    def place_keys():
        for g, base in enumerate(KEY_WINDOWS):
            for n in range(4):
                window = cond[:, base : base + 512]
                kbd[g, n * NQ : (n + 1) * NQ, :] = only_head(window, 4 * g + n, base)
        for tile, first in enumerate(SCORE_WINDOWS):
            for n in range(4):
                window = cond[:, tile * 256 : (tile + 1) * 256]
                kflat[tile, n * NQ : (n + 1) * NQ, :] = only_head(window, first // NQ + n, tile * 256)
        row = lax.broadcasted_iota(jnp.int32, (256, 256), 0) // NQ
        column = lax.broadcasted_iota(jnp.int32, (256, 256), 1) // NQ
        ones[...] = jnp.where(row == column, 1.0, 0.0).astype(BF16)

    def place_values():
        for g, base in enumerate(KEY_WINDOWS):
            window = cond[:, W + base : W + base + 512]
            vals = [only_head(window, 4 * g + n, base) for n in range(4)]
            vw[g] = nn_dot(jnp.concatenate(vals, 0), vhw_ref[base : base + 512, :]).astype(BF16)

    def softmax(c):
        rows = pl.ds(c * TOKENS, TOKENS)
        for g, base in enumerate(KEY_WINDOWS):
            expo = jnp.exp(nt_dot(q[rows, base : base + 512], kbd[g]) * scale)
            total = nn_dot(jnp.minimum(expo, 3.38e38).astype(BF16), ones[...])
            probs[rows, g * 256 : (g + 1) * 256] = expo / total

    def scores_back(c, carry):
        rows = pl.ds(pl.multiple_of(c * TOKENS, TOKENS), TOKENS)
        velocity = hv_ref[rows, :]
        for g in range(4):
            velocity = velocity + nn_dot(probs[rows, g * 256 : (g + 1) * 256].astype(BF16), vw[g])
        vel_ref[rows, :] = velocity
        target = noise_ref[rows, :].astype(F32) - lat_ref[rows, :].astype(F32)
        dvel = ((velocity - target) * gain).astype(BF16)
        for g in range(4):
            p = probs[rows, g * 256 : (g + 1) * 256]
            dprob = nt_dot(dvel, vw[g])
            both = p * dprob
            high = both.astype(BF16)
            low = (both - high.astype(F32)).astype(BF16)
            shift = nn_dot(high, ones[...]) + nn_dot(low, ones[...])
            dsc[:, g * 256 : (g + 1) * 256] = (p * (dprob - shift) * scale).astype(BF16)
        for tile, first in enumerate(SCORE_WINDOWS):
            dq[rows, tile * 256 : (tile + 1) * 256] = nn_dot(dsc[:, first : first + 256], kflat[tile]).astype(BF16)
        return carry

    def product(p, which, target):
        columns = pl.ds(STARTS[p], PIECES[p])

        def part(i, carry):
            rows = nt[pl.ds(pl.multiple_of(which * 1024 + i * 512, 512), 512), :]
            value = nn_dot(rows, dq[:, columns]).astype(BF16)
            target[i] = value.reshape(2, 2, 2, 2, 2, ROWS_PAD, PIECES[p])
            return carry

        lax.fori_loop(0, 2, part, 0)

    def region(p, k, bit):
        index = []
        for dim in range(6):
            age = (dim - p) % 6
            index.append(bits[dim] if age < k else bit if age == k else slice(None))
        return tuple(index)

    def to_sibling(p):
        return pltpu.make_async_remote_copy(
            src_ref=away[p],
            dst_ref=sibling_part[p],
            send_sem=core_send.at[p],
            recv_sem=core_recv.at[p],
            device_id=sibling,
            device_id_type=MESH,
        )

    def exchange(p, k):
        dim = (p + k) % 6
        return pltpu.make_async_remote_copy(
            src_ref=mine[p].at[region(p, k, 1 - bits[dim])],
            dst_ref=landing[p][k],
            send_sem=g_send.at[p, k],
            recv_sem=g_recv.at[p, k],
            device_id=partners[dim],
            device_id_type=MESH,
        )

    def launch(p, copy):
        copy.start()
        flying["grad", p] = copy
        sent.append(copy)

    def accumulate(p, k):
        flying["grad", p].wait_recv()
        if k == 0:
            index = (slice(None),) * 6
            arrived = sibling_part[p]
        else:
            index = region(p, k - 1, bits[(p + k - 1) % 6])
            arrived = landing[p][k - 1]
        total = mine[p][index].astype(F32) + arrived[...].astype(F32)
        if k == 6:
            out_ref[:, STARTS[p] : STARTS[p] + PIECES[p]] = total
        else:
            mine[p][index] = total.astype(BF16)
            launch(p, exchange(p, k))

    chunks = [CHUNKS] + list(range(CHUNKS))
    for n in range(CHUNKS + 1 + 10):
        if n == 0:
            spread(sqb, sq_ref[...])
            send(CHUNKS, 0)
        elif n <= CHUNKS:
            j = chunks[n]
            if j % 2 == 0:
                loads[j // 2].wait()
            value = nn_dot(scaled_ref[...], conn[:, j * COLUMNS : (j + 1) * COLUMNS])
            spread(buf.at[j], value.astype(BF16))
            send(j, 0)
        if 0 <= n - 6 <= CHUNKS:
            settle(chunks[n - 6], 0)
        if 0 <= n - 10 <= CHUNKS:
            settle(chunks[n - 10], 1)
        if n == 19:
            factor = norm_factor()
            for j in range(7):
                condition(j, factor)
            place_keys()
            loads[7].wait()
        if 20 <= n < 24:
            softmax(n - 20)
    for j in range(7, CHUNKS):
        condition(j, factor)
    place_values()
    lax.fori_loop(0, 4, scores_back, 0)
    loads[8].wait()
    for p in range(7):
        if p < 6:
            product(p, 1 - core, away[p])
            launch(p, to_sibling(p))
            product(p, core, mine[p])
        if p > 0:
            accumulate(p - 1, 0)
    for k in range(1, 7):
        for p in range(6):
            accumulate(p, k)
    for copy in sent:
        copy.wait_send()


def finished(scaled, squares, hv, latents, noise, vhw, conn_weight, q, normed_t, gain):
    tokens = latents.shape[0]
    vmem, anywhere = pl.BlockSpec(memory_space=pltpu.VMEM), pl.BlockSpec(memory_space=pl.ANY)
    full = [pltpu.VMEM((2,) * 6 + (ROWS_PAD, c), BF16) for c in PIECES]
    parts = [pltpu.VMEM((2,) * (5 - k) + (ROWS_PAD, c), BF16) for c in PIECES for k in range(6)]
    velocity, out = pl.pallas_call(
        lambda *refs: finish_kernel(gain, *refs),
        out_shape=[jax.ShapeDtypeStruct((tokens, 128), F32), jax.ShapeDtypeStruct((ROWS_PAD, W), F32)],
        in_specs=[vmem] * 6 + [anywhere] * 3,
        out_specs=[vmem] * 2,
        scratch_shapes=[
            pltpu.VMEM(conn_weight.shape, BF16),
            pltpu.VMEM(q.shape, BF16),
            pltpu.VMEM(normed_t.shape, BF16),
            pltpu.VMEM((CHUNKS, 2, 2, 2, NQ, COLUMNS), BF16),
            pltpu.VMEM((CHUNKS, 2, 2, NQ, COLUMNS), BF16),
            pltpu.VMEM((CHUNKS, 2, NQ, COLUMNS), BF16),
            pltpu.VMEM((CHUNKS, NQ, COLUMNS), BF16),
            pltpu.VMEM((2, 2, 2, NQ, 128), F32),
            pltpu.VMEM((2, 2, NQ, 128), F32),
            pltpu.VMEM((2, NQ, 128), F32),
            pltpu.VMEM((NQ, 128), F32),
            pltpu.VMEM((NQ, 2 * W), BF16),
            pltpu.VMEM((4, 4 * NQ, 512), BF16),
            pltpu.VMEM((7, 4 * NQ, 256), BF16),
            pltpu.VMEM((4, 4 * NQ, 128), BF16),
            pltpu.VMEM((256, 256), BF16),
            pltpu.VMEM((tokens, 1024), F32),
            pltpu.VMEM((TOKENS, 1024), BF16),
            pltpu.VMEM((tokens, W), BF16),
            pltpu.SemaphoreType.DMA((9,)),
            pltpu.SemaphoreType.DMA((CHUNKS + 1, 3)),
            pltpu.SemaphoreType.DMA((CHUNKS + 1, 3)),
            pltpu.SemaphoreType.DMA((6,)),
            pltpu.SemaphoreType.DMA((6,)),
            pltpu.SemaphoreType.DMA((6, 6)),
            pltpu.SemaphoreType.DMA((6, 6)),
        ]
        + full
        + full
        + full
        + parts,
        compiler_params=pltpu.CompilerParams(
            collective_id=3, has_side_effects=True, vmem_limit_bytes=62 << 20
        ),
        name="connect_step_grad",
    )(scaled, squares, hv, latents, noise, vhw, conn_weight, q, normed_t)
    return velocity, out[:ROWS_BLOCK]


def on_device(
    prompt_keys,
    prompt_values,
    query_states,
    query_keys,
    query_values,
    lengths,
    residual,
    out_weight,
    final_gain,
    conn_weight,
    owner,
    latents,
    noise,
    timesteps,
    patch_weight,
    time_embedding,
    image_norm_gain,
    query_matrix,
    velocity_head_weight,
):
    count_of_rows = lax.axis_size("dp") * lax.axis_size("tensor") * latents.shape[1]
    scaled, squares, hv, q, normed_t = projected(
        owner,
        lengths,
        timesteps,
        query_states,
        prompt_keys,
        prompt_values,
        query_keys,
        query_values,
        residual,
        final_gain,
        latents[0],
        noise[0],
        patch_weight,
        time_embedding,
        image_norm_gain,
        velocity_head_weight,
        out_weight,
        query_matrix,
    )
    velocity, query_grad = finished(
        scaled,
        squares,
        hv,
        latents[0],
        noise[0],
        velocity_head_weight,
        conn_weight,
        q,
        normed_t,
        grad_gain / math.sqrt(count_of_rows),
    )
    return (velocity[None], query_grad)


def solution(mesh):
    return jax.shard_map(
        on_device,
        mesh=mesh,
        in_specs=(
            P("dp", None, "tensor"),
            P("dp", None, "tensor"),
            P("dp", None, "tensor"),
            P("dp", None, "tensor"),
            P("dp", None, "tensor"),
            P("dp"),
            P("dp", None, "tensor"),
            P("tensor", "dp"),
            P("tensor"),
            P("tensor", None),
            P("dp", None),
            P(("dp", "tensor"), None, None),
            P(("dp", "tensor"), None, None),
            P(("dp", "tensor")),
            P(),
            P(),
            P(),
            P(),
            P(),
        ),
        out_specs=(P(("dp", "tensor"), None, None), P(("dp", "tensor"), None)),
        check_vma=False,
    )
```

```python
import math

import jax
import jax.numpy as jnp
from jax import lax
from jax.experimental import pallas as pl
from jax.experimental.pallas import tpu as pltpu
from jax.sharding import PartitionSpec as P

D = 8192
HEAD = 128
NQ = 64
DHEAD = 112
NT = 1000
W = 1792
IMG_HEADS = 16
F32 = jnp.float32
BF16 = jnp.bfloat16
MESH = pl.DeviceIdType.MESH

eps = 1e-06
grad_gain = 16.0

ROWS_BLOCK = 14
ROWS_PAD = 16
PIECES = (384, 384, 256, 256, 256, 256)
STARTS = (0, 384, 768, 1024, 1280, 1536)
KEY_WINDOWS = (0, 384, 896, 1280)
SCORE_WINDOWS = (0, 128, 256, 384, 512, 640, 768)


def nt_dot(a, b):
    return lax.dot_general(a, b, (((1,), (1,)), ((), ())), preferred_element_type=F32)


def nn_dot(a, b):
    return jnp.dot(a, b, preferred_element_type=F32)


def head_mask(rows, width, head, base):
    lane = lax.broadcasted_iota(jnp.int32, (rows, width), 1) + base
    return (lane >= head * DHEAD) & (lane < (head + 1) * DHEAD)


def only_head(block, head, base):
    return jnp.where(head_mask(*block.shape, head, base), block.astype(F32), 0.0).astype(BF16)


def places():
    dp, tensor = lax.axis_index("dp"), lax.axis_index("tensor")
    return dp // 4, (tensor // 4) * 2 + (dp // 2) % 2, tensor % 4, dp % 2


def device_at(x, y, z, core):
    return (x * 4 + (y % 2) * 2 + core, (y // 2) * 4 + z)


def link_partners(x, y, z, core):
    pair = lambda i: i + 1 - 2 * (i % 2)
    other = lambda i: 3 - i
    return (
        device_at(pair(x), y, z, core),
        device_at(other(x), y, z, core),
        device_at(x, pair(y), z, core),
        device_at(x, other(y), z, core),
        device_at(x, y, pair(z), core),
        device_at(x, y, other(z), core),
    )


def gray_bits(i):
    return (i + i // 2) % 2, i // 2


def attend(m, owner_ref, len_ref, q_ref, pk_ref, pv_ref, ok_ref, ov_ref, att):
    prompt = owner_ref[0, m]
    length = len_ref[prompt]
    scale = 1.0 / HEAD**0.5
    own_k, own_v = ok_ref[prompt], ov_ref[prompt]
    keys, values = pk_ref[prompt], pv_ref[prompt]
    states = q_ref[prompt]
    heads = states.shape[1] // HEAD
    rows = jnp.concatenate([states[:, j * HEAD : (j + 1) * HEAD] for j in range(heads)], 0)
    first = nt_dot(rows, keys) * scale
    second = nt_dot(rows, own_k) * scale
    column = lax.broadcasted_iota(jnp.int32, first.shape, 1)
    first = jnp.where(column < length, first, -jnp.inf)
    row = lax.broadcasted_iota(jnp.int32, second.shape, 0) % NQ
    column = lax.broadcasted_iota(jnp.int32, second.shape, 1)
    second = jnp.where(column <= row, second, -jnp.inf)
    top = jnp.maximum(jnp.max(first, -1, keepdims=True), jnp.max(second, -1, keepdims=True))
    first, second = jnp.exp(first - top), jnp.exp(second - top)
    total = jnp.sum(first, -1, keepdims=True) + jnp.sum(second, -1, keepdims=True)
    out = nn_dot(first.astype(BF16), values) + nn_dot(second.astype(BF16), own_v)
    out = (out / total).astype(BF16)
    rows_at = pl.ds(pl.multiple_of(m * NQ, NQ), NQ)
    for j in range(heads):
        att[rows_at, j * HEAD : (j + 1) * HEAD] = out[j * NQ : (j + 1) * NQ]


def greet(devices):
    barrier = pltpu.get_barrier_semaphore()
    for device in devices:
        pl.semaphore_signal(barrier, inc=1, device_id=device, device_id_type=MESH)
    pl.semaphore_wait(barrier, len(devices))


TOKENS = 256
GRAD_ROWS = 2048


def one_hot_rows(start, rows):
    row = lax.broadcasted_iota(jnp.int32, (rows, 1), 0) + start
    bit = lambda n: row // (ROWS_PAD << n) % 2
    at = lambda n: 2 * bit(n) + (bit(n) + bit(n + 1)) % 2
    z, y, x, core = at(0), at(2), at(4), bit(6)
    natural = ((x * 2 + y % 2) * 2 + core) * 8 + y // 2 * 4 + z
    inside = row % ROWS_PAD
    source = jnp.where(inside < ROWS_BLOCK, natural * ROWS_BLOCK + inside, -1)
    lane = lax.broadcasted_iota(jnp.int32, (rows, W), 1)
    return jnp.where(lane == source, 1.0, 0.0).astype(BF16)


def split_in_three(value):
    parts = []
    for _ in range(3):
        part = value.astype(BF16)
        parts.append(part)
        value = value - part.astype(F32)
    return parts


def project_kernel(
    owner_ref,
    len_ref,
    step_ref,
    ok_ref,
    ov_ref,
    gain_ref,
    lat_ref,
    noise_ref,
    pw_ref,
    time_ref,
    norm_ref,
    vhw_ref,
    w_hbm,
    q_in,
    pk_in,
    pv_in,
    res_in,
    qm_hbm,
    scaled_ref,
    sq_ref,
    hv_ref,
    q_hbm,
    nt_hbm,
    q_ref,
    pk_ref,
    pv_ref,
    res_ref,
    att,
    wg,
    terms,
    land_first,
    land_second,
    zsum,
    relay,
    landy,
    qm,
    packed,
    pwt,
    col,
    q_out,
    nt_out,
    own_sem,
    qm_sem,
    out_sem,
    w_send,
    w_recv,
    r_send,
    r_recv,
    y_send,
    y_recv,
):
    x, y, z, core = places()
    y_lo, y_hi = y % 2, y // 2
    xp, xo, xf = x + 1 - 2 * (x % 2), 3 - x, (x + 2) % 4
    at_y = device_at(x, y + 1 - 2 * y_lo, z, core)
    at_xp, at_xo = device_at(xp, y, z, core), device_at(xo, y, z, core)
    at_ze, at_zo = device_at(x, y, z + 1 - 2 * (z % 2), core), device_at(x, y, 3 - z, core)
    at_yo = device_at(x, 3 - y, z, core)
    at_sib = device_at(x, y, z, 1 - core)
    bit_b = z // 2
    shared = []

    keep = [
        pltpu.make_async_copy(w_hbm.at[:, h * 256 : (h + 1) * 256], wg.at[x, y_lo, core, h], own_sem.at[h])
        for h in range(2)
    ]
    inputs = [
        pltpu.make_async_copy(source, target, qm_sem.at[n])
        for n, (source, target) in enumerate(
            ((q_in, q_ref), (pk_in, pk_ref), (pv_in, pv_ref), (res_in, res_ref), (qm_hbm, qm))
        )
    ]
    load_qm = inputs[4]
    for copy in keep + inputs:
        copy.start()
    greet((at_y, at_yo, at_xp, at_xo, at_ze, at_zo, at_sib))

    def share(xs, ys, h, *targets):
        slot = wg.at[xs, ys, core, h]
        for target in targets:
            copy = pltpu.make_async_remote_copy(
                src_ref=slot,
                dst_ref=slot,
                send_sem=w_send.at[len(shared)],
                recv_sem=w_recv.at[xs, ys, core, h],
                device_id=target,
                device_id_type=MESH,
            )
            copy.start()
            shared.append(copy)

    def arrived(xs, ys, cs, h):
        slot = wg.at[xs, ys, cs, h]
        pltpu.make_async_remote_copy(
            src_ref=slot,
            dst_ref=slot,
            send_sem=w_send.at[0],
            recv_sem=w_recv.at[xs, ys, cs, h],
            device_id=at_sib,
            device_id_type=MESH,
        ).wait_recv()

    def pass_on(xs, ys, h, *targets):
        arrived(xs, ys, core, h)
        share(xs, ys, h, *targets)

    def prepare():
        packed[0:128, :] = pw_ref[...]
        parts = split_in_three(time_ref[...].reshape(1, W)) + split_in_three(norm_ref[...].reshape(1, W))
        packed[128:256, :] = jnp.concatenate(parts + [jnp.zeros((122, W), BF16)], 0)

        def body(i, carry):
            rows = pl.ds(pl.multiple_of(i * 256, 256), 256)
            value = nt_dot(one_hot_rows(i * 256, 256), packed[...])
            pwt[rows, :] = value[:, :128].astype(BF16)
            col[rows, :] = value[:, 128:]
            return carry

        lax.fori_loop(0, GRAD_ROWS // 256, body, 0)

    def prelude(c):
        t = (step_ref[0].astype(F32) + 0.5) / NT
        rows = pl.ds(c * TOKENS, TOKENS)
        noisy = ((1.0 - t) * lat_ref[rows, :].astype(F32) + t * noise_ref[rows, :].astype(F32)).astype(BF16)
        hidden = nn_dot(noisy, pw_ref[...]) + t * time_ref[...].reshape(1, W)
        scale = lax.rsqrt(jnp.mean(hidden * hidden, -1, keepdims=True) + eps)
        normed = (hidden * scale * norm_ref[...].reshape(1, W)).astype(BF16)
        hv_ref[rows, :] = nn_dot(hidden.astype(BF16), vhw_ref[...])
        q_out[...] = nn_dot(normed, qm[...]).astype(BF16)
        time_col = col[:, 0:1] + col[:, 1:2] + col[:, 2:3]
        norm_col = col[:, 3:4] + col[:, 4:5] + col[:, 5:6]
        ht = nt_dot(pwt[...], noisy) + t * time_col
        scale_t = lax.rsqrt(jnp.sum(ht * ht, 0, keepdims=True) / W + eps)
        nt_out[...] = (ht * scale_t * norm_col).astype(BF16)
        copies = (
            pltpu.make_async_copy(q_out, q_hbm.at[c * TOKENS : (c + 1) * TOKENS, :], out_sem.at[c, 0]),
            pltpu.make_async_copy(nt_out, nt_hbm.at[:, c * TOKENS : (c + 1) * TOKENS], out_sem.at[c, 1]),
        )
        for copy in copies:
            copy.start()
        return copies

    def prompts(start, end):
        def body(m, carry):
            attend(m, owner_ref, len_ref, q_ref, pk_ref, pv_ref, ok_ref, ov_ref, att)
            return carry

        lax.fori_loop(start, end, body, 0)

    first_chip = (x // 2, 1 - x // 2)
    chips = ((x, xp), (xo, xf))
    subs = ((core, 0), (1 - core, 0), (core, 1), (1 - core, 1))
    mine = bit_b

    def row_of(batch):
        return y_lo if batch < 2 else 1 - y_lo

    def passing(batch):
        return batch % 2

    def at_end(batch):
        return z % 2 == row_of(batch)

    def between(batch):
        return z % 2 != row_of(batch)

    def remote(s, which, source, landing, device):
        return pltpu.make_async_remote_copy(
            src_ref=source,
            dst_ref=landing,
            send_sem=r_send.at[s, which],
            recv_sem=r_recv.at[s, which],
            device_id=device,
            device_id_type=MESH,
        )

    def out_block(s):
        return (mine + z + row_of(s // 4) + 1) % 2

    def first(s, part):
        block = out_block(s) if part == 0 else 1 - mine
        return remote(s, part, terms.at[s, part, block], land_first.at[s, part], at_ze if part == 0 else at_zo)

    def second(s, part):
        block = 1 - mine if part == 0 else mine
        landing = land_second.at[passing(s // 4), s % 4, part]
        return remote(s, 2 + part, terms.at[s, part, block], landing, at_zo if part == 0 else at_ze)

    def multiply(s):
        batch = s // 4
        cs, h = subs[s % 4]

        def body(u, carry):
            value = nn_dot(att[...], wg[2 * first_chip[passing(batch)] + u, row_of(batch), cs, h]).astype(BF16)
            terms[s, 0, u] = value[:256]
            terms[s, 1, u] = value[256:]
            return carry

        lax.fori_loop(0, 2, body, 0)
        for part in range(2):
            first(s, part).start()

    def halve(s):
        for part in range(2):
            first(s, part).wait_recv()
            block = 1 - out_block(s) if part == 0 else mine
            total = terms[s, part, block].astype(F32) + land_first[s, part].astype(F32)
            terms[s, part, block] = total.astype(BF16)

        @pl.when(between(s // 4))
        def _():
            for part in range(2):
                second(s, part).start()

    def finish(s):
        batch = s // 4

        @pl.when(at_end(batch))
        def _():
            for part in range(2):
                second(s, part).wait_recv()
                landing = land_second[passing(batch), s % 4, part]
                total = terms[s, part, mine].astype(F32) + landing.astype(F32)
                zsum[passing(batch), s % 4, part * 256 : (part + 1) * 256] = total.astype(BF16)

    kept = (x // 2 + y_hi) % 2

    def across(i, leg):
        part = leg % 2
        if leg < 2:
            source, landing = zsum.at[1 - kept, i, part * 256 : (part + 1) * 256], relay.at[i, part]
        else:
            source, landing = relay.at[i, part], landy.at[i, part]
        return pltpu.make_async_remote_copy(
            src_ref=source,
            dst_ref=landing,
            send_sem=y_send.at[i, leg],
            recv_sem=y_recv.at[i, leg],
            device_id=at_y if leg in (0, 3) else at_yo,
            device_id_type=MESH,
        )

    def cross(i):
        across(i, 0).start()
        across(i, 1).start()

    def relay_on(i):
        for part in range(2):
            across(i, part).wait_recv()
            across(i, 2 + part).start()

    def close(i):
        for part in range(2):
            across(i, 2 + part).wait_recv()
        cs, h = subs[i]
        columns = pl.ds(pl.multiple_of(cs * 512 + h * 256, 256), 256)
        gain = gain_ref[:, columns]

        def body(m, carry):
            rows = pl.ds(pl.multiple_of(m * NQ, NQ), NQ)
            part, inside = m // 4, pl.ds(pl.multiple_of(m % 4 * NQ, NQ), NQ)
            value = res_ref[owner_ref[0, m], :, columns].astype(F32)
            value = value + (zsum[kept, i, rows, :].astype(F32) + landy[i, part, inside, :].astype(F32))
            scaled_ref[rows, columns] = (value * gain).astype(BF16)
            square = value * value
            square = square[:, :128] + square[:, 128:]
            sq_ref[rows, :] = square if i == 0 else sq_ref[rows, :] + square
            return carry

        lax.fori_loop(0, 8, body, 0)

    def steps(batch, h):
        for s in (4 * batch + 2 * h, 4 * batch + 2 * h + 1):
            if s % 2 == 1:
                for xs in chips[passing(batch)]:
                    arrived(xs, row_of(batch), 1 - core, h)
            multiply(s)

    def each(do, *numbers):
        for s in numbers:
            do(s)

    keep[0].wait()
    share(x, y_lo, 0, at_xp, at_xo, at_y, at_sib)
    for copy in inputs[:4]:
        copy.wait()
    prompts(0, 4)
    keep[1].wait()
    pass_on(xo, y_lo, 0, at_xp)
    share(x, y_lo, 1, at_xo, at_y)
    share(xo, y_lo, 0, at_sib)
    pass_on(xp, y_lo, 0, at_sib)
    share(x, y_lo, 1, at_sib)
    prompts(4, 8)
    steps(0, 0)
    pass_on(x, 1 - y_lo, 0, at_sib)
    prepare()
    each(halve, 0, 1)

    pass_on(xo, y_lo, 1)
    share(x, y_lo, 1, at_xp)
    share(x, 1 - y_lo, 0, at_xo)
    pass_on(xf, y_lo, 0, at_y, at_sib)
    share(xo, y_lo, 1, at_sib)
    pass_on(x, 1 - y_lo, 1, at_sib)
    steps(1, 0)
    load_qm.wait()
    stores = prelude(0)
    each(halve, 4, 5)
    each(finish, 0, 1)

    pass_on(xp, y_lo, 1, at_xo)
    share(x, 1 - y_lo, 0, at_xp)
    share(xp, y_lo, 1, at_sib)
    pass_on(xo, 1 - y_lo, 0, at_sib)
    steps(0, 1)
    pass_on(xf, 1 - y_lo, 0, at_sib)
    steps(3, 0)
    for copy in stores:
        copy.wait()
    stores = prelude(1)
    each(halve, 2, 3)
    each(finish, 4, 5)

    pass_on(xf, y_lo, 1, at_y)
    share(x, 1 - y_lo, 1, at_xp, at_xo)
    share(xf, y_lo, 1, at_sib)
    pass_on(xp, 1 - y_lo, 0, at_sib)
    steps(2, 0)
    steps(1, 1)
    each(halve, 12, 13)
    for copy in stores:
        copy.wait()
    stores = prelude(2)
    each(halve, 8, 9, 6, 7)
    each(finish, 2, 3)

    pass_on(xp, 1 - y_lo, 1, at_sib)
    multiply(10)
    pass_on(xo, 1 - y_lo, 1, at_sib)
    pass_on(xf, 1 - y_lo, 1, at_sib)
    multiply(14)
    for xs in (x, xp, xo, xf):
        arrived(xs, 1 - y_lo, 1 - core, 1)
    multiply(11)
    multiply(15)
    each(finish, 12, 8)
    cross(0)
    each(finish, 13, 9)
    cross(1)
    for copy in stores:
        copy.wait()
    stores = prelude(3)
    each(halve, 10, 14)
    relay_on(0)
    each(halve, 11, 15)
    relay_on(1)
    each(finish, 6, 10, 14)
    cross(2)
    close(0)
    each(finish, 7, 11, 15)
    cross(3)
    relay_on(2)
    close(1)
    relay_on(3)
    close(2)
    close(3)
    for copy in stores:
        copy.wait()
    for copy in shared:
        copy.wait_send()
    for s in range(16):
        for part in range(2):
            first(s, part).wait_send()

        @pl.when(between(s // 4))
        def _():
            for part in range(2):
                second(s, part).wait_send()

    for i in range(4):
        for leg in range(4):
            across(i, leg).wait_send()


def projected(
    owner,
    lengths,
    timesteps,
    query_states,
    prompt_keys,
    prompt_values,
    query_keys,
    query_values,
    residual,
    gain,
    latents,
    noise,
    patch_weight,
    time_embedding,
    norm_gain,
    vhw,
    weight,
    qm,
):
    rows = query_states.shape[0] * NQ
    tokens = latents.shape[0]
    vmem, smem = pl.BlockSpec(memory_space=pltpu.VMEM), pl.BlockSpec(memory_space=pltpu.SMEM)
    anywhere = pl.BlockSpec(memory_space=pl.ANY)
    return pl.pallas_call(
        project_kernel,
        out_shape=[
            jax.ShapeDtypeStruct((rows, 1024), BF16),
            jax.ShapeDtypeStruct((rows, 128), F32),
            jax.ShapeDtypeStruct((tokens, 128), F32),
            jax.ShapeDtypeStruct((tokens, W), BF16),
            jax.ShapeDtypeStruct((GRAD_ROWS, tokens), BF16),
        ],
        in_specs=[smem] * 3 + [vmem] * 9 + [anywhere] * 6,
        out_specs=[vmem] * 3 + [anywhere] * 2,
        scratch_shapes=[
            pltpu.VMEM(query_states.shape, BF16),
            pltpu.VMEM(prompt_keys.shape, BF16),
            pltpu.VMEM(prompt_values.shape, BF16),
            pltpu.VMEM(residual.shape, BF16),
            pltpu.VMEM((rows, 1024), BF16),
            pltpu.VMEM((4, 2, 2, 2, 1024, 256), BF16),
            pltpu.VMEM((16, 2, 2, 256, 256), BF16),
            pltpu.VMEM((16, 2, 256, 256), BF16),
            pltpu.VMEM((2, 4, 2, 256, 256), BF16),
            pltpu.VMEM((2, 4, rows, 256), BF16),
            pltpu.VMEM((4, 2, 256, 256), BF16),
            pltpu.VMEM((4, 2, 256, 256), BF16),
            pltpu.VMEM(qm.shape, BF16),
            pltpu.VMEM((256, W), BF16),
            pltpu.VMEM((GRAD_ROWS, 128), BF16),
            pltpu.VMEM((GRAD_ROWS, 128), F32),
            pltpu.VMEM((TOKENS, W), BF16),
            pltpu.VMEM((GRAD_ROWS, TOKENS), BF16),
            pltpu.SemaphoreType.DMA((2,)),
            pltpu.SemaphoreType.DMA((5,)),
            pltpu.SemaphoreType.DMA((4, 2)),
            pltpu.SemaphoreType.DMA((32,)),
            pltpu.SemaphoreType.DMA((4, 2, 2, 2)),
            pltpu.SemaphoreType.DMA((16, 4)),
            pltpu.SemaphoreType.DMA((16, 4)),
            pltpu.SemaphoreType.DMA((4, 4)),
            pltpu.SemaphoreType.DMA((4, 4)),
        ],
        compiler_params=pltpu.CompilerParams(
            collective_id=2, has_side_effects=True, vmem_limit_bytes=62 << 20
        ),
        name="attend_project",
    )(
        owner,
        lengths,
        timesteps,
        query_keys,
        query_values,
        gain.reshape(1, -1),
        latents,
        noise,
        patch_weight,
        time_embedding,
        norm_gain,
        vhw,
        weight,
        query_states,
        prompt_keys,
        prompt_values,
        residual,
        qm,
    )


COLUMNS = 256
CHUNKS = 2 * W // COLUMNS


def finish_kernel(
    gain,
    scaled_ref,
    sq_ref,
    hv_ref,
    lat_ref,
    noise_ref,
    vhw_ref,
    conn_hbm,
    q_hbm,
    nt_hbm,
    vel_ref,
    out_ref,
    conn,
    q,
    nt,
    buf,
    land1,
    land2,
    land3,
    sqb,
    sq1,
    sq2,
    sq3,
    cond,
    kbd,
    kflat,
    vw,
    ones,
    probs,
    dsc,
    dq,
    load_sem,
    send_sem,
    recv_sem,
    core_send,
    core_recv,
    g_send,
    g_recv,
    *pieces,
):
    mine, away, sibling_part = pieces[0:6], pieces[6:12], pieces[12:18]
    landing = [pieces[18 + 5 * p : 23 + 5 * p] for p in range(6)]
    x, y, z, core = places()
    y_hi = y // 2
    partners = link_partners(x, y, z, core)
    at_ze, at_zo = partners[4], partners[5]
    at_far = device_at(x, (y + 2) % 4, z, core)
    sibling = device_at(x, y, z, 1 - core)

    def across_two(dim, later):
        place = [x, y, z]
        for flipped in (dim, later):
            i = place[flipped // 2]
            place[flipped // 2] = 3 - i if flipped % 2 else i + 1 - 2 * (i % 2)
        return device_at(*place, core)

    corners = tuple(across_two((p + 4) % 6, (p + 5) % 6) for p in range(6))
    bits = gray_bits(x) + gray_bits(y) + gray_bits(z)
    bit_a, bit_b = gray_bits(z)
    loads = [
        pltpu.make_async_copy(
            conn_hbm.at[:, part * 512 : (part + 1) * 512], conn.at[:, part * 512 : (part + 1) * 512], load_sem.at[part]
        )
        for part in range(7)
    ]
    loads.append(pltpu.make_async_copy(q_hbm, q, load_sem.at[7]))
    loads.append(pltpu.make_async_copy(nt_hbm, nt, load_sem.at[8]))
    for copy in loads:
        copy.start()
    greet(partners + corners + (sibling,))

    sent = []
    flying = {}

    def send(j, phase):
        if j == CHUNKS:
            block, target = sqb, (sq1, sq2, sq3)[phase]
        else:
            block, target = buf.at[j], (land1, land2, land3)[phase].at[j]
        if phase == 0:
            source = block.at[:, 1 - bit_a] if j % 2 == 0 else block.at[:, :, 1 - bit_b]
        elif phase == 1:
            source = block.at[:, bit_a, 1 - bit_b] if j % 2 == 0 else block.at[:, 1 - bit_a, bit_b]
        else:
            source = block.at[1 - y_hi, bit_a, bit_b]
        copy = pltpu.make_async_remote_copy(
            src_ref=source,
            dst_ref=target,
            send_sem=send_sem.at[j, phase],
            recv_sem=recv_sem.at[j, phase],
            device_id=at_far if phase == 2 else at_ze if phase == j % 2 else at_zo,
            device_id_type=MESH,
        )
        copy.start()
        sent.append(copy)
        flying[j] = copy

    def settle(j, phase):
        flying[j].wait_recv()
        if phase == 0:
            index = (slice(None), bit_a) if j % 2 == 0 else (slice(None), slice(None), bit_b)
        else:
            index = (slice(None), bit_a, bit_b)
        if j == CHUNKS:
            sqb[index] = sqb[index] + (sq1, sq2)[phase][...]
        else:
            index = (j,) + index
            total = buf[index].astype(F32) + (land1, land2)[phase][j].astype(F32)
            buf[index] = total.astype(BF16)
        send(j, phase + 1)

    def spread(block, value):
        for m in range(8):
            a, b = gray_bits(m % 4)
            block[m // 4, a, b] = value[m * NQ : (m + 1) * NQ]

    def condition(j, factor):
        flying[j].wait_recv()
        total = buf[j, y_hi, bit_a, bit_b].astype(F32) + land3[j].astype(F32)
        cond[:, j * COLUMNS : (j + 1) * COLUMNS] = (total * factor).astype(BF16)

    def norm_factor():
        flying[CHUNKS].wait_recv()
        squares = sqb[y_hi, bit_a, bit_b] + sq3[...]
        return lax.rsqrt(jnp.sum(squares, -1, keepdims=True) / D + eps)

    scale = 1.0 / DHEAD**0.5

    def place_keys():
        for g, base in enumerate(KEY_WINDOWS):
            for n in range(4):
                window = cond[:, base : base + 512]
                kbd[g, n * NQ : (n + 1) * NQ, :] = only_head(window, 4 * g + n, base)
        for tile, first in enumerate(SCORE_WINDOWS):
            for n in range(4):
                window = cond[:, tile * 256 : (tile + 1) * 256]
                kflat[tile, n * NQ : (n + 1) * NQ, :] = only_head(window, first // NQ + n, tile * 256)
        row = lax.broadcasted_iota(jnp.int32, (256, 256), 0) // NQ
        column = lax.broadcasted_iota(jnp.int32, (256, 256), 1) // NQ
        ones[...] = jnp.where(row == column, 1.0, 0.0).astype(BF16)

    def place_values():
        for g, base in enumerate(KEY_WINDOWS):
            window = cond[:, W + base : W + base + 512]
            vals = [only_head(window, 4 * g + n, base) for n in range(4)]
            vw[g] = nn_dot(jnp.concatenate(vals, 0), vhw_ref[base : base + 512, :]).astype(BF16)

    def softmax(c):
        rows = pl.ds(c * TOKENS, TOKENS)
        for g, base in enumerate(KEY_WINDOWS):
            expo = jnp.exp(nt_dot(q[rows, base : base + 512], kbd[g]) * scale)
            total = nn_dot(jnp.minimum(expo, 3.38e38).astype(BF16), ones[...])
            probs[rows, g * 256 : (g + 1) * 256] = expo / total

    def scores_back(c, carry):
        rows = pl.ds(pl.multiple_of(c * TOKENS, TOKENS), TOKENS)
        velocity = hv_ref[rows, :]
        for g in range(4):
            velocity = velocity + nn_dot(probs[rows, g * 256 : (g + 1) * 256].astype(BF16), vw[g])
        vel_ref[rows, :] = velocity
        target = noise_ref[rows, :].astype(F32) - lat_ref[rows, :].astype(F32)
        dvel = ((velocity - target) * gain).astype(BF16)
        for g in range(4):
            p = probs[rows, g * 256 : (g + 1) * 256]
            dprob = nt_dot(dvel, vw[g])
            both = p * dprob
            high = both.astype(BF16)
            low = (both - high.astype(F32)).astype(BF16)
            shift = nn_dot(high, ones[...]) + nn_dot(low, ones[...])
            dsc[:, g * 256 : (g + 1) * 256] = (p * (dprob - shift) * scale).astype(BF16)
        for tile, first in enumerate(SCORE_WINDOWS):
            dq[rows, tile * 256 : (tile + 1) * 256] = nn_dot(dsc[:, first : first + 256], kflat[tile]).astype(BF16)
        return carry

    def product(p, which, target):
        columns = pl.ds(STARTS[p], PIECES[p])

        def part(i, carry):
            rows = nt[pl.ds(pl.multiple_of(which * 1024 + i * 512, 512), 512), :]
            value = nn_dot(rows, dq[:, columns]).astype(BF16)
            target[i] = value.reshape(2, 2, 2, 2, 2, ROWS_PAD, PIECES[p])
            return carry

        lax.fori_loop(0, 2, part, 0)

    def region(p, k, bit):
        index = []
        for dim in range(6):
            age = (dim - p) % 6
            index.append(bits[dim] if age < k else bit if age == k else slice(None))
        return tuple(index)

    def to_sibling(p):
        return pltpu.make_async_remote_copy(
            src_ref=away[p],
            dst_ref=sibling_part[p],
            send_sem=core_send.at[p],
            recv_sem=core_recv.at[p],
            device_id=sibling,
            device_id_type=MESH,
        )

    def exchange(p, k):
        dim = (p + k) % 6
        return pltpu.make_async_remote_copy(
            src_ref=mine[p].at[region(p, k, 1 - bits[dim])],
            dst_ref=landing[p][k],
            send_sem=g_send.at[p, k],
            recv_sem=g_recv.at[p, k],
            device_id=partners[dim],
            device_id_type=MESH,
        )

    def direct(p, flips):
        dims = ((p + 4) % 6, (p + 5) % 6)
        index = list(bits)
        for n, dim in enumerate(dims):
            if flips >> n & 1:
                index[dim] = 1 - bits[dim]
        device = corners[p] if flips == 3 else partners[dims[flips - 1]]
        return pltpu.make_async_remote_copy(
            src_ref=mine[p].at[tuple(index)],
            dst_ref=landing[p][4].at[flips - 1],
            send_sem=g_send.at[p, 3 + flips],
            recv_sem=g_recv.at[p, 3 + flips],
            device_id=device,
            device_id_type=MESH,
        )

    def launch(p, *copies):
        for copy in copies:
            copy.start()
            sent.append(copy)
        flying["grad", p] = copies

    def accumulate(p, k):
        for copy in flying["grad", p]:
            copy.wait_recv()
        if k == 0:
            index = (slice(None),) * 6
            arrived = sibling_part[p][...].astype(F32)
        elif k == 5:
            index = bits
            arrived = landing[p][4][0].astype(F32) + landing[p][4][1].astype(F32) + landing[p][4][2].astype(F32)
        else:
            index = region(p, k - 1, bits[(p + k - 1) % 6])
            arrived = landing[p][k - 1][...].astype(F32)
        total = mine[p][index].astype(F32) + arrived
        if k == 5:
            out_ref[:, STARTS[p] : STARTS[p] + PIECES[p]] = total
            return
        mine[p][index] = total.astype(BF16)
        if k == 4:
            launch(p, *[direct(p, flips) for flips in (1, 2, 3)])
        else:
            launch(p, exchange(p, k))

    chunks = [CHUNKS] + list(range(CHUNKS))
    for n in range(CHUNKS + 1 + 10):
        if n == 0:
            spread(sqb, sq_ref[...])
            send(CHUNKS, 0)
        elif n <= CHUNKS:
            j = chunks[n]
            if j % 2 == 0:
                loads[j // 2].wait()
            value = nn_dot(scaled_ref[...], conn[:, j * COLUMNS : (j + 1) * COLUMNS])
            spread(buf.at[j], value.astype(BF16))
            send(j, 0)
        if 0 <= n - 6 <= CHUNKS:
            settle(chunks[n - 6], 0)
        if 0 <= n - 10 <= CHUNKS:
            settle(chunks[n - 10], 1)
        if n == 19:
            factor = norm_factor()
            for j in range(7):
                condition(j, factor)
            place_keys()
            loads[7].wait()
        if 20 <= n < 24:
            softmax(n - 20)
    for j in range(7, CHUNKS):
        condition(j, factor)
    place_values()
    lax.fori_loop(0, 4, scores_back, 0)
    loads[8].wait()
    for p in range(7):
        if p < 6:
            product(p, 1 - core, away[p])
            launch(p, to_sibling(p))
            product(p, core, mine[p])
        if p > 0:
            accumulate(p - 1, 0)
    for k in range(1, 6):
        for p in range(6):
            accumulate(p, k)
    for copy in sent:
        copy.wait_send()


def hand_over_kernel(vel_ref, grad_ref, vel_out, grad_out):
    vel_out[...] = vel_ref[...]
    grad_out[...] = grad_ref[0:ROWS_BLOCK, :]


def finished(scaled, squares, hv, latents, noise, vhw, conn_weight, q, normed_t, gain):
    tokens = latents.shape[0]
    vmem, anywhere = pl.BlockSpec(memory_space=pltpu.VMEM), pl.BlockSpec(memory_space=pl.ANY)
    full = [pltpu.VMEM((2,) * 6 + (ROWS_PAD, c), BF16) for c in PIECES]
    parts = [
        pltpu.VMEM(((2,) * (5 - k) if k < 4 else (3,)) + (ROWS_PAD, c), BF16) for c in PIECES for k in range(5)
    ]
    velocity, out = pl.pallas_call(
        lambda *refs: finish_kernel(gain, *refs),
        out_shape=[jax.ShapeDtypeStruct((tokens, 128), F32), jax.ShapeDtypeStruct((ROWS_PAD, W), F32)],
        in_specs=[vmem] * 6 + [anywhere] * 3,
        out_specs=[vmem] * 2,
        scratch_shapes=[
            pltpu.VMEM(conn_weight.shape, BF16),
            pltpu.VMEM(q.shape, BF16),
            pltpu.VMEM(normed_t.shape, BF16),
            pltpu.VMEM((CHUNKS, 2, 2, 2, NQ, COLUMNS), BF16),
            pltpu.VMEM((CHUNKS, 2, 2, NQ, COLUMNS), BF16),
            pltpu.VMEM((CHUNKS, 2, NQ, COLUMNS), BF16),
            pltpu.VMEM((CHUNKS, NQ, COLUMNS), BF16),
            pltpu.VMEM((2, 2, 2, NQ, 128), F32),
            pltpu.VMEM((2, 2, NQ, 128), F32),
            pltpu.VMEM((2, NQ, 128), F32),
            pltpu.VMEM((NQ, 128), F32),
            pltpu.VMEM((NQ, 2 * W), BF16),
            pltpu.VMEM((4, 4 * NQ, 512), BF16),
            pltpu.VMEM((7, 4 * NQ, 256), BF16),
            pltpu.VMEM((4, 4 * NQ, 128), BF16),
            pltpu.VMEM((256, 256), BF16),
            pltpu.VMEM((tokens, 1024), F32),
            pltpu.VMEM((TOKENS, 1024), BF16),
            pltpu.VMEM((tokens, W), BF16),
            pltpu.SemaphoreType.DMA((9,)),
            pltpu.SemaphoreType.DMA((CHUNKS + 1, 3)),
            pltpu.SemaphoreType.DMA((CHUNKS + 1, 3)),
            pltpu.SemaphoreType.DMA((6,)),
            pltpu.SemaphoreType.DMA((6,)),
            pltpu.SemaphoreType.DMA((6, 7)),
            pltpu.SemaphoreType.DMA((6, 7)),
        ]
        + full
        + full
        + full
        + parts,
        compiler_params=pltpu.CompilerParams(
            collective_id=3, has_side_effects=True, vmem_limit_bytes=62 << 20
        ),
        name="connect_step_grad",
    )(scaled, squares, hv, latents, noise, vhw, conn_weight, q, normed_t)
    return pl.pallas_call(
        hand_over_kernel,
        out_shape=[jax.ShapeDtypeStruct((tokens, 128), F32), jax.ShapeDtypeStruct((ROWS_BLOCK, W), F32)],
        in_specs=[vmem] * 2,
        out_specs=[vmem] * 2,
        name="hand_over",
    )(velocity, out)


def on_device(
    prompt_keys,
    prompt_values,
    query_states,
    query_keys,
    query_values,
    lengths,
    residual,
    out_weight,
    final_gain,
    conn_weight,
    owner,
    latents,
    noise,
    timesteps,
    patch_weight,
    time_embedding,
    image_norm_gain,
    query_matrix,
    velocity_head_weight,
):
    count_of_rows = lax.axis_size("dp") * lax.axis_size("tensor") * latents.shape[1]
    scaled, squares, hv, q, normed_t = projected(
        owner,
        lengths,
        timesteps,
        query_states,
        prompt_keys,
        prompt_values,
        query_keys,
        query_values,
        residual,
        final_gain,
        latents[0],
        noise[0],
        patch_weight,
        time_embedding,
        image_norm_gain,
        velocity_head_weight,
        out_weight,
        query_matrix,
    )
    velocity, query_grad = finished(
        scaled,
        squares,
        hv,
        latents[0],
        noise[0],
        velocity_head_weight,
        conn_weight,
        q,
        normed_t,
        grad_gain / math.sqrt(count_of_rows),
    )
    return (velocity[None], query_grad)


def solution(mesh):
    return jax.shard_map(
        on_device,
        mesh=mesh,
        in_specs=(
            P("dp", None, "tensor"),
            P("dp", None, "tensor"),
            P("dp", None, "tensor"),
            P("dp", None, "tensor"),
            P("dp", None, "tensor"),
            P("dp"),
            P("dp", None, "tensor"),
            P("tensor", "dp"),
            P("tensor"),
            P("tensor", None),
            P("dp", None),
            P(("dp", "tensor"), None, None),
            P(("dp", "tensor"), None, None),
            P(("dp", "tensor")),
            P(),
            P(),
            P(),
            P(),
            P(),
        ),
        out_specs=(P(("dp", "tensor"), None, None), P(("dp", "tensor"), None)),
        check_vma=False,
    )
```

```python
import math

import jax
import jax.numpy as jnp
from jax import lax
from jax.experimental import pallas as pl
from jax.experimental.pallas import tpu as pltpu
from jax.sharding import PartitionSpec as P

D = 8192
HEAD = 128
NQ = 64
DHEAD = 112
NT = 1000
W = 1792
IMG_HEADS = 16
F32 = jnp.float32
BF16 = jnp.bfloat16
MESH = pl.DeviceIdType.MESH

eps = 1e-06
grad_gain = 16.0

ROWS_BLOCK = 14
ROWS_PAD = 16
PIECES = (384, 384, 256, 256, 256, 256)
STARTS = (0, 384, 768, 1024, 1280, 1536)
KEY_WINDOWS = (0, 384, 896, 1280)
SCORE_WINDOWS = (0, 128, 256, 384, 512, 640, 768)


def nt_dot(a, b):
    return lax.dot_general(a, b, (((1,), (1,)), ((), ())), preferred_element_type=F32)


def nn_dot(a, b):
    return jnp.dot(a, b, preferred_element_type=F32)


def head_mask(rows, width, head, base):
    lane = lax.broadcasted_iota(jnp.int32, (rows, width), 1) + base
    return (lane >= head * DHEAD) & (lane < (head + 1) * DHEAD)


def only_head(block, head, base):
    return jnp.where(head_mask(*block.shape, head, base), block.astype(F32), 0.0).astype(BF16)


def places():
    dp, tensor = lax.axis_index("dp"), lax.axis_index("tensor")
    return dp // 4, (tensor // 4) * 2 + (dp // 2) % 2, tensor % 4, dp % 2


def device_at(x, y, z, core):
    return (x * 4 + (y % 2) * 2 + core, (y // 2) * 4 + z)


def link_partners(x, y, z, core):
    pair = lambda i: i + 1 - 2 * (i % 2)
    other = lambda i: 3 - i
    return (
        device_at(pair(x), y, z, core),
        device_at(other(x), y, z, core),
        device_at(x, pair(y), z, core),
        device_at(x, other(y), z, core),
        device_at(x, y, pair(z), core),
        device_at(x, y, other(z), core),
    )


def gray_bits(i):
    return (i + i // 2) % 2, i // 2


def attend(m, owner_ref, len_ref, q_ref, pk_ref, pv_ref, ok_ref, ov_ref, att):
    prompt = owner_ref[0, m]
    length = len_ref[prompt]
    scale = 1.0 / HEAD**0.5
    own_k, own_v = ok_ref[prompt], ov_ref[prompt]
    keys, values = pk_ref[prompt], pv_ref[prompt]
    states = q_ref[prompt]
    heads = states.shape[1] // HEAD
    rows = jnp.concatenate([states[:, j * HEAD : (j + 1) * HEAD] for j in range(heads)], 0)
    first = nt_dot(rows, keys) * scale
    second = nt_dot(rows, own_k) * scale
    column = lax.broadcasted_iota(jnp.int32, first.shape, 1)
    first = jnp.where(column < length, first, -jnp.inf)
    row = lax.broadcasted_iota(jnp.int32, second.shape, 0) % NQ
    column = lax.broadcasted_iota(jnp.int32, second.shape, 1)
    second = jnp.where(column <= row, second, -jnp.inf)
    top = jnp.maximum(jnp.max(first, -1, keepdims=True), jnp.max(second, -1, keepdims=True))
    first, second = jnp.exp(first - top), jnp.exp(second - top)
    total = jnp.sum(first, -1, keepdims=True) + jnp.sum(second, -1, keepdims=True)
    out = nn_dot(first.astype(BF16), values) + nn_dot(second.astype(BF16), own_v)
    out = (out / total).astype(BF16)
    rows_at = pl.ds(pl.multiple_of(m * NQ, NQ), NQ)
    for j in range(heads):
        att[rows_at, j * HEAD : (j + 1) * HEAD] = out[j * NQ : (j + 1) * NQ]


def greet(devices):
    barrier = pltpu.get_barrier_semaphore()
    for device in devices:
        pl.semaphore_signal(barrier, inc=1, device_id=device, device_id_type=MESH)
    pl.semaphore_wait(barrier, len(devices))


TOKENS = 256
GRAD_ROWS = 2048


def one_hot_rows(start, rows):
    row = lax.broadcasted_iota(jnp.int32, (rows, 1), 0) + start
    bit = lambda n: row // (ROWS_PAD << n) % 2
    at = lambda n: 2 * bit(n) + (bit(n) + bit(n + 1)) % 2
    z, y, x, core = at(0), at(2), at(4), bit(6)
    natural = ((x * 2 + y % 2) * 2 + core) * 8 + y // 2 * 4 + z
    inside = row % ROWS_PAD
    source = jnp.where(inside < ROWS_BLOCK, natural * ROWS_BLOCK + inside, -1)
    lane = lax.broadcasted_iota(jnp.int32, (rows, W), 1)
    return jnp.where(lane == source, 1.0, 0.0).astype(BF16)


def split_in_three(value):
    parts = []
    for _ in range(3):
        part = value.astype(BF16)
        parts.append(part)
        value = value - part.astype(F32)
    return parts


def project_kernel(
    owner_ref,
    len_ref,
    step_ref,
    ok_ref,
    ov_ref,
    gain_ref,
    lat_ref,
    noise_ref,
    pw_ref,
    time_ref,
    norm_ref,
    vhw_ref,
    w_hbm,
    q_in,
    pk_in,
    pv_in,
    res_in,
    qm_hbm,
    scaled_ref,
    sq_ref,
    hv_ref,
    q_hbm,
    nt_hbm,
    q_ref,
    pk_ref,
    pv_ref,
    res_ref,
    att,
    wg,
    terms,
    land_first,
    land_second,
    zsum,
    relay,
    landy,
    qm,
    packed,
    pwt,
    col,
    q_out,
    nt_out,
    own_sem,
    qm_sem,
    out_sem,
    w_send,
    w_recv,
    r_send,
    r_recv,
    y_send,
    y_recv,
):
    x, y, z, core = places()
    y_lo, y_hi = y % 2, y // 2
    xp, xo, xf = x + 1 - 2 * (x % 2), 3 - x, (x + 2) % 4
    at_y = device_at(x, y + 1 - 2 * y_lo, z, core)
    at_xp, at_xo = device_at(xp, y, z, core), device_at(xo, y, z, core)
    at_ze, at_zo = device_at(x, y, z + 1 - 2 * (z % 2), core), device_at(x, y, 3 - z, core)
    at_yo = device_at(x, 3 - y, z, core)
    at_sib = device_at(x, y, z, 1 - core)
    bit_b = z // 2
    shared = []

    keep = [
        pltpu.make_async_copy(w_hbm.at[:, h * 256 : (h + 1) * 256], wg.at[x, y_lo, core, h], own_sem.at[h])
        for h in range(2)
    ]
    inputs = [
        pltpu.make_async_copy(source, target, qm_sem.at[n])
        for n, (source, target) in enumerate(
            ((q_in, q_ref), (pk_in, pk_ref), (pv_in, pv_ref), (res_in, res_ref), (qm_hbm, qm))
        )
    ]
    load_qm = inputs[4]
    for copy in keep + inputs:
        copy.start()
    greet((at_y, at_yo, at_xp, at_xo, at_ze, at_zo, at_sib))

    def share(xs, ys, h, *targets):
        slot = wg.at[xs, ys, core, h]
        for target in targets:
            copy = pltpu.make_async_remote_copy(
                src_ref=slot,
                dst_ref=slot,
                send_sem=w_send.at[len(shared)],
                recv_sem=w_recv.at[xs, ys, core, h],
                device_id=target,
                device_id_type=MESH,
            )
            copy.start()
            shared.append(copy)

    def arrived(xs, ys, cs, h):
        slot = wg.at[xs, ys, cs, h]
        pltpu.make_async_remote_copy(
            src_ref=slot,
            dst_ref=slot,
            send_sem=w_send.at[0],
            recv_sem=w_recv.at[xs, ys, cs, h],
            device_id=at_sib,
            device_id_type=MESH,
        ).wait_recv()

    def pass_on(xs, ys, h, *targets):
        arrived(xs, ys, core, h)
        share(xs, ys, h, *targets)

    def prepare():
        packed[0:128, :] = pw_ref[...]
        parts = split_in_three(time_ref[...].reshape(1, W)) + split_in_three(norm_ref[...].reshape(1, W))
        packed[128:256, :] = jnp.concatenate(parts + [jnp.zeros((122, W), BF16)], 0)

        def body(i, carry):
            rows = pl.ds(pl.multiple_of(i * 256, 256), 256)
            value = nt_dot(one_hot_rows(i * 256, 256), packed[...])
            pwt[rows, :] = value[:, :128].astype(BF16)
            col[rows, :] = value[:, 128:]
            return carry

        lax.fori_loop(0, GRAD_ROWS // 256, body, 0)

    def prelude(c):
        t = (step_ref[0].astype(F32) + 0.5) / NT
        rows = pl.ds(c * TOKENS, TOKENS)
        noisy = ((1.0 - t) * lat_ref[rows, :].astype(F32) + t * noise_ref[rows, :].astype(F32)).astype(BF16)
        hidden = nn_dot(noisy, pw_ref[...]) + t * time_ref[...].reshape(1, W)
        scale = lax.rsqrt(jnp.mean(hidden * hidden, -1, keepdims=True) + eps)
        normed = (hidden * scale * norm_ref[...].reshape(1, W)).astype(BF16)
        hv_ref[rows, :] = nn_dot(hidden.astype(BF16), vhw_ref[...])
        q_out[...] = nn_dot(normed, qm[...]).astype(BF16)
        time_col = col[:, 0:1] + col[:, 1:2] + col[:, 2:3]
        norm_col = col[:, 3:4] + col[:, 4:5] + col[:, 5:6]
        ht = nt_dot(pwt[...], noisy) + t * time_col
        scale_t = lax.rsqrt(jnp.sum(ht * ht, 0, keepdims=True) / W + eps)
        nt_out[...] = (ht * scale_t * norm_col).astype(BF16)
        copies = (
            pltpu.make_async_copy(q_out, q_hbm.at[c * TOKENS : (c + 1) * TOKENS, :], out_sem.at[c, 0]),
            pltpu.make_async_copy(nt_out, nt_hbm.at[:, c * TOKENS : (c + 1) * TOKENS], out_sem.at[c, 1]),
        )
        for copy in copies:
            copy.start()
        return copies

    def prompts(start, end):
        def body(m, carry):
            attend(m, owner_ref, len_ref, q_ref, pk_ref, pv_ref, ok_ref, ov_ref, att)
            return carry

        lax.fori_loop(start, end, body, 0)

    first_chip = (x // 2, 1 - x // 2)
    chips = ((x, xp), (xo, xf))
    subs = ((core, 0), (1 - core, 0), (core, 1), (1 - core, 1))
    mine = bit_b

    def row_of(batch):
        return y_lo if batch < 2 else 1 - y_lo

    def passing(batch):
        return batch % 2

    def at_end(batch):
        return z % 2 == row_of(batch)

    def between(batch):
        return z % 2 != row_of(batch)

    def remote(s, which, source, landing, device):
        return pltpu.make_async_remote_copy(
            src_ref=source,
            dst_ref=landing,
            send_sem=r_send.at[s, which],
            recv_sem=r_recv.at[s, which],
            device_id=device,
            device_id_type=MESH,
        )

    def out_block(s):
        return (mine + z + row_of(s // 4) + 1) % 2

    def first(s, part):
        block = out_block(s) if part == 0 else 1 - mine
        return remote(s, part, terms.at[s, part, block], land_first.at[s, part], at_ze if part == 0 else at_zo)

    def second(s, part):
        block = 1 - mine if part == 0 else mine
        landing = land_second.at[passing(s // 4), s % 4, part]
        return remote(s, 2 + part, terms.at[s, part, block], landing, at_zo if part == 0 else at_ze)

    def multiply(s):
        batch = s // 4
        cs, h = subs[s % 4]

        def body(u, carry):
            value = nn_dot(att[...], wg[2 * first_chip[passing(batch)] + u, row_of(batch), cs, h]).astype(BF16)
            terms[s, 0, u] = value[:256]
            terms[s, 1, u] = value[256:]
            return carry

        lax.fori_loop(0, 2, body, 0)
        for part in range(2):
            first(s, part).start()

    def halve(s):
        for part in range(2):
            first(s, part).wait_recv()
            block = 1 - out_block(s) if part == 0 else mine
            total = terms[s, part, block].astype(F32) + land_first[s, part].astype(F32)
            terms[s, part, block] = total.astype(BF16)

        @pl.when(between(s // 4))
        def _():
            for part in range(2):
                second(s, part).start()

    def finish(s):
        batch = s // 4

        @pl.when(at_end(batch))
        def _():
            for part in range(2):
                second(s, part).wait_recv()
                landing = land_second[passing(batch), s % 4, part]
                total = terms[s, part, mine].astype(F32) + landing.astype(F32)
                zsum[passing(batch), s % 4, part * 256 : (part + 1) * 256] = total.astype(BF16)

    kept = (x // 2 + y_hi) % 2

    def across(i, leg):
        part = leg % 2
        if leg < 2:
            source, landing = zsum.at[1 - kept, i, part * 256 : (part + 1) * 256], relay.at[i, part]
        else:
            source, landing = relay.at[i, part], landy.at[i, part]
        return pltpu.make_async_remote_copy(
            src_ref=source,
            dst_ref=landing,
            send_sem=y_send.at[i, leg],
            recv_sem=y_recv.at[i, leg],
            device_id=at_y if leg in (0, 3) else at_yo,
            device_id_type=MESH,
        )

    def cross(i):
        across(i, 0).start()
        across(i, 1).start()

    def relay_on(i):
        for part in range(2):
            across(i, part).wait_recv()
            across(i, 2 + part).start()

    def close(i):
        for part in range(2):
            across(i, 2 + part).wait_recv()
        cs, h = subs[i]
        columns = pl.ds(pl.multiple_of(cs * 512 + h * 256, 256), 256)
        gain = gain_ref[:, columns]

        def body(m, carry):
            rows = pl.ds(pl.multiple_of(m * NQ, NQ), NQ)
            part, inside = m // 4, pl.ds(pl.multiple_of(m % 4 * NQ, NQ), NQ)
            value = res_ref[owner_ref[0, m], :, columns].astype(F32)
            value = value + (zsum[kept, i, rows, :].astype(F32) + landy[i, part, inside, :].astype(F32))
            scaled_ref[rows, columns] = (value * gain).astype(BF16)
            square = value * value
            square = square[:, :128] + square[:, 128:]
            sq_ref[rows, :] = square if i == 0 else sq_ref[rows, :] + square
            return carry

        lax.fori_loop(0, 8, body, 0)

    def steps(batch, h):
        for s in (4 * batch + 2 * h, 4 * batch + 2 * h + 1):
            if s % 2 == 1:
                for xs in chips[passing(batch)]:
                    arrived(xs, row_of(batch), 1 - core, h)
            multiply(s)

    def each(do, *numbers):
        for s in numbers:
            do(s)

    keep[0].wait()
    share(x, y_lo, 0, at_xp, at_xo, at_y, at_sib)
    for copy in inputs[:4]:
        copy.wait()
    prompts(0, 4)
    keep[1].wait()
    pass_on(xo, y_lo, 0, at_xp)
    share(x, y_lo, 1, at_xo, at_y)
    share(xo, y_lo, 0, at_sib)
    pass_on(xp, y_lo, 0, at_sib)
    share(x, y_lo, 1, at_sib)
    prompts(4, 8)
    steps(0, 0)
    pass_on(x, 1 - y_lo, 0, at_sib)
    share(x, y_lo, 1, at_xp)
    share(x, 1 - y_lo, 0, at_xo)
    prepare()
    each(halve, 0, 1)

    pass_on(xo, y_lo, 1)
    pass_on(xf, y_lo, 0, at_y, at_sib)
    share(xo, y_lo, 1, at_sib)
    pass_on(x, 1 - y_lo, 1, at_sib)
    steps(1, 0)
    load_qm.wait()
    stores = prelude(0)
    each(halve, 4, 5)
    each(finish, 0, 1)

    pass_on(xp, y_lo, 1, at_xo)
    share(x, 1 - y_lo, 0, at_xp)
    share(xp, y_lo, 1, at_sib)
    pass_on(xo, 1 - y_lo, 0, at_sib)
    steps(0, 1)
    pass_on(xf, 1 - y_lo, 0, at_sib)
    steps(3, 0)
    for copy in stores:
        copy.wait()
    stores = prelude(1)
    each(halve, 2, 3)
    each(finish, 4, 5)

    pass_on(xf, y_lo, 1, at_y)
    share(x, 1 - y_lo, 1, at_xp, at_xo)
    share(xf, y_lo, 1, at_sib)
    pass_on(xp, 1 - y_lo, 0, at_sib)
    steps(2, 0)
    steps(1, 1)
    each(halve, 12, 13)
    for copy in stores:
        copy.wait()
    stores = prelude(2)
    each(halve, 8, 9, 6, 7)
    each(finish, 2, 3)

    pass_on(xp, 1 - y_lo, 1, at_sib)
    multiply(10)
    pass_on(xo, 1 - y_lo, 1, at_sib)
    pass_on(xf, 1 - y_lo, 1, at_sib)
    multiply(14)
    for xs in (x, xp, xo, xf):
        arrived(xs, 1 - y_lo, 1 - core, 1)
    multiply(11)
    multiply(15)
    each(finish, 12, 8)
    cross(0)
    each(finish, 13, 9)
    cross(1)
    for copy in stores:
        copy.wait()
    stores = prelude(3)
    each(halve, 10, 14)
    relay_on(0)
    each(halve, 11, 15)
    relay_on(1)
    each(finish, 6, 10, 14)
    cross(2)
    close(0)
    each(finish, 7, 11, 15)
    cross(3)
    relay_on(2)
    close(1)
    relay_on(3)
    close(2)
    close(3)
    for copy in stores:
        copy.wait()
    for copy in shared:
        copy.wait_send()
    for s in range(16):
        for part in range(2):
            first(s, part).wait_send()

        @pl.when(between(s // 4))
        def _():
            for part in range(2):
                second(s, part).wait_send()

    for i in range(4):
        for leg in range(4):
            across(i, leg).wait_send()


def projected(
    owner,
    lengths,
    timesteps,
    query_states,
    prompt_keys,
    prompt_values,
    query_keys,
    query_values,
    residual,
    gain,
    latents,
    noise,
    patch_weight,
    time_embedding,
    norm_gain,
    vhw,
    weight,
    qm,
):
    rows = query_states.shape[0] * NQ
    tokens = latents.shape[0]
    vmem, smem = pl.BlockSpec(memory_space=pltpu.VMEM), pl.BlockSpec(memory_space=pltpu.SMEM)
    anywhere = pl.BlockSpec(memory_space=pl.ANY)
    return pl.pallas_call(
        project_kernel,
        out_shape=[
            jax.ShapeDtypeStruct((rows, 1024), BF16),
            jax.ShapeDtypeStruct((rows, 128), F32),
            jax.ShapeDtypeStruct((tokens, 128), F32),
            jax.ShapeDtypeStruct((tokens, W), BF16),
            jax.ShapeDtypeStruct((GRAD_ROWS, tokens), BF16),
        ],
        in_specs=[smem] * 3 + [vmem] * 9 + [anywhere] * 6,
        out_specs=[vmem] * 3 + [anywhere] * 2,
        scratch_shapes=[
            pltpu.VMEM(query_states.shape, BF16),
            pltpu.VMEM(prompt_keys.shape, BF16),
            pltpu.VMEM(prompt_values.shape, BF16),
            pltpu.VMEM(residual.shape, BF16),
            pltpu.VMEM((rows, 1024), BF16),
            pltpu.VMEM((4, 2, 2, 2, 1024, 256), BF16),
            pltpu.VMEM((16, 2, 2, 256, 256), BF16),
            pltpu.VMEM((16, 2, 256, 256), BF16),
            pltpu.VMEM((2, 4, 2, 256, 256), BF16),
            pltpu.VMEM((2, 4, rows, 256), BF16),
            pltpu.VMEM((4, 2, 256, 256), BF16),
            pltpu.VMEM((4, 2, 256, 256), BF16),
            pltpu.VMEM(qm.shape, BF16),
            pltpu.VMEM((256, W), BF16),
            pltpu.VMEM((GRAD_ROWS, 128), BF16),
            pltpu.VMEM((GRAD_ROWS, 128), F32),
            pltpu.VMEM((TOKENS, W), BF16),
            pltpu.VMEM((GRAD_ROWS, TOKENS), BF16),
            pltpu.SemaphoreType.DMA((2,)),
            pltpu.SemaphoreType.DMA((5,)),
            pltpu.SemaphoreType.DMA((4, 2)),
            pltpu.SemaphoreType.DMA((32,)),
            pltpu.SemaphoreType.DMA((4, 2, 2, 2)),
            pltpu.SemaphoreType.DMA((16, 4)),
            pltpu.SemaphoreType.DMA((16, 4)),
            pltpu.SemaphoreType.DMA((4, 4)),
            pltpu.SemaphoreType.DMA((4, 4)),
        ],
        compiler_params=pltpu.CompilerParams(
            collective_id=2, has_side_effects=True, vmem_limit_bytes=62 << 20
        ),
        name="attend_project",
    )(
        owner,
        lengths,
        timesteps,
        query_keys,
        query_values,
        gain.reshape(1, -1),
        latents,
        noise,
        patch_weight,
        time_embedding,
        norm_gain,
        vhw,
        weight,
        query_states,
        prompt_keys,
        prompt_values,
        residual,
        qm,
    )


COLUMNS = 256
CHUNKS = 2 * W // COLUMNS


def finish_kernel(
    gain,
    scaled_ref,
    sq_ref,
    hv_ref,
    lat_ref,
    noise_ref,
    vhw_ref,
    conn_hbm,
    q_hbm,
    nt_hbm,
    vel_ref,
    out_ref,
    conn,
    q,
    nt,
    buf,
    land1,
    land2,
    land3,
    sqb,
    sq1,
    sq2,
    sq3,
    cond,
    kbd,
    kflat,
    vw,
    ones,
    probs,
    dsc,
    dq,
    load_sem,
    send_sem,
    recv_sem,
    core_send,
    core_recv,
    g_send,
    g_recv,
    *pieces,
):
    mine, away, sibling_part = pieces[0:6], pieces[6:12], pieces[12:18]
    landing = [pieces[18 + 5 * p : 23 + 5 * p] for p in range(6)]
    x, y, z, core = places()
    y_hi = y // 2
    partners = link_partners(x, y, z, core)
    at_ze, at_zo = partners[4], partners[5]
    at_far = device_at(x, (y + 2) % 4, z, core)
    sibling = device_at(x, y, z, 1 - core)

    def across_two(dim, later):
        place = [x, y, z]
        for flipped in (dim, later):
            i = place[flipped // 2]
            place[flipped // 2] = 3 - i if flipped % 2 else i + 1 - 2 * (i % 2)
        return device_at(*place, core)

    corners = tuple(across_two((p + 4) % 6, (p + 5) % 6) for p in range(6))
    bits = gray_bits(x) + gray_bits(y) + gray_bits(z)
    bit_a, bit_b = gray_bits(z)
    loads = [
        pltpu.make_async_copy(
            conn_hbm.at[:, part * 512 : (part + 1) * 512], conn.at[:, part * 512 : (part + 1) * 512], load_sem.at[part]
        )
        for part in range(7)
    ]
    loads.append(pltpu.make_async_copy(q_hbm, q, load_sem.at[7]))
    loads.append(pltpu.make_async_copy(nt_hbm, nt, load_sem.at[8]))
    for copy in loads:
        copy.start()
    greet(partners + corners + (sibling,))

    sent = []
    flying = {}

    def send(j, phase):
        if j == CHUNKS:
            block, target = sqb, (sq1, sq2, sq3)[phase]
        else:
            block, target = buf.at[j], (land1, land2, land3)[phase].at[j]
        if phase == 0:
            source = block.at[:, 1 - bit_a] if j % 2 == 0 else block.at[:, :, 1 - bit_b]
        elif phase == 1:
            source = block.at[:, bit_a, 1 - bit_b] if j % 2 == 0 else block.at[:, 1 - bit_a, bit_b]
        else:
            source = block.at[1 - y_hi, bit_a, bit_b]
        copy = pltpu.make_async_remote_copy(
            src_ref=source,
            dst_ref=target,
            send_sem=send_sem.at[j, phase],
            recv_sem=recv_sem.at[j, phase],
            device_id=at_far if phase == 2 else at_ze if phase == j % 2 else at_zo,
            device_id_type=MESH,
        )
        copy.start()
        sent.append(copy)
        flying[j] = copy

    def settle(j, phase):
        flying[j].wait_recv()
        if phase == 0:
            index = (slice(None), bit_a) if j % 2 == 0 else (slice(None), slice(None), bit_b)
        else:
            index = (slice(None), bit_a, bit_b)
        if j == CHUNKS:
            sqb[index] = sqb[index] + (sq1, sq2)[phase][...]
        else:
            index = (j,) + index
            total = buf[index].astype(F32) + (land1, land2)[phase][j].astype(F32)
            buf[index] = total.astype(BF16)
        send(j, phase + 1)

    def spread(block, value):
        for m in range(8):
            a, b = gray_bits(m % 4)
            block[m // 4, a, b] = value[m * NQ : (m + 1) * NQ]

    def condition(j, factor):
        flying[j].wait_recv()
        total = buf[j, y_hi, bit_a, bit_b].astype(F32) + land3[j].astype(F32)
        cond[:, j * COLUMNS : (j + 1) * COLUMNS] = (total * factor).astype(BF16)

    def norm_factor():
        flying[CHUNKS].wait_recv()
        squares = sqb[y_hi, bit_a, bit_b] + sq3[...]
        return lax.rsqrt(jnp.sum(squares, -1, keepdims=True) / D + eps)

    scale = 1.0 / DHEAD**0.5

    def place_keys():
        for g, base in enumerate(KEY_WINDOWS):
            for n in range(4):
                window = cond[:, base : base + 512]
                kbd[g, n * NQ : (n + 1) * NQ, :] = only_head(window, 4 * g + n, base)
        for tile, first in enumerate(SCORE_WINDOWS):
            for n in range(4):
                window = cond[:, tile * 256 : (tile + 1) * 256]
                kflat[tile, n * NQ : (n + 1) * NQ, :] = only_head(window, first // NQ + n, tile * 256)
        row = lax.broadcasted_iota(jnp.int32, (256, 256), 0) // NQ
        column = lax.broadcasted_iota(jnp.int32, (256, 256), 1) // NQ
        ones[...] = jnp.where(row == column, 1.0, 0.0).astype(BF16)

    def place_values():
        for g, base in enumerate(KEY_WINDOWS):
            window = cond[:, W + base : W + base + 512]
            vals = [only_head(window, 4 * g + n, base) for n in range(4)]
            vw[g] = nn_dot(jnp.concatenate(vals, 0), vhw_ref[base : base + 512, :]).astype(BF16)

    def softmax(c):
        rows = pl.ds(c * TOKENS, TOKENS)
        for g, base in enumerate(KEY_WINDOWS):
            expo = jnp.exp(nt_dot(q[rows, base : base + 512], kbd[g]) * scale)
            total = nn_dot(jnp.minimum(expo, 3.38e38).astype(BF16), ones[...])
            probs[rows, g * 256 : (g + 1) * 256] = expo / total

    def scores_back(c, carry):
        rows = pl.ds(pl.multiple_of(c * TOKENS, TOKENS), TOKENS)
        velocity = hv_ref[rows, :]
        for g in range(4):
            velocity = velocity + nn_dot(probs[rows, g * 256 : (g + 1) * 256].astype(BF16), vw[g])
        vel_ref[rows, :] = velocity
        target = noise_ref[rows, :].astype(F32) - lat_ref[rows, :].astype(F32)
        dvel = ((velocity - target) * gain).astype(BF16)
        for g in range(4):
            p = probs[rows, g * 256 : (g + 1) * 256]
            dprob = nt_dot(dvel, vw[g])
            both = p * dprob
            high = both.astype(BF16)
            low = (both - high.astype(F32)).astype(BF16)
            shift = nn_dot(high, ones[...]) + nn_dot(low, ones[...])
            dsc[:, g * 256 : (g + 1) * 256] = (p * (dprob - shift) * scale).astype(BF16)
        for tile, first in enumerate(SCORE_WINDOWS):
            dq[rows, tile * 256 : (tile + 1) * 256] = nn_dot(dsc[:, first : first + 256], kflat[tile]).astype(BF16)
        return carry

    def product(p, which, target):
        columns = pl.ds(STARTS[p], PIECES[p])

        def part(i, carry):
            rows = nt[pl.ds(pl.multiple_of(which * 1024 + i * 512, 512), 512), :]
            value = nn_dot(rows, dq[:, columns]).astype(BF16)
            target[i] = value.reshape(2, 2, 2, 2, 2, ROWS_PAD, PIECES[p])
            return carry

        lax.fori_loop(0, 2, part, 0)

    def region(p, k, bit):
        index = []
        for dim in range(6):
            age = (dim - p) % 6
            index.append(bits[dim] if age < k else bit if age == k else slice(None))
        return tuple(index)

    def to_sibling(p):
        return pltpu.make_async_remote_copy(
            src_ref=away[p],
            dst_ref=sibling_part[p],
            send_sem=core_send.at[p],
            recv_sem=core_recv.at[p],
            device_id=sibling,
            device_id_type=MESH,
        )

    def exchange(p, k):
        dim = (p + k) % 6
        return pltpu.make_async_remote_copy(
            src_ref=mine[p].at[region(p, k, 1 - bits[dim])],
            dst_ref=landing[p][k],
            send_sem=g_send.at[p, k],
            recv_sem=g_recv.at[p, k],
            device_id=partners[dim],
            device_id_type=MESH,
        )

    def direct(p, flips):
        dims = ((p + 4) % 6, (p + 5) % 6)
        index = list(bits)
        for n, dim in enumerate(dims):
            if flips >> n & 1:
                index[dim] = 1 - bits[dim]
        device = corners[p] if flips == 3 else partners[dims[flips - 1]]
        return pltpu.make_async_remote_copy(
            src_ref=mine[p].at[tuple(index)],
            dst_ref=landing[p][4].at[flips - 1],
            send_sem=g_send.at[p, 3 + flips],
            recv_sem=g_recv.at[p, 3 + flips],
            device_id=device,
            device_id_type=MESH,
        )

    def launch(p, *copies):
        for copy in copies:
            copy.start()
            sent.append(copy)
        flying["grad", p] = copies

    def accumulate(p, k):
        for copy in flying["grad", p]:
            copy.wait_recv()
        if k == 0:
            index = (slice(None),) * 6
            arrived = sibling_part[p][...].astype(F32)
        elif k == 5:
            index = bits
            arrived = landing[p][4][0].astype(F32) + landing[p][4][1].astype(F32) + landing[p][4][2].astype(F32)
        else:
            index = region(p, k - 1, bits[(p + k - 1) % 6])
            arrived = landing[p][k - 1][...].astype(F32)
        total = mine[p][index].astype(F32) + arrived
        if k == 5:
            out_ref[:, STARTS[p] : STARTS[p] + PIECES[p]] = total
            return
        mine[p][index] = total.astype(BF16)
        if k == 4:
            launch(p, *[direct(p, flips) for flips in (1, 2, 3)])
        else:
            launch(p, exchange(p, k))

    chunks = [CHUNKS] + list(range(CHUNKS))
    for n in range(CHUNKS + 1 + 10):
        if n == 0:
            spread(sqb, sq_ref[...])
            send(CHUNKS, 0)
        elif n <= CHUNKS:
            j = chunks[n]
            if j % 2 == 0:
                loads[j // 2].wait()
            value = nn_dot(scaled_ref[...], conn[:, j * COLUMNS : (j + 1) * COLUMNS])
            spread(buf.at[j], value.astype(BF16))
            send(j, 0)
        if 0 <= n - 6 <= CHUNKS:
            settle(chunks[n - 6], 0)
        if 0 <= n - 10 <= CHUNKS:
            settle(chunks[n - 10], 1)
        if n == 19:
            factor = norm_factor()
            for j in range(7):
                condition(j, factor)
            place_keys()
            loads[7].wait()
        if 20 <= n < 24:
            softmax(n - 20)
    for j in range(7, CHUNKS):
        condition(j, factor)
    place_values()
    lax.fori_loop(0, 4, scores_back, 0)
    loads[8].wait()
    for p in range(7):
        if p < 6:
            product(p, 1 - core, away[p])
            launch(p, to_sibling(p))
            product(p, core, mine[p])
        if p > 0:
            accumulate(p - 1, 0)
    for k in range(1, 6):
        for p in range(6):
            accumulate(p, k)
    for copy in sent:
        copy.wait_send()


def hand_over_kernel(vel_ref, grad_ref, vel_out, grad_out):
    vel_out[...] = vel_ref[...]
    grad_out[...] = grad_ref[0:ROWS_BLOCK, :]


def finished(scaled, squares, hv, latents, noise, vhw, conn_weight, q, normed_t, gain):
    tokens = latents.shape[0]
    vmem, anywhere = pl.BlockSpec(memory_space=pltpu.VMEM), pl.BlockSpec(memory_space=pl.ANY)
    full = [pltpu.VMEM((2,) * 6 + (ROWS_PAD, c), BF16) for c in PIECES]
    parts = [
        pltpu.VMEM(((2,) * (5 - k) if k < 4 else (3,)) + (ROWS_PAD, c), BF16) for c in PIECES for k in range(5)
    ]
    velocity, out = pl.pallas_call(
        lambda *refs: finish_kernel(gain, *refs),
        out_shape=[jax.ShapeDtypeStruct((tokens, 128), F32), jax.ShapeDtypeStruct((ROWS_PAD, W), F32)],
        in_specs=[vmem] * 6 + [anywhere] * 3,
        out_specs=[vmem] * 2,
        scratch_shapes=[
            pltpu.VMEM(conn_weight.shape, BF16),
            pltpu.VMEM(q.shape, BF16),
            pltpu.VMEM(normed_t.shape, BF16),
            pltpu.VMEM((CHUNKS, 2, 2, 2, NQ, COLUMNS), BF16),
            pltpu.VMEM((CHUNKS, 2, 2, NQ, COLUMNS), BF16),
            pltpu.VMEM((CHUNKS, 2, NQ, COLUMNS), BF16),
            pltpu.VMEM((CHUNKS, NQ, COLUMNS), BF16),
            pltpu.VMEM((2, 2, 2, NQ, 128), F32),
            pltpu.VMEM((2, 2, NQ, 128), F32),
            pltpu.VMEM((2, NQ, 128), F32),
            pltpu.VMEM((NQ, 128), F32),
            pltpu.VMEM((NQ, 2 * W), BF16),
            pltpu.VMEM((4, 4 * NQ, 512), BF16),
            pltpu.VMEM((7, 4 * NQ, 256), BF16),
            pltpu.VMEM((4, 4 * NQ, 128), BF16),
            pltpu.VMEM((256, 256), BF16),
            pltpu.VMEM((tokens, 1024), F32),
            pltpu.VMEM((TOKENS, 1024), BF16),
            pltpu.VMEM((tokens, W), BF16),
            pltpu.SemaphoreType.DMA((9,)),
            pltpu.SemaphoreType.DMA((CHUNKS + 1, 3)),
            pltpu.SemaphoreType.DMA((CHUNKS + 1, 3)),
            pltpu.SemaphoreType.DMA((6,)),
            pltpu.SemaphoreType.DMA((6,)),
            pltpu.SemaphoreType.DMA((6, 7)),
            pltpu.SemaphoreType.DMA((6, 7)),
        ]
        + full
        + full
        + full
        + parts,
        compiler_params=pltpu.CompilerParams(
            collective_id=3, has_side_effects=True, vmem_limit_bytes=62 << 20
        ),
        name="connect_step_grad",
    )(scaled, squares, hv, latents, noise, vhw, conn_weight, q, normed_t)
    return pl.pallas_call(
        hand_over_kernel,
        out_shape=[jax.ShapeDtypeStruct((tokens, 128), F32), jax.ShapeDtypeStruct((ROWS_BLOCK, W), F32)],
        in_specs=[vmem] * 2,
        out_specs=[vmem] * 2,
        name="hand_over",
    )(velocity, out)


def on_device(
    prompt_keys,
    prompt_values,
    query_states,
    query_keys,
    query_values,
    lengths,
    residual,
    out_weight,
    final_gain,
    conn_weight,
    owner,
    latents,
    noise,
    timesteps,
    patch_weight,
    time_embedding,
    image_norm_gain,
    query_matrix,
    velocity_head_weight,
):
    count_of_rows = lax.axis_size("dp") * lax.axis_size("tensor") * latents.shape[1]
    scaled, squares, hv, q, normed_t = projected(
        owner,
        lengths,
        timesteps,
        query_states,
        prompt_keys,
        prompt_values,
        query_keys,
        query_values,
        residual,
        final_gain,
        latents[0],
        noise[0],
        patch_weight,
        time_embedding,
        image_norm_gain,
        velocity_head_weight,
        out_weight,
        query_matrix,
    )
    velocity, query_grad = finished(
        scaled,
        squares,
        hv,
        latents[0],
        noise[0],
        velocity_head_weight,
        conn_weight,
        q,
        normed_t,
        grad_gain / math.sqrt(count_of_rows),
    )
    return (velocity[None], query_grad)


def solution(mesh):
    return jax.shard_map(
        on_device,
        mesh=mesh,
        in_specs=(
            P("dp", None, "tensor"),
            P("dp", None, "tensor"),
            P("dp", None, "tensor"),
            P("dp", None, "tensor"),
            P("dp", None, "tensor"),
            P("dp"),
            P("dp", None, "tensor"),
            P("tensor", "dp"),
            P("tensor"),
            P("tensor", None),
            P("dp", None),
            P(("dp", "tensor"), None, None),
            P(("dp", "tensor"), None, None),
            P(("dp", "tensor")),
            P(),
            P(),
            P(),
            P(),
            P(),
        ),
        out_specs=(P(("dp", "tensor"), None, None), P(("dp", "tensor"), None)),
        check_vma=False,
    )
```
